32 devices in a mesh: sect: 2 (over x), exp: 8 (over z, y), dp: 2 (over core).
Axes of the slice: x: 2, y: 2, z: 4, core: 2. Of those that a mesh axis runs over, the one named last changes fastest.
Arguments:
- decode_states: bfloat16 [256, 2048], P('exp'), may hold values from -15 to 15
- norm_gain: float32 [2048], replicated, may hold values from 0.25 to 1.75
- decode_routes: int32 [4, 256, 2], P(None, 'exp'), may hold values from 0 to 7, all different within a row; in each aligned block of 32 rows (0 to 31, 32 to 63, ..., all dimensions but the last counted through in order) at most 12 rows name the same one
- decode_gates: float32 [4, 256, 2], P(None, 'exp'), may hold values from 0.2 to 1
- up_weight: bfloat16 [2, 8, 1536, 2048], P('sect', 'exp', 'dp'), may hold values from -5 to 5
- down_weight: bfloat16 [2, 8, 1536, 2048], P('sect', 'exp', 'dp'), may hold values from -5 to 5
- traj_inputs: bfloat16 [2, 256, 2048], P('sect', 'exp'), may hold values from -6 to 6
- traj_cotangents: bfloat16 [2, 256, 2048], P('sect', 'exp'), may hold values from -6 to 6
- traj_lengths: int32 [8, 2, 4], P('exp'), may hold values from 1 to 16, 32 in all within a row
- packing: int32 [8, 8], P('exp'), may hold values from 0 to 7, each once within a row
- learner_routes: int32 [1024, 2], P('exp'), may hold values from 0 to 7, all different within a row; in each aligned block of 128 rows (0 to 127, 128 to 255, ...) at most 48 rows name the same one
- learner_gates: float32 [1024, 2], P('exp'), may hold values from 0.2 to 1
Outputs:
- final_states: bfloat16 [256, 2048], P('exp', 'sect')
- fresh_up: bfloat16 [2, 8, 1536, 2048], P('sect', 'exp', 'dp')
- fresh_down: bfloat16 [2, 8, 1536, 2048], P('sect', 'exp', 'dp')
The draws below stay inside these ranges and needn't reach their ends.
Inputs may be any that keep to these rules, and one draw needn't show every extreme that they name: `decode_routes`: within each aligned block of 32 rows of one step (the rows of one index of exp), no expert is named more than 12 times, and that bound is met. `learner_routes`: within each aligned block of 128 rows (the slots of one learner shard), no expert is named more than 48 times, and that bound is met. `traj_lengths`: each row of 4 lengths sums to 32 and its largest is 16. `packing`: each row is a permutation of the 8 learner shards, so every holder sends exactly one trajectory to every shard.
All inputs are finite; a program needn't handle non-finite values.
Results may differ from the reference program's by a relative error of at most 0.02.
Values may be sent and summed in bfloat16 or wider, within the bound.
No kernel may reach another device: no remote copies, remote signals or barrier semaphores. Data moves between devices by JAX's collectives and lax.ppermute only.
A program may use at most 128 MiB of HBM per device.

```python
import math
import jax
import jax.numpy as jnp
import numpy as np
from jax import lax

D = 2048
H = 1536
K = 2
STEPS = 4
DEC_ROWS = 32
LRN_ROWS = 128
EXPERTS = 8
ROWS = 256
CAP_D = 12
CAP_L = 48
CAP_T = 16
NT = 4
SRC_ROWS = 32
N_EXP = 8
N_DP = 2


def draw_decode_states(key, part):
    key_values = jax.random.fold_in(key, 11)
    key_rows = jax.random.fold_in(key, 12)
    key_cols = jax.random.fold_in(key, 13)
    row_scale = jnp.exp(jax.random.uniform(key_rows, (ROWS, 1), jnp.float32, 0.0, 2.302585))
    col_scale = jnp.exp(jax.random.uniform(key_cols, (1, D), jnp.float32, 0.0, 2.302585))
    unit_values = jnp.clip(jax.random.normal(key_values, (ROWS, D), jnp.float32), -5.0, 5.0)
    return (0.03 * unit_values * row_scale * col_scale).astype(jnp.bfloat16)


def steps_of(own_key, shape, cuts, least, high):
    factor_of = 1.0
    for position, blocks in cuts:
        heights = jax.random.uniform(jax.random.fold_in(jax.random.fold_in(own_key, 6), position), (blocks,), jnp.float32, least / len(cuts), high / len(cuts))
        factor_of = factor_of * jnp.repeat(jnp.exp(heights), shape[position] // blocks).reshape((-1,) + (1,) * (len(shape) - 1 - position))
    return factor_of


def length_profile(amount, total, reach, slope):
    weights = [(1 << 20) // math.isqrt(standing ** slope) + 1 for standing in range(2, amount + 1)]
    rest, counts = total - reach - (amount - 1), [1] * (amount - 1)
    while rest > 0:
        candidates = [i for i in range(amount - 1) if counts[i] < reach]
        mass, remaining = sum([weights[i] for i in candidates]), rest
        for i in candidates:
            more = min(reach - counts[i], max(1, remaining * weights[i] // mass), rest)
            counts[i] = counts[i] + more
            rest = rest - more
    return np.array([reach] + counts)


def ragged(stream_key, number_of, total, reach, slope):
    if number_of == 2:
        one = jax.random.randint(stream_key, (), max(1, total - reach), min(reach, total - 1) + 1)
        return jnp.stack([one, total - one])
    tallies = jnp.asarray(length_profile(number_of, total, reach, slope), jnp.int32)
    couples = (number_of - 1) // 2
    source_of, taker = tallies[1:1 + 2 * couples:2], tallies[2:2 + 2 * couples:2]
    slack = jnp.minimum(source_of - 1, reach - taker)
    shifted = jax.random.randint(jax.random.fold_in(stream_key, 1), (couples,), 0, 1 << 20) % (slack + 1)
    tallies = tallies.at[1:1 + 2 * couples:2].set(source_of - shifted).at[2:2 + 2 * couples:2].set(taker + shifted)
    return tallies[jax.random.permutation(jax.random.fold_in(stream_key, 2), number_of)]


def shared_out(key, own, number, rows, amount, top, most, skew):
    ranking = jax.random.permutation(key, amount)
    packed, ordinary = portions_of(amount, rows * top, most, skew, True), portions_of(amount, rows * top, most, skew, False)
    places = jnp.arange(amount)

    def named(sizes, offset_by):
        used = int((sizes > 0).sum())
        fixed = max(1, used // 4)
        moved = fixed + (places - fixed + offset_by * (used - fixed)) % max(1, amount - fixed)
        return jnp.zeros((amount,), jnp.int32).at[ranking[jnp.where(places < fixed, places, moved)]].set(jnp.asarray(sizes, jnp.int32))

    sizes = jnp.where(number % 4 == 0, named(packed, number // 4), named(ordinary, number - number // 4 - 1))
    mixed = jax.random.permutation(jax.random.fold_in(own, 3), amount)
    giver, taker = mixed[0:amount // 2 * 2:2], mixed[1:amount // 2 * 2:2]
    room = jnp.minimum(sizes[giver] - 1, most - sizes[taker]) // 2
    room = jnp.where((giver == ranking[0]) | (taker == ranking[0]) | (sizes[taker] == 0), 0, jnp.maximum(room, 0))
    moved = jax.random.randint(jax.random.fold_in(own, 4), (amount // 2,), 0, 1 << 20) % (room + 1)
    sizes = sizes.at[giver].add(-moved).at[taker].add(moved)
    items = jnp.searchsorted(jnp.cumsum(sizes), jnp.arange(rows * top), side="right").astype(jnp.int32)
    grid = items.reshape(top, rows).T
    grid = grid[jax.random.permutation(jax.random.fold_in(own, 1), rows)]
    offset_by = jax.random.randint(jax.random.fold_in(own, 2), (rows, 1), 0, top)
    return jnp.take_along_axis(grid, (jnp.arange(top)[None, :] + offset_by) % top, axis=1)


def portions_of(amount, total, bound, skew, full):
    weights = [(1 << 20) // math.isqrt(grade ** skew) + 1 for grade in range(1, amount + 1)]
    largest = bound if full else min(bound, max(-(-total // amount), total * weights[0] // sum(weights)))
    least = 1 if total - largest >= amount - 1 else 0
    given, rest = [largest] + [least] * (amount - 1), total - largest - least * (amount - 1)
    while rest > 0:
        candidates = [i for i in range(1, amount) if given[i] < largest] or [i for i in range(1, amount) if given[i] < bound]
        mass, remaining = sum([weights[i] for i in candidates]), rest
        for i in candidates:
            addition = min(bound - given[i], max(1, remaining * weights[i] // mass), rest)
            given[i] = given[i] + addition
            rest = rest - addition
    return np.array(given)


def normal_values(rng, shape, spread, bound, shards=(), held_as=jnp.bfloat16):
    result = spread * jax.random.normal(rng, shape, jnp.float32)
    if shards:
        result = result * steps_of(rng, shape, shards, -0.22, 0.18)
    return jnp.clip(result, -bound, bound).astype(held_as)


def setup_inputs(seed: int = 0) -> dict:
    streams_of = jax.random.split(jax.random.key(seed), 13)
    decode_states = draw_decode_states(jax.random.fold_in(streams_of[12], 71), 0)
    norm_gain = jnp.clip(1.0 + 0.15 * jax.random.normal(streams_of[1], (D,), jnp.float32), 0.25, 1.75)
    decode_routes_keys = jax.random.split(jax.random.fold_in(streams_of[2], 1), STEPS * ROWS // DEC_ROWS)
    decode_routes_turns = jax.random.permutation(jax.random.fold_in(streams_of[2], 3), STEPS * ROWS // DEC_ROWS)
    decode_routes = jax.vmap(lambda own, number: shared_out(jax.random.fold_in(streams_of[2], 2), own, number, DEC_ROWS, N_EXP, K, CAP_D, 2))(decode_routes_keys, decode_routes_turns).reshape((STEPS, ROWS, K))
    decode_gates = jnp.clip(0.2 + 0.8 * jax.random.uniform(streams_of[3], (STEPS, ROWS, K), jnp.float32) ** steps_of(streams_of[3], (STEPS, ROWS, K), ((1, 8),), -0.2, 0.2), 0.2, 1.0)
    up_weight = normal_values(streams_of[4], (2, EXPERTS, H, D), 1.0, 5.0, ((0, 2), (1, 8), (2, 2)))
    down_weight = normal_values(streams_of[5], (2, EXPERTS, H, D), 1.0, 5.0, ((0, 2), (1, 8), (2, 2)))
    traj_inputs = normal_values(streams_of[6], (2, N_EXP * SRC_ROWS, D), 1.0, 6.0, ((0, 2), (1, 8)))
    traj_cotangents = normal_values(streams_of[7], (2, N_EXP * SRC_ROWS, D), 1.0, 6.0, ((0, 2), (1, 8)))
    traj_lengths = jax.vmap(lambda own: ragged(own, NT, SRC_ROWS, CAP_T, 2))(jax.random.split(streams_of[8], N_EXP * 2)).reshape((N_EXP, 2, NT)).astype(jnp.int32)
    packing = jax.vmap(lambda own: jax.random.permutation(own, N_EXP))(jax.random.split(streams_of[9], N_EXP)).reshape((N_EXP, N_EXP)).astype(jnp.int32)
    learner_routes_keys = jax.random.split(jax.random.fold_in(streams_of[10], 1), (N_EXP * LRN_ROWS) // LRN_ROWS)
    learner_routes_turns = jax.random.permutation(jax.random.fold_in(streams_of[10], 3), (N_EXP * LRN_ROWS) // LRN_ROWS)
    learner_routes = jax.vmap(lambda own, number: shared_out(jax.random.fold_in(streams_of[10], 2), own, number, LRN_ROWS, N_EXP, K, CAP_L, 2))(learner_routes_keys, learner_routes_turns).reshape((N_EXP * LRN_ROWS, K))
    learner_gates = jnp.clip(0.2 + 0.8 * jax.random.uniform(streams_of[11], (N_EXP * LRN_ROWS, K), jnp.float32) ** steps_of(streams_of[11], (N_EXP * LRN_ROWS, K), ((0, 8),), -0.2, 0.2), 0.2, 1.0)
    return dict(decode_states=decode_states, norm_gain=norm_gain, decode_routes=decode_routes, decode_gates=decode_gates, up_weight=up_weight, down_weight=down_weight, traj_inputs=traj_inputs, traj_cotangents=traj_cotangents, traj_lengths=traj_lengths, packing=packing, learner_routes=learner_routes, learner_gates=learner_gates)


step_size = 3.0
norm_eps = 1e-06
highest = lax.Precision.HIGHEST

def slot_table(routes, capacity):
    flat_routes = routes.reshape(-1).astype(jnp.int32)
    member = (flat_routes[:, None] == jnp.arange(EXPERTS, dtype=jnp.int32)[None, :]).astype(jnp.int32)
    earlier = (jnp.cumsum(member, axis=0) - member).astype(jnp.int32)
    within = lax.optimization_barrier(jnp.sum(earlier * member, axis=1)).astype(jnp.int32)
    target = flat_routes * capacity + within
    one_hot = (target[:, None] == jnp.arange(EXPERTS * capacity, dtype=jnp.int32)[None, :]).astype(jnp.float32)
    return one_hot.reshape(routes.shape[0], routes.shape[1], EXPERTS * capacity)

def pack_rows(held_rows, lengths, row_pack):
    traj_count = lengths.shape[1]
    per_half = held_rows.shape[0] // 2
    column_ids = jnp.arange(row_pack.shape[0], dtype=jnp.int32)
    starts = (jnp.cumsum(lengths, axis=1) - lengths).astype(jnp.int32)
    matches = (row_pack[None, :] == column_ids[:, None]).astype(jnp.int32)
    chosen = lax.optimization_barrier(jnp.sum(matches * column_ids[None, :], axis=1)).astype(jnp.int32)
    half_index = chosen // traj_count
    length_of = jnp.take(lengths.reshape(-1), chosen)
    first_row = half_index * per_half + jnp.take(starts.reshape(-1), chosen)
    offsets = jnp.arange(CAP_T, dtype=jnp.int32)
    in_length = offsets[None, :] < length_of[:, None]
    row_index = jnp.where(in_length, first_row[:, None] + offsets[None, :], 0).reshape(-1).astype(jnp.int32)
    picked = jnp.take(held_rows, row_index, axis=0)
    return jnp.where(in_length.reshape(-1)[:, None, None], picked, jnp.zeros_like(picked))

def update_expert(operands):
    inputs, scaled_grad, up_mat, down_mat = operands
    before_act = jnp.einsum('sd,hd->sh', inputs.astype(jnp.float32), up_mat.astype(jnp.float32), precision=highest) * D ** (-0.5)
    sigmoid_val = jax.nn.sigmoid(before_act)
    activated = (before_act * sigmoid_val).astype(jnp.bfloat16)
    hidden_grad = jnp.einsum('sd,hd->sh', scaled_grad.astype(jnp.float32), down_mat.astype(jnp.float32), precision=highest) * H ** (-0.5)
    pre_grad = (hidden_grad * sigmoid_val * (1.0 + before_act * (1.0 - sigmoid_val))).astype(jnp.bfloat16)
    down_grad = jnp.einsum('sh,sd->hd', activated.astype(jnp.float32), scaled_grad.astype(jnp.float32), precision=highest) * H ** (-0.5)
    up_grad = jnp.einsum('sh,sd->hd', pre_grad.astype(jnp.float32), inputs.astype(jnp.float32), precision=highest) * D ** (-0.5)
    new_up = (up_mat.astype(jnp.float32) - step_size * up_grad).astype(jnp.bfloat16)
    new_down = (down_mat.astype(jnp.float32) - step_size * down_grad).astype(jnp.bfloat16)
    return (new_up, new_down)

def learner_fresh(up_weight, down_weight, traj_inputs, traj_cotangents, traj_lengths, packing, learner_routes, learner_gates):
    pairs = jnp.stack([traj_inputs, traj_cotangents], axis=2)
    holders = pairs.reshape(2, N_EXP, SRC_ROWS, 2, D).transpose(1, 0, 2, 3, 4).reshape(N_EXP, 2 * SRC_ROWS, 2, D)
    outgoing = lax.map(lambda operands: pack_rows(operands[0], operands[1], operands[2]), (holders, traj_lengths, packing))
    batches = outgoing.reshape(N_EXP, EXPERTS, CAP_T, 2, D).transpose(1, 0, 2, 3, 4).reshape(EXPERTS, LRN_ROWS, 2, D)
    shard_routes = learner_routes.reshape(N_EXP, LRN_ROWS, K)
    shard_gates = learner_gates.reshape(N_EXP, LRN_ROWS, K)
    one_hots = jax.vmap(lambda route_block: slot_table(route_block, CAP_L))(shard_routes)
    token_part = jnp.einsum('erks,erd->esd', one_hots, batches[:, :, 0, :].astype(jnp.float32), precision=highest).astype(jnp.bfloat16)
    grad_part = jnp.einsum('erks,erd->esd', one_hots * shard_gates[:, :, :, None], batches[:, :, 1, :].astype(jnp.float32), precision=highest).astype(jnp.bfloat16)
    token_in = token_part.reshape(N_EXP, EXPERTS, CAP_L, D).transpose(1, 0, 2, 3).reshape(EXPERTS, N_EXP * CAP_L, D)
    grad_in = grad_part.reshape(N_EXP, EXPERTS, CAP_L, D).transpose(1, 0, 2, 3).reshape(EXPERTS, N_EXP * CAP_L, D)
    return lax.map(update_expert, (token_in, grad_in, up_weight[1], down_weight[1]))

def expert_forward(operands):
    slot_rows, up_mat, down_mat = operands
    before_act = jnp.einsum('sd,hd->sh', slot_rows.astype(jnp.float32), up_mat.astype(jnp.float32), precision=highest) * D ** (-0.5)
    activated = jax.nn.silu(before_act).astype(jnp.bfloat16)
    act_blocks = activated.reshape(slot_rows.shape[0], N_DP, H // N_DP).astype(jnp.float32)
    down_blocks = down_mat.reshape(N_DP, H // N_DP, D).astype(jnp.float32)
    parts = (jnp.einsum('snh,nhd->nsd', act_blocks, down_blocks, precision=highest) * H ** (-0.5)).astype(jnp.bfloat16)
    return lax.optimization_barrier(jnp.sum(parts.astype(jnp.float32), axis=0)).astype(jnp.bfloat16)

def decode_step(states, norm_gain, routes, gate_values, up_all, down_all):
    normed = (states * lax.rsqrt(lax.optimization_barrier(jnp.mean(states * states, axis=1, keepdims=True)) + norm_eps) * norm_gain).astype(jnp.bfloat16)
    src_routes = routes.reshape(N_EXP, DEC_ROWS, K)
    one_hots = jax.vmap(lambda route_block: slot_table(route_block, CAP_D))(src_routes)
    outgoing = jnp.einsum('erks,erd->esd', one_hots, normed.reshape(N_EXP, DEC_ROWS, D).astype(jnp.float32), precision=highest).astype(jnp.bfloat16)
    arrived = outgoing.reshape(N_EXP, EXPERTS, CAP_D, D).transpose(1, 0, 2, 3).reshape(EXPERTS, N_EXP * CAP_D, D)
    results = lax.map(expert_forward, (arrived, up_all, down_all))
    returned = results.reshape(EXPERTS, N_EXP, CAP_D, D).transpose(1, 0, 2, 3).reshape(N_EXP, EXPERTS * CAP_D, D)
    weighted = one_hots * gate_values.reshape(N_EXP, DEC_ROWS, K)[:, :, :, None]
    mixed = jnp.einsum('erks,esd->erd', weighted, returned.astype(jnp.float32), precision=highest)
    return states + mixed.reshape(ROWS, D)

def reference(decode_states, norm_gain, decode_routes, decode_gates, up_weight, down_weight, traj_inputs, traj_cotangents, traj_lengths, packing, learner_routes, learner_gates):
    fresh_up, fresh_down = learner_fresh(up_weight, down_weight, traj_inputs, traj_cotangents, traj_lengths, packing, learner_routes, learner_gates)
    states = decode_states.astype(jnp.float32)
    for step_index in range(STEPS):
        if step_index < STEPS // 2:
            up_all = up_weight[0]
            down_all = down_weight[0]
        else:
            up_all = fresh_up
            down_all = fresh_down
        states = decode_step(states, norm_gain, decode_routes[step_index], decode_gates[step_index], up_all, down_all)
    return (states.astype(jnp.bfloat16), jnp.stack([fresh_up, fresh_up]), jnp.stack([fresh_down, fresh_down]))
```

```python
import functools

import jax
import jax.numpy as jnp
import numpy as np
from jax import lax
from jax.experimental import pallas as pl
from jax.experimental.pallas import tpu as pltpu
from jax.sharding import PartitionSpec as P

step_size = 3.0
norm_eps = 1e-06
lanes = 256
f32, bf16, i32 = jnp.float32, jnp.bfloat16, jnp.int32
nt_dims = (((1,), (1,)), ((), ()))
tn_dims = (((0,), (0,)), ((), ()))
smem = pl.BlockSpec(memory_space=pltpu.SMEM)


def shifted(array, axis, by):
    size = lax.axis_size(axis)
    return lax.ppermute(array, axis, [(i, (i + by) % size) for i in range(size)])


def flipped(array, axis, bit):
    return lax.ppermute(array, axis, [(i, i ^ bit) for i in range(lax.axis_size(axis))])


def fits(megabytes):
    return pltpu.CompilerParams(vmem_limit_bytes=megabytes * 1024 * 1024)


def dot(a, b, dims=(((1,), (0,)), ((), ()))):
    return lax.dot_general(a, b, dims, preferred_element_type=f32)


def picked(shape, targets):
    rows = lax.broadcasted_iota(i32, shape, 0)
    return [rows == target for target in targets]


def prepare_kernel(experts, capacity, part_ref, routes_ref, rows_ref, targets_ref, states_ref, payload_ref):
    row_count = rows_ref.shape[0]
    stacked, width = states_ref.shape
    blocks = stacked // row_count
    before = lax.broadcasted_iota(i32, (stacked, stacked), 0)
    after = lax.broadcasted_iota(i32, (stacked, stacked), 1)
    row_of = lax.rem(after, row_count)
    first = before < row_count
    earlier = jnp.where(first & (before < row_of), 1.0, 0.0).astype(bf16)
    every = jnp.where(first, 1.0, 0.0).astype(bf16)
    block_of = lax.div(lax.broadcasted_iota(i32, (1, stacked), 1), row_count)
    expert_ids = lax.broadcasted_iota(i32, (experts, stacked), 0)
    for step in range(routes_ref.shape[0]):
        seen = jnp.zeros((experts, stacked), f32)
        for k in range(routes_ref.shape[1]):
            route = routes_ref[step, k : k + 1, :]
            member = jnp.where(expert_ids == route, 1.0, 0.0)
            ahead = dot(member.astype(bf16), earlier) + seen
            rank = jnp.sum(member * ahead, axis=0, keepdims=True).astype(i32)
            seen = seen + dot(member.astype(bf16), every)
            place = (route * blocks + block_of) * capacity + rank
            targets_ref[step, k : k + 1, :] = place
    start = part_ref[0] * (blocks * width)
    for block in range(blocks):
        column = pl.multiple_of(start + block * width, width)
        states_ref[block * row_count : (block + 1) * row_count, :] = rows_ref[:, pl.ds(column, width)].astype(f32)
    targets = [targets_ref[0, k : k + 1, :] for k in range(routes_ref.shape[1])]
    chosen = sum(jnp.where(hit, 1.0, 0.0) for hit in picked((payload_ref.shape[0], stacked), targets))
    payload_ref[...] = dot(chosen.astype(bf16), states_ref[...].astype(bf16)).astype(bf16)


def combine_kernel(last, targets_ref, gates_ref, next_ref, states_ref, returned_ref, new_ref, *payload_ref):
    routes = gates_ref.shape[0]
    shape = (returned_ref.shape[0], states_ref.shape[0])
    targets = [targets_ref[k : k + 1, :] for k in range(routes)]
    weights = sum(jnp.where(hit, gates_ref[k : k + 1, :], 0.0) for k, hit in enumerate(picked(shape, targets)))
    mixed = lax.dot_general(
        weights,
        returned_ref[...].astype(f32),
        tn_dims,
        precision=lax.Precision.HIGHEST,
        preferred_element_type=f32,
    )
    states = states_ref[...] + mixed
    new_ref[...] = states
    if not last:
        targets = [next_ref[k : k + 1, :] for k in range(routes)]
        chosen = sum(jnp.where(hit, 1.0, 0.0) for hit in picked(shape, targets))
        payload_ref[0][...] = dot(chosen.astype(bf16), states.astype(bf16)).astype(bf16)


def expert_kernel(parts, slots, features, hidden, part_ref, gain_ref, order_ref, *refs):
    arrived, (up_ref, down_ref) = refs[:parts], refs[parts : parts + 2]
    outs, (normed_ref, sums_ref, stack_ref) = refs[parts + 2 : 2 * parts + 2], refs[2 * parts + 2 :]
    width = arrived[0].shape[1]
    blocks = features // (parts * width)
    me = part_ref[0]

    @pl.when(pl.program_id(0) == 0)
    def _():
        square = jnp.zeros((slots, 1), f32)
        stacks = []
        for ref in arrived:
            stack = dot(order_ref[...], ref[...], tn_dims)
            stacks.append(stack)
            for block in range(blocks):
                rows = stack[block * slots : (block + 1) * slots]
                square = square + jnp.sum(rows * rows, axis=1, keepdims=True)
        scale = lax.rsqrt(square * (1.0 / features) + norm_eps)
        for j, stack in enumerate(stacks):
            start = lax.rem(me + parts - j, parts) * (blocks * width)
            for block in range(blocks):
                rows = stack[block * slots : (block + 1) * slots]
                columns = pl.ds(pl.multiple_of(start + block * width, width), width)
                normed_ref[:, columns] = (rows * scale * gain_ref[:, columns]).astype(bf16)
        sums_ref[...] = jnp.zeros_like(sums_ref)

    before_act = dot(normed_ref[...], up_ref[...], nt_dims) * features ** (-0.5)
    activated = (before_act / (1.0 + jnp.exp(-before_act))).astype(bf16)
    sums_ref[...] += dot(activated, down_ref[...])

    @pl.when(pl.program_id(0) == pl.num_programs(0) - 1)
    def _():
        for j, out_ref in enumerate(outs):
            start = lax.rem(me + j, parts) * (blocks * width)
            for block in range(blocks):
                columns = pl.ds(pl.multiple_of(start + block * width, width), width)
                stack_ref[block * slots : (block + 1) * slots, :] = (sums_ref[:, columns] * hidden ** (-0.5)).astype(bf16)
            out_ref[...] = dot(order_ref[...], stack_ref[...]).astype(bf16)


def update_kernel(parts, features, hidden, part_ref, weight_ref, *refs):
    held, (up_ref, down_ref, new_up_ref, new_down_ref) = refs[:parts], refs[parts:]
    count = held[0].shape[0] // 2
    width = held[0].shape[1]
    me = part_ref[0]
    columns = [pl.ds(pl.multiple_of(lax.rem(me + parts - j, parts) * width, width), width) for j in range(parts)]
    weight = weight_ref[...]
    before_act = sum(dot(up_ref[:, c], ref[:count], nt_dims) for c, ref in zip(columns, held)) * features ** (-0.5)
    sigmoid = 1.0 / (1.0 + jnp.exp(-before_act))
    hidden_grad = sum(dot(down_ref[:, c], ref[count:], nt_dims) for c, ref in zip(columns, held)) * hidden ** (-0.5)
    pre_grad = hidden_grad * weight * sigmoid * (1.0 + before_act * (1.0 - sigmoid))
    pre_grad = pre_grad.astype(bf16)
    activated = (before_act * sigmoid * weight).astype(bf16)
    for c, ref in zip(columns, held):
        up_grad = dot(pre_grad, ref[:count])
        new_up_ref[:, c] = (up_ref[:, c].astype(f32) - (step_size * features ** (-0.5)) * up_grad).astype(bf16)
        down_grad = dot(activated, ref[count:])
        new_down_ref[:, c] = (down_ref[:, c].astype(f32) - (step_size * hidden ** (-0.5)) * down_grad).astype(bf16)


def unset_kernel(*refs):
    pass


def unset(*like):
    return pl.pallas_call(
        unset_kernel,
        out_shape=[jax.ShapeDtypeStruct(a.shape, a.dtype) for a in like],
        out_specs=[pl.BlockSpec(memory_space=pl.ANY)] * len(like),
    )()


def on_device(
    decode_states,
    norm_gain,
    decode_routes,
    decode_gates,
    up_weight,
    down_weight,
    traj_inputs,
    traj_cotangents,
    traj_lengths,
    packing,
    learner_routes,
    learner_gates,
):
    experts, parts = lax.axis_size("exp"), lax.axis_size("dp")
    is_rollout = lax.axis_index("sect") == 0
    me = lax.axis_index("exp")
    part = lax.axis_index("dp")
    part_ref = part.reshape(1).astype(i32)
    up_here, down_here = up_weight[0, 0], down_weight[0, 0]
    hidden_here, features = up_here.shape
    hidden = hidden_here * parts
    steps, row_count, routes_each = decode_routes.shape
    share = features // parts
    blocks = share // lanes
    capacity = 3 * row_count * routes_each // (2 * experts)
    slots = experts * capacity
    stacked = blocks * row_count
    moved = blocks * slots
    tile = hidden_here // 3

    own_rows = lax.dynamic_slice_in_dim(jnp.concatenate([traj_inputs[0], traj_cotangents[0]]), part * share, share, 1)
    crossed_rows = flipped(own_rows, "sect", 1)
    up_there = lax.ppermute(up_here, "sect", [(1, 0)])

    routes = jnp.tile(jnp.swapaxes(decode_routes, 1, 2), (1, 1, blocks))
    gates = jnp.tile(jnp.swapaxes(decode_gates, 1, 2), (1, 1, blocks))
    targets, states, payload = pl.pallas_call(
        functools.partial(prepare_kernel, experts, capacity),
        out_shape=[
            jax.ShapeDtypeStruct(routes.shape, i32),
            jax.ShapeDtypeStruct((stacked, lanes), f32),
            jax.ShapeDtypeStruct((moved, lanes), bf16),
        ],
        in_specs=[smem, pl.BlockSpec(memory_space=pltpu.VMEM), pl.BlockSpec(memory_space=pltpu.VMEM)],
        compiler_params=fits(16),
    )(part_ref, routes, decode_states)
    gain = norm_gain.reshape(1, features)
    place = np.arange(moved)
    source = (place // capacity % blocks) * slots + place // (capacity * blocks) * capacity + place % capacity
    order = jnp.asarray((source[:, None] == place[None, :]).astype(np.float32), bf16)

    def whole(array):
        return pl.BlockSpec(array.shape, lambda i: (0,) * array.ndim)

    def expert_forward(arrived, up_mat, down_mat):
        tiles = pl.BlockSpec((tile, features), lambda i: (i, 0))
        out = jax.ShapeDtypeStruct((moved, lanes), bf16)
        return pl.pallas_call(
            functools.partial(expert_kernel, parts, slots, features, hidden),
            grid=(hidden_here // tile,),
            out_shape=[out] * parts,
            in_specs=[smem, whole(gain), whole(order)] + [whole(a) for a in arrived] + [tiles, tiles],
            out_specs=[whole(out)] * parts,
            scratch_shapes=[
                pltpu.VMEM((slots, features), bf16),
                pltpu.VMEM((slots, features), f32),
                pltpu.VMEM((moved, lanes), bf16),
            ],
            compiler_params=fits(24),
        )(part_ref, gain, order, *arrived, up_mat, down_mat)

    def decode_step(step, states, payload, up_mat, down_mat):
        last = step == steps - 1
        arrived = lax.all_to_all(payload, "exp", split_axis=0, concat_axis=0, tiled=True)
        arrived = [arrived] + [shifted(arrived, "dp", j) for j in range(1, parts)]
        partials = expert_forward(arrived, up_mat, down_mat)
        received = [shifted(partials[j], "dp", j) for j in range(1, parts)]
        summed = sum((r.astype(f32) for r in received), partials[0].astype(f32)).astype(bf16)
        returned = lax.all_to_all(summed, "exp", split_axis=0, concat_axis=0, tiled=True)
        outs = [jax.ShapeDtypeStruct((stacked, lanes), f32)]
        if not last:
            outs = outs + [jax.ShapeDtypeStruct((moved, lanes), bf16)]
        results = pl.pallas_call(
            functools.partial(combine_kernel, last),
            out_shape=outs,
            compiler_params=fits(16),
        )(targets[step], gates[step], targets[min(step + 1, steps - 1)], states, returned)
        return results[0], (payload if last else results[1])

    def learner_rows():
        first = jnp.where(is_rollout, own_rows, crossed_rows)
        second = jnp.where(is_rollout, crossed_rows, own_rows)
        half = first.shape[0] // 2
        rows = jnp.stack([first[:half], second[:half], first[half:], second[half:]]).reshape(2, 2 * half, share)
        flat = [learner_routes.T.reshape(-1), learner_gates.T.reshape(-1), traj_lengths.reshape(-1), packing.reshape(-1)]
        notes = jnp.concatenate([a.astype(f32) for a in flat])
        notes = jnp.pad(notes, (0, -notes.shape[0] % 1024)).reshape(1, -1, 128)
        bit = experts // 2
        while bit:
            rows = jnp.concatenate([rows, flipped(rows, "exp", bit)], axis=1)
            notes = jnp.concatenate([notes, flipped(notes, "exp", bit)], axis=0)
            bit //= 2
        rows = rows.reshape(-1, share)
        rows = [rows] + [shifted(rows, "dp", j) for j in range(1, parts)]
        return rows, weights_of(notes.reshape(experts, -1))

    def weights_of(notes):
        slot_count, each = learner_routes.shape
        halves, trajs = traj_lengths.shape[1:]
        per_half = traj_inputs.shape[1]
        longest = slot_count // experts
        ids = jnp.arange(experts, dtype=i32)
        holder_of = ids
        holder_of = jnp.zeros((experts,), i32)
        bit, low = experts // 2, 1
        while bit:
            holder_of = holder_of + jnp.where(ids // low % 2 == 1, bit, 0)
            bit, low = bit // 2, low * 2
        holder_of = holder_of ^ me
        sizes = [slot_count * each, slot_count * each, halves * trajs, experts]
        cuts = np.cumsum(sizes)
        route_table = notes[:, : cuts[0]].reshape(experts, each, slot_count)
        gate_table = notes[:, cuts[0] : cuts[1]].reshape(experts, each, slot_count)
        lengths = notes[:, cuts[1] : cuts[2]].reshape(experts, halves, trajs).astype(i32)
        shards = notes[:, cuts[2] : cuts[3]].astype(i32)
        here = jnp.sum(jnp.where(route_table == me.astype(f32), gate_table, 0.0), axis=1)
        here = here.reshape(experts, experts, longest)
        held = holder_of[:, None] == ids[None, :]
        by_holder = jnp.sum(jnp.where(held[None, :, :, None], here[:, None], 0.0), axis=2)
        sent = shards[:, :, None] == holder_of[None, None, :]
        by_traj = jnp.sum(jnp.where(sent[:, :, :, None], jnp.swapaxes(by_holder, 0, 1)[:, None], 0.0), axis=2)
        by_traj = by_traj.reshape(experts, halves, trajs, longest)
        starts = jnp.cumsum(lengths, axis=2) - lengths
        offset = jnp.arange(per_half, dtype=i32) - starts[..., None]
        inside = (offset >= 0) & (offset < lengths[..., None])
        chosen = inside[..., None] & (offset[..., None] == jnp.arange(longest, dtype=i32))
        weights = jnp.sum(jnp.where(chosen, by_traj[:, :, :, None, :], 0.0), axis=(2, 4))
        return weights.reshape(1, -1)

    def update(rows, weights, up_mat, down_mat):
        small = hidden_here // 6
        tiles = pl.BlockSpec((small, features), lambda i: (i, 0))
        return pl.pallas_call(
            functools.partial(update_kernel, parts, features, hidden),
            grid=(hidden_here // small,),
            out_shape=[jax.ShapeDtypeStruct(up_mat.shape, bf16)] * 2,
            in_specs=[smem, whole(weights)] + [whole(a) for a in rows] + [tiles, tiles],
            out_specs=[tiles, tiles],
            compiler_params=fits(48),
        )(part_ref, weights, *rows, up_mat, down_mat)

    half_steps = steps // 2

    def first_rollout():
        now, sent = states, payload
        for step in range(half_steps):
            now, sent = decode_step(step, now, sent, up_here, down_here)
        return (now, sent) + tuple(unset(up_here, down_here))

    def first_learner():
        rows, weights = learner_rows()
        return (states, payload) + tuple(update(rows, weights, up_here, down_here))

    states, payload, new_up, new_down = lax.cond(is_rollout, first_rollout, first_learner)
    states_there = lax.ppermute(states, "sect", [(0, 1)])
    payload_there = lax.ppermute(payload, "sect", [(0, 1)])
    down_late, _ = lax.optimization_barrier((down_here, states))
    down_there = lax.ppermute(down_late, "sect", [(1, 0)])

    def second_rollout():
        rows, weights = learner_rows()
        return states, rows, weights

    def second_learner():
        now, sent = states_there, payload_there
        for step in range(half_steps, steps):
            now, sent = decode_step(step, now, sent, new_up, new_down)
        gathered = jax.ShapeDtypeStruct((2 * experts * 2 * traj_inputs.shape[1], share), bf16)
        weights = jax.ShapeDtypeStruct((1, gathered.shape[0] // 2), f32)
        *rows, weights = unset(*[gathered] * parts, weights)
        return now, rows, weights

    states, rows, weights = lax.cond(is_rollout, second_rollout, second_learner)

    mine = states.astype(bf16).reshape(blocks, row_count, lanes).swapaxes(0, 1).reshape(row_count, share)
    spread = jnp.zeros((parts, row_count, share), bf16)
    for j in range(parts):
        piece = shifted(mine, "dp", j) if j else mine
        spread = lax.dynamic_update_slice(spread, piece[None], (lax.rem(part + parts - j, parts), 0, 0))
    joined = spread.swapaxes(0, 1).reshape(row_count, features)
    delivered = lax.ppermute(joined[:, : features // 2], "sect", [(1, 0)])
    final_states = jnp.where(is_rollout, delivered, joined[:, features // 2 :])

    new_up, new_down = lax.cond(
        is_rollout,
        lambda: tuple(update(rows, weights, up_there, down_there)),
        lambda: (new_up, new_down),
    )
    return final_states, new_up[None, None], new_down[None, None]


def solution(mesh):
    in_specs = (
        P("exp", None),
        P(),
        P(None, "exp", None),
        P(None, "exp", None),
        P("sect", "exp", "dp", None),
        P("sect", "exp", "dp", None),
        P("sect", "exp", None),
        P("sect", "exp", None),
        P("exp", None, None),
        P("exp", None),
        P("exp", None),
        P("exp", None),
    )
    out_specs = (P("exp", "sect"), P("sect", "exp", "dp", None), P("sect", "exp", "dp", None))
    return jax.shard_map(on_device, mesh=mesh, in_specs=in_specs, out_specs=out_specs, check_vma=False)
```

```python
import functools

import jax
import jax.numpy as jnp
from jax import lax
from jax.experimental import pallas as pl
from jax.experimental.pallas import tpu as pltpu
from jax.sharding import PartitionSpec as P

step_size = 3.0
norm_eps = 1e-06
lanes = 256
note_rows = 16
f32, bf16, i32 = jnp.float32, jnp.bfloat16, jnp.int32
nt_dims = (((1,), (1,)), ((), ()))
tn_dims = (((0,), (0,)), ((), ()))
smem = pl.BlockSpec(memory_space=pltpu.SMEM)
vmem = pl.BlockSpec(memory_space=pltpu.VMEM)
anywhere = pl.BlockSpec(memory_space=pl.ANY)
stays = pl.BlockSpec(memory_space=pltpu.HBM)


def shifted(array, axis, by):
    size = lax.axis_size(axis)
    return lax.ppermute(array, axis, [(i, (i + by) % size) for i in range(size)])


def flipped(array, axis, bit):
    return lax.ppermute(array, axis, [(i, i ^ bit) for i in range(lax.axis_size(axis))])


def fits(megabytes):
    return pltpu.CompilerParams(vmem_limit_bytes=megabytes * 1024 * 1024)


def costs(flops, moved):
    return pl.CostEstimate(flops=flops, bytes_accessed=moved, transcendentals=0)


def dot(a, b, dims=(((1,), (0,)), ((), ())), precision=None):
    return lax.dot_general(a, b, dims, precision=precision, preferred_element_type=f32)


def one_hot(rows, targets_ref):
    ids = lax.broadcasted_iota(i32, (rows, targets_ref.shape[1]), 0)
    hits = [jnp.where(ids == targets_ref[k : k + 1, :], 1.0, 0.0) for k in range(targets_ref.shape[0])]
    return sum(hits[1:], hits[0]).astype(bf16)


def prepare_kernel(
    experts, capacity, part_ref, routes_ref, gates_ref, all_rows_ref, inputs_ref, grads_ref,
    targets_ref, tiled_ref, states_ref, payload_ref, own_ref, rows_ref, sems,
):
    row_count, share = rows_ref.shape
    steps, routes_each = targets_ref.shape[:2]
    stacked, width = states_ref.shape
    blocks = stacked // row_count
    own = pl.ds(pl.multiple_of(part_ref[0] * share, share), share)
    held = inputs_ref.shape[0]
    row_copy = pltpu.make_async_copy(all_rows_ref.at[:, own], rows_ref, sems.at[0])
    copies = [
        pltpu.make_async_copy(inputs_ref.at[:, own], own_ref.at[pl.ds(0, held)], sems.at[1]),
        pltpu.make_async_copy(grads_ref.at[:, own], own_ref.at[pl.ds(held, held)], sems.at[2]),
    ]
    row_copy.start()
    for copy in copies:
        copy.start()
    before = lax.broadcasted_iota(i32, (row_count, stacked), 0)
    after = lax.rem(lax.broadcasted_iota(i32, (row_count, stacked), 1), row_count)
    repeat = jnp.where(before == after, 1.0, 0.0)
    earlier = jnp.where(before < after, 1.0, 0.0).astype(bf16)
    every = jnp.ones((row_count, stacked), bf16)
    block_of = lax.div(lax.broadcasted_iota(i32, (1, stacked), 1), row_count)
    expert_ids = lax.broadcasted_iota(i32, (experts, row_count), 0)
    tall_ids = lax.broadcasted_iota(i32, (experts, stacked), 0)
    routes = dot(routes_ref[...].astype(f32), repeat, precision=lax.Precision.HIGHEST)
    routes = (routes + 0.5).astype(i32)
    tiled_ref[...] = dot(gates_ref[...], repeat, precision=lax.Precision.HIGHEST)
    for step in range(steps):
        seen = jnp.zeros((experts, stacked), f32)
        for k in range(routes_each):
            at = step * routes_each + k
            member = jnp.where(expert_ids == routes_ref[at : at + 1, :], 1.0, 0.0).astype(bf16)
            route = routes[at : at + 1, :]
            ahead = dot(member, earlier) + seen
            rank = jnp.sum(jnp.where(tall_ids == route, ahead, 0.0), axis=0, keepdims=True)
            seen = seen + dot(member, every)
            place = (route * blocks + block_of) * capacity + (rank + 0.5).astype(i32)
            targets_ref[step, k : k + 1, :] = place
    row_copy.wait()
    for block in range(blocks):
        columns = slice(block * width, (block + 1) * width)
        states_ref[block * row_count : (block + 1) * row_count, :] = rows_ref[:, columns].astype(f32)
    payload_ref[...] = dot(one_hot(payload_ref.shape[0], targets_ref.at[0]), states_ref[...].astype(bf16)).astype(bf16)
    for copy in copies:
        copy.wait()


def dispatch_kernel(step, targets_ref, states_ref, payload_ref):
    payload_ref[...] = dot(one_hot(payload_ref.shape[0], targets_ref.at[step]), states_ref[...].astype(bf16)).astype(bf16)


def combine_kernel(step, last, targets_ref, gates_ref, states_ref, returned_ref, new_ref, payload_ref):
    ids = lax.broadcasted_iota(i32, (returned_ref.shape[0], states_ref.shape[0]), 0)
    weights = jnp.zeros(ids.shape, f32)
    routes_each = targets_ref.shape[1]
    for k in range(routes_each):
        at = step * routes_each + k
        weights = weights + jnp.where(ids == targets_ref[step, k : k + 1, :], gates_ref[at : at + 1, :], 0.0)
    high = weights.astype(bf16)
    low = (weights - high.astype(f32)).astype(bf16)
    returned = returned_ref[...]
    states = states_ref[...] + (dot(high, returned, tn_dims) + dot(low, returned, tn_dims))
    new_ref[...] = states
    if last:
        payload_ref[...] = states.astype(bf16)
    else:
        payload_ref[...] = dot(one_hot(returned.shape[0], targets_ref.at[step + 1]), states.astype(bf16)).astype(bf16)


def expert_kernel(parts, slots, capacity, features, hidden, part_ref, gain_ref, *refs):
    arrived, (up_ref, down_ref) = refs[:parts], refs[parts : parts + 2]
    outs = refs[parts + 2 : 2 * parts + 2]
    up_held, down_held, normed_ref, stack_ref, order_ref, sems = refs[2 * parts + 2 :]
    width = arrived[0].shape[1]
    blocks = features // (parts * width)
    me = part_ref[0]
    up_copy = pltpu.make_async_copy(up_ref, up_held, sems.at[0])
    down_copy = pltpu.make_async_copy(down_ref, down_held, sems.at[1])
    up_copy.start()
    down_copy.start()
    moved = blocks * slots
    column = lax.broadcasted_iota(i32, (1, moved), 1)
    slot = lax.rem(column, slots)
    target = (lax.div(slot, capacity) * blocks + lax.div(column, slots)) * capacity + lax.rem(slot, capacity)
    hits = lax.broadcasted_iota(i32, (moved, moved), 0) == target
    order_ref[...] = jnp.where(hits, 1.0, 0.0).astype(bf16)
    square = jnp.zeros((slots, 1), f32)
    stacks = []
    for ref in arrived:
        stack = dot(order_ref[...], ref[...], tn_dims)
        stacks.append(stack)
        for block in range(blocks):
            rows = stack[block * slots : (block + 1) * slots]
            square = square + jnp.sum(rows * rows, axis=1, keepdims=True)
    scale = lax.rsqrt(square * (1.0 / features) + norm_eps)
    for j, stack in enumerate(stacks):
        start = lax.rem(me + parts - j, parts) * (blocks * width)
        for block in range(blocks):
            rows = stack[block * slots : (block + 1) * slots]
            columns = pl.ds(pl.multiple_of(start + block * width, width), width)
            normed_ref[:, columns] = (rows * scale * gain_ref[:, columns]).astype(bf16)
    up_copy.wait()
    before_act = dot(normed_ref[...], up_held[...], nt_dims) * features ** (-0.5)
    activated = (before_act / (1.0 + jnp.exp(-before_act))).astype(bf16)
    down_copy.wait()
    normed_ref[...] = (dot(activated, down_held[...]) * hidden ** (-0.5)).astype(bf16)
    for j, out_ref in enumerate(outs):
        start = lax.rem(me + j, parts) * (blocks * width)
        for block in range(blocks):
            columns = pl.ds(pl.multiple_of(start + block * width, width), width)
            stack_ref[block * slots : (block + 1) * slots, :] = normed_ref[:, columns]
        out_ref[...] = dot(order_ref[...], stack_ref[...]).astype(bf16)


def gathered_copies(part, parts, height, units, inputs_ref, grads_ref, sems):
    per_part = len(units) // parts
    width = units[0].shape[1]
    rows = (height - note_rows) // 2
    in_copies, grad_copies = [], []
    for j in range(parts):
        columns = pl.ds(pl.multiple_of(lax.rem(part + parts - j, parts) * width, width), width)
        blocks = [(u, at) for u in units[j * per_part : (j + 1) * per_part] for at in range(0, u.shape[0], height)]
        for i, (unit, at) in enumerate(blocks):
            place, sem = pl.ds(i * rows, rows), 2 * (j * len(blocks) + i)
            source = unit.at[pl.ds(at, rows)]
            in_copies.append(pltpu.make_async_copy(source, inputs_ref.at[place, columns], sems.at[sem]))
            source = unit.at[pl.ds(at + rows, rows)]
            grad_copies.append(pltpu.make_async_copy(source, grads_ref.at[place, columns], sems.at[sem + 1]))
    return in_copies, grad_copies


def unit_kernel(first_ref, second_ref, routes_ref, gates_ref, lengths_ref, shards_ref, unit_ref, sems):
    held = first_ref.shape[0] // 2
    copies = []
    for i, ref in enumerate((first_ref, second_ref)):
        for j in range(2):
            place = pl.ds((2 * j + i) * held, held)
            source = ref.at[pl.ds(j * held, held)]
            copies.append(pltpu.make_async_copy(source, unit_ref.at[place], sems.at[2 * i + j]))
    for copy in copies:
        copy.start()
    wide = routes_ref.shape[1]

    def widened(ref):
        count = ref.shape[1]
        places = lax.broadcasted_iota(i32, (count, wide), 0) == lax.broadcasted_iota(i32, (count, wide), 1)
        return dot(ref[...].astype(f32), jnp.where(places, 1.0, 0.0))

    gates = gates_ref[...]
    terms = []
    for _ in range(3):
        terms.append(gates.astype(bf16).astype(f32))
        gates = gates - terms[-1]
    tables = [routes_ref[...].astype(f32)] + terms + [widened(lengths_ref), widened(shards_ref)]
    ids = lax.broadcasted_iota(i32, (note_rows, wide), 0)
    notes, at = jnp.zeros((note_rows, wide), f32), 0
    for table in tables:
        for row in range(table.shape[0]):
            notes = notes + jnp.where(ids == at, table[row : row + 1, :], 0.0)
            at += 1
    base = 4 * held
    unit_ref[base:, :] = jnp.zeros((note_rows, unit_ref.shape[1]), bf16)
    unit_ref[base:, :wide] = notes.astype(bf16)
    for copy in copies:
        copy.wait()


def weights_kernel(height, halves, each, trajs, wide, sources, me_ref, *refs):
    units, (weights_ref, notes_ref, table_ref, sems) = refs[:-4], refs[-4:]
    blocks = [(u, at) for u in units for at in range(0, u.shape[0], height)]
    count = len(blocks)
    per_half = (height - note_rows) // (2 * halves)
    longest = wide // count
    total = weights_ref.shape[1]
    copies = []
    for i, (unit, at) in enumerate(blocks):
        source = unit.at[pl.ds(at + height - note_rows, note_rows), pl.ds(0, wide)]
        copies.append(pltpu.make_async_copy(source, notes_ref.at[i], sems.at[i]))
    for copy in copies:
        copy.start()
    for copy in copies:
        copy.wait()
    me = me_ref[0]
    holders = []
    for group, flip, far, near in sources:
        place = lax.rem((lax.rem(me, group) ^ flip) + group - far, group)
        holders.append((lax.div(me, group) * group + place) ^ near)
    ids = lax.broadcasted_iota(i32, (count, 1), 0)
    holder_of = jnp.zeros((count, 1), i32)
    for i, holder in enumerate(holders):
        holder_of = holder_of + jnp.where(ids == i, holder, 0)
        notes = notes_ref[i].astype(f32)
        row = jnp.zeros((1, wide), f32)
        for k in range(each):
            gate = sum(notes[(1 + t) * each + k : (1 + t) * each + k + 1, :] for t in range(3))
            row = row + jnp.where(notes[k : k + 1, :] == me.astype(f32), gate, 0.0)
        table_ref[i : i + 1, :] = row
    exact = lax.Precision.HIGHEST
    slot = lax.broadcasted_iota(i32, (wide, longest), 0) - lax.broadcasted_iota(i32, (wide, longest), 1)
    down = lax.broadcasted_iota(i32, (trajs, wide), 0)
    across = lax.broadcasted_iota(i32, (trajs, wide), 1)
    row_ids = lax.broadcasted_iota(i32, (1, total), 1)
    offset_ids = lax.broadcasted_iota(i32, (longest, total), 0)
    weights = jnp.zeros((1, total), f32)
    for i, holder in enumerate(holders):
        own_slots = dot(table_ref[...], jnp.where(slot == holder * longest, 1.0, 0.0), precision=exact)
        notes = notes_ref[i].astype(f32)
        at = 4 * each + halves
        sent = jnp.where(holder_of.astype(f32) == notes[at : at + 1, :count], 1.0, 0.0)
        by_traj = dot(own_slots, sent, tn_dims, precision=exact)
        for half in range(halves):
            lengths = notes[4 * each + half : 4 * each + half + 1, :]
            length = jnp.sum(jnp.where(across == down, lengths, 0.0), axis=1, keepdims=True).astype(i32)
            start = jnp.sum(jnp.where(across < down, lengths, 0.0), axis=1, keepdims=True).astype(i32)
            place = row_ids - (i * halves + half) * per_half
            inside = (place >= start) & (place < start + length)
            offset = place - jnp.sum(jnp.where(inside, start, 0), axis=0, keepdims=True)
            spread = dot(by_traj[:, half * trajs : (half + 1) * trajs], jnp.where(inside, 1.0, 0.0), precision=exact)
            weights = weights + jnp.sum(jnp.where(offset_ids == offset, spread, 0.0), axis=0, keepdims=True)
    weights_ref[...] = weights


def tile_copies(ref, held, tile, sems):
    places = [pl.ds(start, tile) for start in range(0, held.shape[0], tile)]
    return [pltpu.make_async_copy(ref.at[p], held.at[p], sems.at[i]) for i, p in enumerate(places)]


def start_all(*groups):
    for copies in groups:
        for copy in copies:
            copy.start()


def wait_all(copies):
    for copy in copies:
        copy.wait()


def activation(features, up_tile, inputs, weight):
    before_act = dot(up_tile, inputs, nt_dims) * features ** (-0.5)
    sigmoid = 1.0 / (1.0 + jnp.exp(-before_act))
    return (before_act * sigmoid * weight).astype(bf16), sigmoid * (1.0 + before_act * (1.0 - sigmoid)) * weight


def new_tile(old, step, change, rows):
    return (old.astype(f32) - (step_size * step) * dot(change, rows)).astype(bf16)


def learner_kernel(parts, height, features, hidden, tile, part_ref, weight_ref, *refs):
    units, (up_ref, down_ref, new_up_ref, new_down_ref, inputs, grads, up, down, new_up, new_down) = refs[:-13], refs[-13:-3]
    row_sems, sems, out_sems = refs[-3:]
    in_copies, grad_copies = gathered_copies(part_ref[0], parts, height, units, inputs, grads, row_sems)
    up_copies = tile_copies(up_ref, up, tile, sems.at[0])
    down_copies = tile_copies(down_ref, down, tile, sems.at[1])
    up_outs = tile_copies(new_up, new_up_ref, tile, out_sems.at[0])
    down_outs = tile_copies(new_down, new_down_ref, tile, out_sems.at[1])
    start_all(up_copies[:1], in_copies, down_copies[:1], grad_copies, up_copies[1:], down_copies[1:])
    weight = weight_ref[...]
    for i in range(len(up_copies)):
        here = pl.ds(i * tile, tile)
        up_copies[i].wait()
        if i == 0:
            wait_all(in_copies)
        activated, slope = activation(features, up[here, :], inputs[...], weight)
        down_copies[i].wait()
        if i == 0:
            wait_all(grad_copies)
        pre_grad = (dot(down[here, :], grads[...], nt_dims) * hidden ** (-0.5) * slope).astype(bf16)
        new_down[here, :] = new_tile(down[here, :], hidden ** (-0.5), activated, grads[...])
        down_outs[i].start()
        new_up[here, :] = new_tile(up[here, :], features ** (-0.5), pre_grad, inputs[...])
        up_outs[i].start()
    wait_all(up_outs + down_outs)


def forward_kernel(parts, height, features, tile, part_ref, weight_ref, *refs):
    units, (up_ref, inputs, grads, activated, slopes, up, row_sems, sems) = refs[:-8], refs[-8:]
    in_copies, grad_copies = gathered_copies(part_ref[0], parts, height, units, inputs, grads, row_sems)
    up_copies = tile_copies(up_ref, up, tile, sems)
    start_all(up_copies[:1], in_copies, up_copies[1:], grad_copies)
    wait_all(in_copies)
    for i, copy in enumerate(up_copies):
        here = pl.ds(i * tile, tile)
        copy.wait()
        activated[here, :], slopes[here, :] = activation(features, up[here, :], inputs[...], weight_ref[...])
    wait_all(grad_copies)


def late_kernel(features, hidden, tile, go_ref, *refs):
    refs, (up, down, inputs, grads, activated, slopes, new_up, new_down, row_sems, sems, out_sems) = refs[:-11], refs[-11:]
    up_ref, down_ref, inputs_ref, grads_ref, activated_ref, slopes_ref, _, _, new_up_ref, new_down_ref = refs

    @pl.when(go_ref[0] == 1)
    def _():
        up_copies = tile_copies(up_ref, up, tile, sems.at[0])
        down_copies = tile_copies(down_ref, down, tile, sems.at[1])
        active_copies = tile_copies(activated_ref, activated, tile, sems.at[2])
        slope_copies = tile_copies(slopes_ref, slopes, tile, sems.at[3])
        grad_copy = pltpu.make_async_copy(grads_ref, grads, row_sems.at[0])
        in_copy = pltpu.make_async_copy(inputs_ref, inputs, row_sems.at[1])
        up_outs = tile_copies(new_up, new_up_ref, tile, out_sems.at[0])
        down_outs = tile_copies(new_down, new_down_ref, tile, out_sems.at[1])
        start_all([grad_copy], down_copies[:1], slope_copies[:1], active_copies[:1], [in_copy])
        start_all(up_copies[:1], down_copies[1:], slope_copies[1:], active_copies[1:], up_copies[1:])
        grad_copy.wait()
        for i in range(len(up_copies)):
            here = pl.ds(i * tile, tile)
            down_copies[i].wait()
            slope_copies[i].wait()
            hidden_grad = dot(down[here, :], grads[...], nt_dims) * hidden ** (-0.5)
            pre_grad = (hidden_grad * slopes[here, :]).astype(bf16)
            active_copies[i].wait()
            new_down[here, :] = new_tile(down[here, :], hidden ** (-0.5), activated[here, :], grads[...])
            down_outs[i].start()
            if i == 0:
                in_copy.wait()
            up_copies[i].wait()
            new_up[here, :] = new_tile(up[here, :], features ** (-0.5), pre_grad, inputs[...])
            up_outs[i].start()
        wait_all(up_outs + down_outs)


def join_kernel(parts, row_count, part_ref, *refs):
    pieces, (left_ref, right_ref, joined_ref) = refs[:parts], refs[parts:]
    width = pieces[0].shape[1]
    blocks = pieces[0].shape[0] // row_count
    for j, piece in enumerate(pieces):
        start = lax.rem(part_ref[0] + parts - j, parts) * (blocks * width)
        for block in range(blocks):
            columns = pl.ds(pl.multiple_of(start + block * width, width), width)
            joined_ref[:, columns] = piece[block * row_count : (block + 1) * row_count, :]
    half = left_ref.shape[1]
    left_ref[...] = joined_ref[:, :half]
    right_ref[...] = joined_ref[:, half:]


def unset_kernel(*refs):
    pass


def unset(*like):
    arrays = pl.pallas_call(
        unset_kernel,
        out_shape=[jax.ShapeDtypeStruct(a.shape, a.dtype) for a in like],
        out_specs=[anywhere] * len(like),
        cost_estimate=costs(1, 1),
    )()
    return tuple(arrays)


def on_device(
    decode_states,
    norm_gain,
    decode_routes,
    decode_gates,
    up_weight,
    down_weight,
    traj_inputs,
    traj_cotangents,
    traj_lengths,
    packing,
    learner_routes,
    learner_gates,
):
    experts, parts = lax.axis_size("exp"), lax.axis_size("dp")
    is_rollout = lax.axis_index("sect") == 0
    go = is_rollout.astype(i32).reshape(1)
    me = lax.axis_index("exp")
    part_ref = lax.axis_index("dp").reshape(1).astype(i32)
    up_here, down_here = up_weight[0, 0], down_weight[0, 0]
    hidden_here, features = up_here.shape
    hidden = hidden_here * parts
    steps, row_count, routes_each = decode_routes.shape
    half_steps = steps // 2
    share = features // parts
    blocks = share // lanes
    capacity = 3 * row_count * routes_each // (2 * experts)
    slots = experts * capacity
    stacked = blocks * row_count
    moved = blocks * slots
    tile = hidden_here // 3
    line = 8
    per_half = traj_inputs.shape[1]
    gathered = experts * 2 * per_half
    height = 4 * per_half + note_rows

    routes = jnp.swapaxes(decode_routes, 1, 2).reshape(steps * routes_each, row_count)
    gates = jnp.swapaxes(decode_gates, 1, 2).reshape(steps * routes_each, row_count)
    targets, gates, states, payload, own_rows = pl.pallas_call(
        functools.partial(prepare_kernel, experts, capacity),
        out_shape=[
            jax.ShapeDtypeStruct((steps, routes_each, stacked), i32),
            jax.ShapeDtypeStruct((steps * routes_each, stacked), f32),
            jax.ShapeDtypeStruct((stacked, lanes), f32),
            jax.ShapeDtypeStruct((moved, lanes), bf16),
            jax.ShapeDtypeStruct((2 * per_half, share), bf16),
        ],
        in_specs=[smem, vmem, vmem] + [stays] * 3,
        scratch_shapes=[pltpu.VMEM((row_count, share), bf16), pltpu.SemaphoreType.DMA((3,))],
        compiler_params=fits(60),
        cost_estimate=costs(1, 1),
    )(part_ref, routes, gates, decode_states, traj_inputs[0], traj_cotangents[0])

    crossed_rows = flipped(own_rows, "sect", 1)
    up_sent, down_sent, crossed_rows = lax.optimization_barrier((up_here, down_here, crossed_rows))
    up_there = lax.ppermute(up_sent, "sect", [(1, 0)])
    down_there = lax.ppermute(down_sent, "sect", [(1, 0)])

    gain = norm_gain.reshape(1, features)
    def expert_forward(arrived, up_mat, down_mat):
        return pl.pallas_call(
            functools.partial(expert_kernel, parts, slots, capacity, features, hidden),
            out_shape=[jax.ShapeDtypeStruct((moved, lanes), bf16)] * parts,
            in_specs=[smem, vmem] + [vmem] * parts + [stays, stays],
            scratch_shapes=[
                pltpu.VMEM((hidden_here, features), bf16),
                pltpu.VMEM((hidden_here, features), bf16),
                pltpu.VMEM((slots, features), bf16),
                pltpu.VMEM((moved, lanes), bf16),
                pltpu.VMEM((moved, moved), bf16),
                pltpu.SemaphoreType.DMA((2,)),
            ],
            compiler_params=fits(48),
            cost_estimate=costs(1, 1),
        )(part_ref, gain, *arrived, up_mat, down_mat)

    def decode_step(step, states, payload, up_mat, down_mat):
        last = step in (half_steps - 1, steps - 1)
        arrived = lax.all_to_all(payload, "exp", split_axis=0, concat_axis=0, tiled=True)
        arrived = [arrived] + [shifted(arrived, "dp", j) for j in range(1, parts)]
        partials = expert_forward(arrived, up_mat, down_mat)
        received = [shifted(partials[j], "dp", j) for j in range(1, parts)]
        summed = sum((r.astype(f32) for r in received), partials[0].astype(f32)).astype(bf16)
        returned = lax.all_to_all(summed, "exp", split_axis=0, concat_axis=0, tiled=True)
        outs = [
            jax.ShapeDtypeStruct((stacked, lanes), f32),
            jax.ShapeDtypeStruct((stacked if last else moved, lanes), bf16),
        ]
        results = pl.pallas_call(
            functools.partial(combine_kernel, step, last),
            out_shape=outs,
            compiler_params=fits(16),
            cost_estimate=costs(1, 1),
        )(targets, gates, states, returned)
        return tuple(results)
    def learner_rows(halves):
        wide = learner_routes.shape[0]
        notes = [learner_routes.T, learner_gates.T, traj_lengths[0], packing]
        unit = pl.pallas_call(
            unit_kernel,
            out_shape=jax.ShapeDtypeStruct((height, share), bf16),
            in_specs=[anywhere] * 2 + [vmem] * 4,
            scratch_shapes=[pltpu.SemaphoreType.DMA((4,))],
            compiler_params=fits(16),
            cost_estimate=costs(1, 1),
        )(*halves, *notes)
        others, group = [0], experts
        while group > line:
            group = group // 2
            unit = jnp.concatenate([unit, flipped(unit, "exp", group)])
            others = others + [o ^ group for o in others]
        far = group // 2
        shifts = sorted(range(1, far), key=lambda s: (min(s, far - s), s))

        def along(s):
            pairs = [(i, i // group * group + (i + 2 * s) % group) for i in range(experts)]
            return lax.ppermute(unit, "exp", pairs)

        near = jnp.concatenate([along(s) for s in shifts[:-1]])
        sides = [flipped(unit, "exp", 1), flipped(near, "exp", 1)]
        last = along(shifts[-1])
        units = [jnp.concatenate([unit, sides[0], near]), sides[1], last, flipped(last, "exp", 1)]
        places = [(0, 0), (1, 0)] + [(flip, s) for flip in range(2) for s in shifts[:-1]]
        places = places + [(0, shifts[-1]), (1, shifts[-1])]
        sources = [(group, flip, 2 * s, o) for flip, s in places for o in others]
        return units, sources

    def with_parts(units, sources):
        units = list(units)
        others = [shifted(u, "dp", j) for j in range(1, parts) for u in units]
        wide = learner_routes.shape[0]
        weights = pl.pallas_call(
            functools.partial(
                weights_kernel, height, 2, learner_routes.shape[1], traj_lengths.shape[2], wide, sources
            ),
            out_shape=jax.ShapeDtypeStruct((1, gathered), f32),
            in_specs=[smem] + [anywhere] * len(units),
            scratch_shapes=[
                pltpu.VMEM((experts, note_rows, wide), bf16),
                pltpu.VMEM((experts, wide), f32),
                pltpu.SemaphoreType.DMA((experts,)),
            ],
            compiler_params=fits(16),
            cost_estimate=costs(1, 1),
        )(me.reshape(1).astype(i32), *units)
        return units + others, weights

    rows_like = jax.ShapeDtypeStruct((gathered, features), bf16)
    weight_like = jax.ShapeDtypeStruct((hidden_here, features), bf16)
    active_like = jax.ShapeDtypeStruct((hidden_here, gathered), bf16)
    slopes_like = jax.ShapeDtypeStruct((hidden_here, gathered), f32)
    row_space = [pltpu.VMEM(rows_like.shape, bf16)] * 2
    weight_space = pltpu.VMEM(weight_like.shape, bf16)

    def sems_of(*shape):
        return pltpu.SemaphoreType.DMA(shape)

    def update(units, weights, up_mat, down_mat):
        return pl.pallas_call(
            functools.partial(learner_kernel, parts, height, features, hidden, tile),
            out_shape=[weight_like] * 2,
            in_specs=[smem, vmem] + [anywhere] * (len(units) + 2),
            out_specs=[anywhere] * 2,
            scratch_shapes=row_space + [weight_space] * 4 + [sems_of(2 * parts * experts), sems_of(2, 3), sems_of(2, 3)],
            compiler_params=fits(56),
            cost_estimate=costs(1, 1),
        )(part_ref, weights, *units, up_mat, down_mat)

    def update_forward(units, weights):
        return pl.pallas_call(
            functools.partial(forward_kernel, parts, height, features, tile),
            out_shape=[rows_like, rows_like, active_like, slopes_like],
            in_specs=[smem, vmem] + [anywhere] * (len(units) + 1),
            scratch_shapes=[weight_space, sems_of(2 * parts * experts), sems_of(3)],
            compiler_params=fits(56),
            cost_estimate=costs(1, 1),
        )(part_ref, weights, *units, up_there)

    def update_late(known, new_up, new_down):
        space = [weight_space] * 2 + row_space + [pltpu.VMEM(a.shape, a.dtype) for a in (active_like, slopes_like)]
        return pl.pallas_call(
            functools.partial(late_kernel, features, hidden, tile),
            out_shape=[weight_like] * 2,
            in_specs=[smem] + [stays] * 8,
            out_specs=[anywhere] * 2,
            scratch_shapes=space + [weight_space] * 2 + [sems_of(2), sems_of(4, 3), sems_of(2, 3)],
            input_output_aliases={7: 0, 8: 1},
            compiler_params=fits(60),
            cost_estimate=costs(1, 1),
        )(go, up_there, down_there, *known, new_up, new_down)

    final_like = jax.ShapeDtypeStruct((stacked, lanes), bf16)
    block_rows = height * max(1, experts // line)
    gather_like = [jax.ShapeDtypeStruct((block_rows * n, share), bf16) for n in (line // 2, line // 2 - 2, 1, 1)]

    sources = []

    def first_rollout():
        return decode_step(0, states, payload, up_here, down_here) + unset(*gather_like)

    def first_learner():
        units, places = learner_rows([crossed_rows, own_rows])
        sources.append(places)
        return (states, payload) + tuple(units)

    states, payload, *rows = lax.cond(is_rollout, first_rollout, first_learner)

    def second_rollout():
        now, sent = states, payload
        for step in range(1, half_steps):
            now, sent = decode_step(step, now, sent, up_here, down_here)
        return (now,) + tuple(unset(up_here, down_here))

    def second_learner():
        units, weights = with_parts(rows, sources[0])
        return (states,) + tuple(update(units, weights, up_here, down_here))

    states, new_up, new_down = lax.cond(is_rollout, second_rollout, second_learner)
    states_there = lax.ppermute(states, "sect", [(0, 1)])

    def third_rollout():
        return (states, payload) + tuple(learner_rows([own_rows, crossed_rows])[0])

    def third_learner():
        sent = pl.pallas_call(
            functools.partial(dispatch_kernel, half_steps),
            out_shape=jax.ShapeDtypeStruct((moved, lanes), bf16),
            compiler_params=fits(16),
            cost_estimate=costs(1, 1),
        )(targets, states_there)
        return decode_step(half_steps, states_there, sent, new_up, new_down) + unset(*gather_like)

    states, payload, *rows = lax.cond(is_rollout, third_rollout, third_learner)

    def fourth_rollout():
        return unset(final_like) + tuple(update_forward(*with_parts(rows, sources[0])))

    def fourth_learner():
        now, sent = states, payload
        for step in range(half_steps + 1, steps):
            now, sent = decode_step(step, now, sent, new_up, new_down)
        return (sent,) + unset(rows_like, rows_like, active_like, slopes_like)

    mine, *known = lax.cond(is_rollout, fourth_rollout, fourth_learner)

    pieces = [mine] + [shifted(mine, "dp", j) for j in range(1, parts)]
    left, right = pl.pallas_call(
        functools.partial(join_kernel, parts, row_count),
        out_shape=[jax.ShapeDtypeStruct((row_count, features // 2), bf16)] * 2,
        in_specs=[smem] + [vmem] * parts,
        scratch_shapes=[pltpu.VMEM((row_count, features), bf16)],
        cost_estimate=costs(1, 1),
    )(part_ref, *pieces)
    delivered = lax.ppermute(left, "sect", [(1, 0)])
    new_up, new_down = update_late(known, new_up, new_down)
    final_states = jnp.where(is_rollout, delivered, right)
    return final_states, new_up[None, None], new_down[None, None]


def solution(mesh):
    in_specs = (
        P("exp", None),
        P(),
        P(None, "exp", None),
        P(None, "exp", None),
        P("sect", "exp", "dp", None),
        P("sect", "exp", "dp", None),
        P("sect", "exp", None),
        P("sect", "exp", None),
        P("exp", None, None),
        P("exp", None),
        P("exp", None),
        P("exp", None),
    )
    out_specs = (P("exp", "sect"), P("sect", "exp", "dp", None), P("sect", "exp", "dp", None))
    return jax.shard_map(on_device, mesh=mesh, in_specs=in_specs, out_specs=out_specs, check_vma=False)
```

```python
import functools

import jax
import jax.numpy as jnp
from jax import lax
from jax.experimental import pallas as pl
from jax.experimental.pallas import tpu as pltpu
from jax.sharding import PartitionSpec as P

step_size = 3.0
norm_eps = 1e-06
lanes = 256
note_rows = 16
f32, bf16, i32 = jnp.float32, jnp.bfloat16, jnp.int32
nt_dims = (((1,), (1,)), ((), ()))
tn_dims = (((0,), (0,)), ((), ()))
smem = pl.BlockSpec(memory_space=pltpu.SMEM)
vmem = pl.BlockSpec(memory_space=pltpu.VMEM)
anywhere = pl.BlockSpec(memory_space=pl.ANY)
stays = pl.BlockSpec(memory_space=pltpu.HBM)


def shifted(array, axis, by):
    size = lax.axis_size(axis)
    return lax.ppermute(array, axis, [(i, (i + by) % size) for i in range(size)])


def flipped(array, axis, bit):
    return lax.ppermute(array, axis, [(i, i ^ bit) for i in range(lax.axis_size(axis))])


def fits(megabytes):
    return pltpu.CompilerParams(vmem_limit_bytes=megabytes * 1024 * 1024)


def costs(flops, moved):
    return pl.CostEstimate(flops=flops, bytes_accessed=moved, transcendentals=0)


def dot(a, b, dims=(((1,), (0,)), ((), ())), precision=None):
    return lax.dot_general(a, b, dims, precision=precision, preferred_element_type=f32)


def one_hot(rows, targets_ref):
    ids = lax.broadcasted_iota(i32, (rows, targets_ref.shape[1]), 0)
    hits = [jnp.where(ids == targets_ref[k : k + 1, :], 1.0, 0.0) for k in range(targets_ref.shape[0])]
    return sum(hits[1:], hits[0]).astype(bf16)


def prepare_kernel(
    experts, capacity, part_ref, routes_ref, gates_ref, all_rows_ref, inputs_ref, grads_ref,
    targets_ref, tiled_ref, states_ref, payload_ref, own_ref, rows_ref, sems,
):
    row_count, share = rows_ref.shape
    steps, routes_each = targets_ref.shape[:2]
    stacked, width = states_ref.shape
    blocks = stacked // row_count
    own = pl.ds(pl.multiple_of(part_ref[0] * share, share), share)
    held = inputs_ref.shape[0]
    row_copy = pltpu.make_async_copy(all_rows_ref.at[:, own], rows_ref, sems.at[0])
    copies = [
        pltpu.make_async_copy(inputs_ref.at[:, own], own_ref.at[pl.ds(0, held)], sems.at[1]),
        pltpu.make_async_copy(grads_ref.at[:, own], own_ref.at[pl.ds(held, held)], sems.at[2]),
    ]
    row_copy.start()
    for copy in copies:
        copy.start()
    before = lax.broadcasted_iota(i32, (row_count, stacked), 0)
    after = lax.rem(lax.broadcasted_iota(i32, (row_count, stacked), 1), row_count)
    repeat = jnp.where(before == after, 1.0, 0.0)
    earlier = jnp.where(before < after, 1.0, 0.0).astype(bf16)
    every = jnp.ones((row_count, stacked), bf16)
    block_of = lax.div(lax.broadcasted_iota(i32, (1, stacked), 1), row_count)
    expert_ids = lax.broadcasted_iota(i32, (experts, row_count), 0)
    tall_ids = lax.broadcasted_iota(i32, (experts, stacked), 0)
    routes = dot(routes_ref[...].astype(f32), repeat, precision=lax.Precision.HIGHEST)
    routes = (routes + 0.5).astype(i32)
    tiled_ref[...] = dot(gates_ref[...], repeat, precision=lax.Precision.HIGHEST)
    for step in range(steps):
        seen = jnp.zeros((experts, stacked), f32)
        for k in range(routes_each):
            at = step * routes_each + k
            member = jnp.where(expert_ids == routes_ref[at : at + 1, :], 1.0, 0.0).astype(bf16)
            route = routes[at : at + 1, :]
            ahead = dot(member, earlier) + seen
            rank = jnp.sum(jnp.where(tall_ids == route, ahead, 0.0), axis=0, keepdims=True)
            seen = seen + dot(member, every)
            place = (route * blocks + block_of) * capacity + (rank + 0.5).astype(i32)
            targets_ref[step, k : k + 1, :] = place
    row_copy.wait()
    for block in range(blocks):
        columns = slice(block * width, (block + 1) * width)
        states_ref[block * row_count : (block + 1) * row_count, :] = rows_ref[:, columns].astype(f32)
    payload_ref[...] = dot(one_hot(payload_ref.shape[0], targets_ref.at[0]), states_ref[...].astype(bf16)).astype(bf16)
    for copy in copies:
        copy.wait()


def dispatch_kernel(step, targets_ref, states_ref, payload_ref):
    payload_ref[...] = dot(one_hot(payload_ref.shape[0], targets_ref.at[step]), states_ref[...].astype(bf16)).astype(bf16)


def combine_kernel(step, last, targets_ref, gates_ref, states_ref, returned_ref, new_ref, payload_ref):
    ids = lax.broadcasted_iota(i32, (returned_ref.shape[0], states_ref.shape[0]), 0)
    weights = jnp.zeros(ids.shape, f32)
    routes_each = targets_ref.shape[1]
    for k in range(routes_each):
        at = step * routes_each + k
        weights = weights + jnp.where(ids == targets_ref[step, k : k + 1, :], gates_ref[at : at + 1, :], 0.0)
    high = weights.astype(bf16)
    low = (weights - high.astype(f32)).astype(bf16)
    returned = returned_ref[...]
    states = states_ref[...] + (dot(high, returned, tn_dims) + dot(low, returned, tn_dims))
    new_ref[...] = states
    if last:
        payload_ref[...] = states.astype(bf16)
    else:
        payload_ref[...] = dot(one_hot(returned.shape[0], targets_ref.at[step + 1]), states.astype(bf16)).astype(bf16)


def expert_kernel(parts, slots, capacity, features, hidden, part_ref, gain_ref, *refs):
    arrived, (up_ref, down_ref) = refs[:parts], refs[parts : parts + 2]
    outs = refs[parts + 2 : 2 * parts + 2]
    up_held, down_held, normed_ref, stack_ref, order_ref, sems = refs[2 * parts + 2 :]
    width = arrived[0].shape[1]
    blocks = features // (parts * width)
    me = part_ref[0]
    up_copy = pltpu.make_async_copy(up_ref, up_held, sems.at[0])
    down_copy = pltpu.make_async_copy(down_ref, down_held, sems.at[1])
    up_copy.start()
    down_copy.start()
    moved = blocks * slots
    column = lax.broadcasted_iota(i32, (1, moved), 1)
    slot = lax.rem(column, slots)
    target = (lax.div(slot, capacity) * blocks + lax.div(column, slots)) * capacity + lax.rem(slot, capacity)
    hits = lax.broadcasted_iota(i32, (moved, moved), 0) == target
    order_ref[...] = jnp.where(hits, 1.0, 0.0).astype(bf16)
    square = jnp.zeros((slots, 1), f32)
    stacks = []
    for ref in arrived:
        stack = dot(order_ref[...], ref[...], tn_dims)
        stacks.append(stack)
        for block in range(blocks):
            rows = stack[block * slots : (block + 1) * slots]
            square = square + jnp.sum(rows * rows, axis=1, keepdims=True)
    scale = lax.rsqrt(square * (1.0 / features) + norm_eps)
    for j, stack in enumerate(stacks):
        start = lax.rem(me + parts - j, parts) * (blocks * width)
        for block in range(blocks):
            rows = stack[block * slots : (block + 1) * slots]
            columns = pl.ds(pl.multiple_of(start + block * width, width), width)
            normed_ref[:, columns] = (rows * scale * gain_ref[:, columns]).astype(bf16)
    up_copy.wait()
    before_act = dot(normed_ref[...], up_held[...], nt_dims) * features ** (-0.5)
    activated = (before_act / (1.0 + jnp.exp(-before_act))).astype(bf16)
    down_copy.wait()
    normed_ref[...] = (dot(activated, down_held[...]) * hidden ** (-0.5)).astype(bf16)
    for j, out_ref in enumerate(outs):
        start = lax.rem(me + j, parts) * (blocks * width)
        for block in range(blocks):
            columns = pl.ds(pl.multiple_of(start + block * width, width), width)
            stack_ref[block * slots : (block + 1) * slots, :] = normed_ref[:, columns]
        out_ref[...] = dot(order_ref[...], stack_ref[...]).astype(bf16)


def gathered_copies(part, parts, height, units, inputs_ref, grads_ref, sems):
    per_part = len(units) // parts
    width = units[0].shape[1]
    rows = (height - note_rows) // 2
    in_copies, grad_copies = [], []
    for j in range(parts):
        columns = pl.ds(pl.multiple_of(lax.rem(part + parts - j, parts) * width, width), width)
        blocks = [(u, at) for u in units[j * per_part : (j + 1) * per_part] for at in range(0, u.shape[0], height)]
        for i, (unit, at) in enumerate(blocks):
            place, sem = pl.ds(i * rows, rows), 2 * (j * len(blocks) + i)
            source = unit.at[pl.ds(at, rows)]
            in_copies.append(pltpu.make_async_copy(source, inputs_ref.at[place, columns], sems.at[sem]))
            source = unit.at[pl.ds(at + rows, rows)]
            grad_copies.append(pltpu.make_async_copy(source, grads_ref.at[place, columns], sems.at[sem + 1]))
    return in_copies, grad_copies


def unit_kernel(first_ref, second_ref, routes_ref, gates_ref, lengths_ref, shards_ref, unit_ref, sems):
    held = first_ref.shape[0] // 2
    copies = []
    for i, ref in enumerate((first_ref, second_ref)):
        for j in range(2):
            place = pl.ds((2 * j + i) * held, held)
            source = ref.at[pl.ds(j * held, held)]
            copies.append(pltpu.make_async_copy(source, unit_ref.at[place], sems.at[2 * i + j]))
    for copy in copies:
        copy.start()
    wide = routes_ref.shape[1]

    def widened(ref):
        count = ref.shape[1]
        places = lax.broadcasted_iota(i32, (count, wide), 0) == lax.broadcasted_iota(i32, (count, wide), 1)
        return dot(ref[...].astype(f32), jnp.where(places, 1.0, 0.0))

    gates = gates_ref[...]
    terms = []
    for _ in range(3):
        terms.append(gates.astype(bf16).astype(f32))
        gates = gates - terms[-1]
    tables = [routes_ref[...].astype(f32)] + terms + [widened(lengths_ref), widened(shards_ref)]
    ids = lax.broadcasted_iota(i32, (note_rows, wide), 0)
    notes, at = jnp.zeros((note_rows, wide), f32), 0
    for table in tables:
        for row in range(table.shape[0]):
            notes = notes + jnp.where(ids == at, table[row : row + 1, :], 0.0)
            at += 1
    base = 4 * held
    unit_ref[base:, :] = jnp.zeros((note_rows, unit_ref.shape[1]), bf16)
    unit_ref[base:, :wide] = notes.astype(bf16)
    for copy in copies:
        copy.wait()


def weights_kernel(height, halves, each, trajs, wide, sources, me_ref, *refs):
    units, (weights_ref, notes_ref, table_ref, facts_ref, sems) = refs[:-5], refs[-5:]
    blocks = [(u, at) for u in units for at in range(0, u.shape[0], height)]
    count = len(blocks)
    per_half = (height - note_rows) // (2 * halves)
    longest = wide // count
    total = weights_ref.shape[1]
    copies = []
    for i, (unit, at) in enumerate(blocks):
        source = unit.at[pl.ds(at + height - note_rows, note_rows), pl.ds(0, wide)]
        copies.append(pltpu.make_async_copy(source, notes_ref.at[i], sems.at[i]))
    for copy in copies:
        copy.start()
    for copy in copies:
        copy.wait()
    me = me_ref[0]
    ids = lax.broadcasted_iota(i32, (count, 1), 0)
    places = lax.broadcasted_iota(i32, (note_rows, wide), 1)
    holder_of = jnp.zeros((count, 1), f32)
    for i, (group, flip, far, near) in enumerate(sources):
        place = lax.rem((lax.rem(me, group) ^ flip) + group - far, group)
        holder = ((lax.div(me, group) * group + place) ^ near).astype(f32)
        holder_of = holder_of + jnp.where(ids == i, holder, 0.0)
        notes = notes_ref[i].astype(f32)
        row = jnp.zeros((1, wide), f32)
        for k in range(each):
            gate = sum(notes[(1 + t) * each + k : (1 + t) * each + k + 1, :] for t in range(3))
            row = row + jnp.where(notes[k : k + 1, :] == me.astype(f32), gate, 0.0)
        table_ref[i : i + 1, :] = row
        for half in range(halves):
            shards = pltpu.roll(notes, (trajs - half * trajs) % wide, 1) if half != 1 else notes
            shards = jnp.where((places >= trajs) & (places < 2 * trajs), shards, 0.0)
            shards = jnp.where(places == 2 * trajs, holder, shards)
            facts = notes[4 * each + half : 4 * each + half + 1, :] + shards[4 * each + halves : 4 * each + halves + 1, :]
            facts_ref[i * halves + half : i * halves + half + 1, :] = facts
    facts = facts_ref[...]
    down, across = [lax.broadcasted_iota(i32, (wide, wide), d) for d in (0, 1)]
    starts = dot(facts, jnp.where((down < across) & (down < trajs), 1.0, 0.0))
    row_ids = lax.broadcasted_iota(i32, (count * halves, total), 1)
    of_row = lax.div(row_ids, per_half) == lax.broadcasted_iota(i32, (count * halves, total), 0)
    of_row = jnp.where(of_row, 1.0, 0.0)
    facts, starts = dot(facts, of_row, tn_dims), dot(starts, of_row, tn_dims)[:trajs]
    place = lax.rem(lax.broadcasted_iota(i32, (1, total), 1), per_half).astype(f32)
    inside = (place >= starts) & (place < starts + facts[:trajs])
    offset = jnp.sum(jnp.where(inside, place - starts, 0.0), axis=0, keepdims=True)
    shard = jnp.sum(jnp.where(inside, facts[trajs : 2 * trajs], 0.0), axis=0, keepdims=True)
    slot = (facts[2 * trajs : 2 * trajs + 1] * longest + offset + 0.5).astype(i32)
    chosen = jnp.where(lax.broadcasted_iota(i32, (wide, total), 0) == slot, 1.0, 0.0)
    gates = dot(table_ref[...], chosen, precision=lax.Precision.HIGHEST)
    weights_ref[...] = jnp.sum(jnp.where(holder_of == shard, gates, 0.0), axis=0, keepdims=True)


def tile_copies(ref, held, tile, sems):
    places = [pl.ds(start, tile) for start in range(0, ref.shape[0], tile)]
    return [pltpu.make_async_copy(ref.at[p], held.at[p], sems.at[i]) for i, p in enumerate(places)]


def start_all(*groups):
    for copies in groups:
        for copy in copies:
            copy.start()


def wait_all(copies):
    for copy in copies:
        copy.wait()


def activation(features, up_tile, inputs, weight):
    before_act = dot(up_tile, inputs, nt_dims) * features ** (-0.5)
    sigmoid = 1.0 / (1.0 + jnp.exp(-before_act))
    return (before_act * sigmoid * weight).astype(bf16), sigmoid * (1.0 + before_act * (1.0 - sigmoid)) * weight


def new_tile(old, step, change, rows):
    return (old.astype(f32) - (step_size * step) * dot(change, rows)).astype(bf16)


def cut_kernel(go_ref, up_ref, down_ref, first_ref, second_ref, held, sems):
    rows, most = up_ref.shape[0], first_ref.shape[0]

    @pl.when(go_ref[0] == 0)
    def _():
        moves = [
            (up_ref, pl.ds(0, rows), first_ref.at[pl.ds(0, rows)]),
            (down_ref.at[pl.ds(0, most - rows)], pl.ds(rows, most - rows), first_ref.at[pl.ds(rows, most - rows)]),
            (down_ref.at[pl.ds(most - rows, 2 * rows - most)], pl.ds(most, 2 * rows - most), second_ref),
        ]
        ins = [pltpu.make_async_copy(a, held.at[p], sems.at[0, i]) for i, (a, p, _) in enumerate(moves)]
        outs = [pltpu.make_async_copy(held.at[p], b, sems.at[1, i]) for i, (_, p, b) in enumerate(moves)]
        start_all(ins)
        for copy, out in zip(ins, outs):
            copy.wait()
            out.start()
        wait_all(outs)


def update_rows(features, hidden, tile, weight, in_copies, grad_copies, up_from, down_from, up_to, down_to, space):
    inputs, grads, up, down, new_up, new_down, sems, out_sems = space
    up_copies = tile_copies(up_from, up, tile, sems.at[0])
    down_copies = tile_copies(down_from, down, tile, sems.at[1])
    up_outs = tile_copies(new_up, up_to, tile, out_sems.at[0])
    down_outs = tile_copies(new_down, down_to, tile, out_sems.at[1])
    start_all(up_copies[:1], in_copies, down_copies[:1], grad_copies, up_copies[1:], down_copies[1:])
    for i in range(len(up_copies)):
        here = pl.ds(i * tile, tile)
        up_copies[i].wait()
        if i == 0:
            wait_all(in_copies)
        activated, slope = activation(features, up[here, :], inputs[...], weight)
        down_copies[i].wait()
        if i == 0:
            wait_all(grad_copies)
        pre_grad = (dot(down[here, :], grads[...], nt_dims) * hidden ** (-0.5) * slope).astype(bf16)
        new_down[here, :] = new_tile(down[here, :], hidden ** (-0.5), activated, grads[...])
        down_outs[i].start()
        new_up[here, :] = new_tile(up[here, :], features ** (-0.5), pre_grad, inputs[...])
        up_outs[i].start()
    wait_all(up_outs + down_outs)


def learner_kernel(parts, height, features, hidden, tile, part_ref, weight_ref, *refs):
    units, (up_ref, down_ref, new_up_ref, new_down_ref), row_sems, space = refs[:-13], refs[-13:-9], refs[-9], refs[-8:]
    copies = gathered_copies(part_ref[0], parts, height, units, space[0], space[1], row_sems)
    rows = (up_ref, down_ref, new_up_ref, new_down_ref)
    update_rows(features, hidden, tile, weight_ref[...], *copies, *rows, space)


def assemble_kernel(parts, height, part_ref, *refs):
    units, (inputs_ref, grads_ref, sems) = refs[:-3], refs[-3:]
    in_copies, grad_copies = gathered_copies(part_ref[0], parts, height, units, inputs_ref, grads_ref, sems)
    start_all(in_copies, grad_copies)
    wait_all(in_copies + grad_copies)


def late_kernel(features, hidden, tile, places, go_ref, weight_ref, *refs):
    inputs_ref, grads_ref, up_ref, down_ref, _, _, new_up_ref, new_down_ref, row_sems, *space = refs
    count, to, up_at, down_at = places

    @pl.when(go_ref[0] == 1)
    def _():
        in_copies = [pltpu.make_async_copy(inputs_ref, space[0], row_sems.at[0])]
        grad_copies = [pltpu.make_async_copy(grads_ref, space[1], row_sems.at[1])]
        rows = [up_ref.at[pl.ds(up_at, count)], down_ref.at[pl.ds(down_at, count)]]
        rows = rows + [ref.at[pl.ds(to, count)] for ref in (new_up_ref, new_down_ref)]
        update_rows(features, hidden, tile, weight_ref[...], in_copies, grad_copies, *rows, space)


def join_kernel(parts, row_count, part_ref, *refs):
    pieces, (left_ref, right_ref, joined_ref) = refs[:parts], refs[parts:]
    width = pieces[0].shape[1]
    blocks = pieces[0].shape[0] // row_count
    for j, piece in enumerate(pieces):
        start = lax.rem(part_ref[0] + parts - j, parts) * (blocks * width)
        for block in range(blocks):
            columns = pl.ds(pl.multiple_of(start + block * width, width), width)
            joined_ref[:, columns] = piece[block * row_count : (block + 1) * row_count, :]
    half = left_ref.shape[1]
    left_ref[...] = joined_ref[:, :half]
    right_ref[...] = joined_ref[:, half:]


def unset_kernel(*refs):
    pass


def unset(*like):
    arrays = pl.pallas_call(
        unset_kernel,
        out_shape=[jax.ShapeDtypeStruct(a.shape, a.dtype) for a in like],
        out_specs=[anywhere] * len(like),
        cost_estimate=costs(1, 1),
    )()
    return tuple(arrays)


def on_device(
    decode_states,
    norm_gain,
    decode_routes,
    decode_gates,
    up_weight,
    down_weight,
    traj_inputs,
    traj_cotangents,
    traj_lengths,
    packing,
    learner_routes,
    learner_gates,
):
    experts, parts = lax.axis_size("exp"), lax.axis_size("dp")
    is_rollout = lax.axis_index("sect") == 0
    go = is_rollout.astype(i32).reshape(1)
    me = lax.axis_index("exp")
    part_ref = lax.axis_index("dp").reshape(1).astype(i32)
    up_here, down_here = up_weight[0, 0], down_weight[0, 0]
    hidden_here, features = up_here.shape
    hidden = hidden_here * parts
    steps, row_count, routes_each = decode_routes.shape
    half_steps = steps // 2
    share = features // parts
    blocks = share // lanes
    capacity = 3 * row_count * routes_each // (2 * experts)
    slots = experts * capacity
    stacked = blocks * row_count
    moved = blocks * slots
    tile = hidden_here // 3
    line = 8
    per_half = traj_inputs.shape[1]
    gathered = experts * 2 * per_half
    height = 4 * per_half + note_rows

    routes = jnp.swapaxes(decode_routes, 1, 2).reshape(steps * routes_each, row_count)
    gates = jnp.swapaxes(decode_gates, 1, 2).reshape(steps * routes_each, row_count)
    targets, gates, states, payload, own_rows = pl.pallas_call(
        functools.partial(prepare_kernel, experts, capacity),
        out_shape=[
            jax.ShapeDtypeStruct((steps, routes_each, stacked), i32),
            jax.ShapeDtypeStruct((steps * routes_each, stacked), f32),
            jax.ShapeDtypeStruct((stacked, lanes), f32),
            jax.ShapeDtypeStruct((moved, lanes), bf16),
            jax.ShapeDtypeStruct((2 * per_half, share), bf16),
        ],
        in_specs=[smem, vmem, vmem] + [stays] * 3,
        scratch_shapes=[pltpu.VMEM((row_count, share), bf16), pltpu.SemaphoreType.DMA((3,))],
        compiler_params=fits(60),
        cost_estimate=costs(1, 1),
    )(part_ref, routes, gates, decode_states, traj_inputs[0], traj_cotangents[0])

    crossed_rows = flipped(own_rows, "sect", 1)
    up_sent, down_sent, _ = lax.optimization_barrier((up_here, down_here, own_rows))
    cut = hidden_here + 2 * tile
    pieces = pl.pallas_call(
        cut_kernel,
        out_shape=[jax.ShapeDtypeStruct((rows, features), bf16) for rows in (cut, tile)],
        in_specs=[smem] + [stays] * 2,
        out_specs=[stays] * 2,
        scratch_shapes=[pltpu.VMEM((2 * hidden_here, features), bf16), pltpu.SemaphoreType.DMA((2, 3))],
        compiler_params=fits(60),
        cost_estimate=costs(1, 1),
    )(go, up_sent, down_sent)
    first_piece, second_piece, crossed_rows = lax.optimization_barrier((*pieces, crossed_rows))
    first_there = lax.ppermute(first_piece, "sect", [(1, 0)])
    second_there = lax.ppermute(second_piece, "sect", [(1, 0)])

    gain = norm_gain.reshape(1, features)
    def expert_forward(arrived, up_mat, down_mat):
        return pl.pallas_call(
            functools.partial(expert_kernel, parts, slots, capacity, features, hidden),
            out_shape=[jax.ShapeDtypeStruct((moved, lanes), bf16)] * parts,
            in_specs=[smem, vmem] + [vmem] * parts + [stays, stays],
            scratch_shapes=[
                pltpu.VMEM((hidden_here, features), bf16),
                pltpu.VMEM((hidden_here, features), bf16),
                pltpu.VMEM((slots, features), bf16),
                pltpu.VMEM((moved, lanes), bf16),
                pltpu.VMEM((moved, moved), bf16),
                pltpu.SemaphoreType.DMA((2,)),
            ],
            compiler_params=fits(48),
            cost_estimate=costs(1, 1),
        )(part_ref, gain, *arrived, up_mat, down_mat)

    def decode_step(step, states, payload, up_mat, down_mat):
        last = step in (half_steps - 1, steps - 1)
        arrived = lax.all_to_all(payload, "exp", split_axis=0, concat_axis=0, tiled=True)
        arrived = [arrived] + [shifted(arrived, "dp", j) for j in range(1, parts)]
        partials = expert_forward(arrived, up_mat, down_mat)
        received = [shifted(partials[j], "dp", j) for j in range(1, parts)]
        summed = sum((r.astype(f32) for r in received), partials[0].astype(f32)).astype(bf16)
        returned = lax.all_to_all(summed, "exp", split_axis=0, concat_axis=0, tiled=True)
        outs = [
            jax.ShapeDtypeStruct((stacked, lanes), f32),
            jax.ShapeDtypeStruct((stacked if last else moved, lanes), bf16),
        ]
        results = pl.pallas_call(
            functools.partial(combine_kernel, step, last),
            out_shape=outs,
            compiler_params=fits(16),
            cost_estimate=costs(1, 1),
        )(targets, gates, states, returned)
        return tuple(results)
    def learner_rows(halves):
        wide = learner_routes.shape[0]
        notes = [learner_routes.T, learner_gates.T, traj_lengths[0], packing]
        unit = pl.pallas_call(
            unit_kernel,
            out_shape=jax.ShapeDtypeStruct((height, share), bf16),
            in_specs=[anywhere] * 2 + [vmem] * 4,
            scratch_shapes=[pltpu.SemaphoreType.DMA((4,))],
            compiler_params=fits(16),
            cost_estimate=costs(1, 1),
        )(*halves, *notes)
        others, group = [0], experts
        while group > line:
            group = group // 2
            unit = jnp.concatenate([unit, flipped(unit, "exp", group)])
            others = others + [o ^ group for o in others]
        far = group // 2
        shifts = sorted(range(1, far), key=lambda s: (min(s, far - s), s))

        def along(array, s):
            pairs = [(i, i // group * group + (i + 2 * s) % group) for i in range(experts)]
            return lax.ppermute(array, "exp", pairs)

        side = flipped(unit, "exp", 1)
        near = [along(unit, s) for s in shifts[:-1]]
        unit, side, *near = lax.optimization_barrier((unit, side, *near))
        last = along(unit, shifts[-1])
        sides = [flipped(n, "exp", 1) for n in near]
        units = [
            jnp.concatenate([unit, side, *near]),
            jnp.concatenate(sides),
            jnp.concatenate([last, flipped(last, "exp", 1)]),
        ]
        places = [(0, 0), (1, 0)] + [(f, s) for f in range(2) for s in shifts[:-1]] + [(f, shifts[-1]) for f in range(2)]
        sources = [(group, flip, 2 * s, o) for flip, s in places for o in others]
        return units, sources

    def with_parts(units, sources):
        units = list(units)
        others = [shifted(u, "dp", j) for j in range(1, parts) for u in units]
        wide = learner_routes.shape[0]
        weights = pl.pallas_call(
            functools.partial(
                weights_kernel, height, 2, learner_routes.shape[1], traj_lengths.shape[2], wide, sources
            ),
            out_shape=jax.ShapeDtypeStruct((1, gathered), f32),
            in_specs=[smem] + [anywhere] * len(units),
            scratch_shapes=[
                pltpu.VMEM((experts, note_rows, wide), bf16),
                pltpu.VMEM((experts, wide), f32),
                pltpu.VMEM((2 * experts, wide), f32),
                pltpu.SemaphoreType.DMA((experts,)),
            ],
            compiler_params=fits(16),
            cost_estimate=costs(1, 1),
        )(me.reshape(1).astype(i32), *units)
        return units + others, weights

    rows_like = jax.ShapeDtypeStruct((gathered, features), bf16)
    weight_like = jax.ShapeDtypeStruct((hidden_here, features), bf16)
    weights_like = jax.ShapeDtypeStruct((1, gathered), f32)

    def sems_of(*shape):
        return pltpu.SemaphoreType.DMA(shape)

    def update_space(rows):
        held = [pltpu.VMEM((gathered, features), bf16)] * 2 + [pltpu.VMEM((rows, features), bf16)] * 4
        return held + [sems_of(2, rows // tile)] * 2

    def update(units, weights, up_mat, down_mat):
        return pl.pallas_call(
            functools.partial(learner_kernel, parts, height, features, hidden, tile),
            out_shape=[weight_like] * 2,
            in_specs=[smem, vmem] + [anywhere] * (len(units) + 2),
            out_specs=[anywhere] * 2,
            scratch_shapes=[sems_of(2 * parts * experts)] + update_space(hidden_here),
            compiler_params=fits(56),
            cost_estimate=costs(1, 1),
        )(part_ref, weights, *units, up_mat, down_mat)

    def update_late(count, places, piece, new_up, new_down):
        return pl.pallas_call(
            functools.partial(late_kernel, features, hidden, tile, (count, *places)),
            out_shape=[weight_like] * 2,
            in_specs=[smem, vmem] + [stays] * 6,
            out_specs=[anywhere] * 2,
            scratch_shapes=[sems_of(2)] + update_space(count),
            input_output_aliases={6: 0, 7: 1},
            compiler_params=fits(60),
            cost_estimate=costs(1, 1),
        )(go, weights, inputs, grads, first_there, piece, new_up, new_down)

    final_like = jax.ShapeDtypeStruct((stacked, lanes), bf16)
    block_rows = height * max(1, experts // line)
    gather_like = [jax.ShapeDtypeStruct((block_rows * n, share), bf16) for n in (line // 2, line // 2 - 2, 2)]

    sources = []

    def first_rollout():
        return decode_step(0, states, payload, up_here, down_here) + unset(*gather_like)

    def first_learner():
        units, places = learner_rows([crossed_rows, own_rows])
        sources.append(places)
        return (states, payload) + tuple(units)

    states, payload, *rows = lax.cond(is_rollout, first_rollout, first_learner)

    def second_rollout():
        now, sent = states, payload
        for step in range(1, half_steps):
            now, sent = decode_step(step, now, sent, up_here, down_here)
        return (now,) + tuple(unset(up_here, down_here))

    def second_learner():
        units, weights = with_parts(rows, sources[0])
        return (states,) + tuple(update(units, weights, up_here, down_here))

    states, new_up, new_down = lax.cond(is_rollout, second_rollout, second_learner)
    states_there = lax.ppermute(states, "sect", [(0, 1)])

    def third_rollout():
        return (states, payload) + tuple(learner_rows([own_rows, crossed_rows])[0])

    def third_learner():
        sent = pl.pallas_call(
            functools.partial(dispatch_kernel, half_steps),
            out_shape=jax.ShapeDtypeStruct((moved, lanes), bf16),
            compiler_params=fits(16),
            cost_estimate=costs(1, 1),
        )(targets, states_there)
        return decode_step(half_steps, states_there, sent, new_up, new_down) + unset(*gather_like)

    states, payload, *rows = lax.cond(is_rollout, third_rollout, third_learner)

    def fourth_rollout():
        units, weights = with_parts(rows, sources[0])
        whole = pl.pallas_call(
            functools.partial(assemble_kernel, parts, height),
            out_shape=[rows_like] * 2,
            in_specs=[smem] + [anywhere] * len(units),
            scratch_shapes=[sems_of(2 * parts * experts)],
            compiler_params=fits(32),
            cost_estimate=costs(1, 1),
        )(part_ref, *units)
        return unset(final_like) + tuple(whole) + (weights,)

    def fourth_learner():
        now, sent = states, payload
        for step in range(half_steps + 1, steps):
            now, sent = decode_step(step, now, sent, new_up, new_down)
        return (sent,) + unset(rows_like, rows_like, weights_like)

    mine, inputs, grads, weights = lax.cond(is_rollout, fourth_rollout, fourth_learner)

    pieces = [mine] + [shifted(mine, "dp", j) for j in range(1, parts)]
    left, right = pl.pallas_call(
        functools.partial(join_kernel, parts, row_count),
        out_shape=[jax.ShapeDtypeStruct((row_count, features // 2), bf16)] * 2,
        in_specs=[smem] + [vmem] * parts,
        scratch_shapes=[pltpu.VMEM((row_count, features), bf16)],
        cost_estimate=costs(1, 1),
    )(part_ref, *pieces)
    new_up, new_down = update_late(2 * tile, (0, 0, hidden_here), first_there, new_up, new_down)
    left, new_up = lax.optimization_barrier((left, new_up))
    delivered = lax.ppermute(left, "sect", [(1, 0)])
    new_up, new_down = update_late(tile, (2 * tile, 2 * tile, 0), second_there, new_up, new_down)
    final_states = jnp.where(is_rollout, delivered, right)
    return final_states, new_up[None, None], new_down[None, None]


def solution(mesh):
    in_specs = (
        P("exp", None),
        P(),
        P(None, "exp", None),
        P(None, "exp", None),
        P("sect", "exp", "dp", None),
        P("sect", "exp", "dp", None),
        P("sect", "exp", None),
        P("sect", "exp", None),
        P("exp", None, None),
        P("exp", None),
        P("exp", None),
        P("exp", None),
    )
    out_specs = (P("exp", "sect"), P("sect", "exp", "dp", None), P("sect", "exp", "dp", None))
    return jax.shard_map(on_device, mesh=mesh, in_specs=in_specs, out_specs=out_specs, check_vma=False)
```

```python
import functools

import jax
import jax.numpy as jnp
from jax import lax
from jax.experimental import pallas as pl
from jax.experimental.pallas import tpu as pltpu
from jax.sharding import PartitionSpec as P

step_size = 3.0
norm_eps = 1e-06
lanes = 256
note_rows = 16
f32, bf16, i32 = jnp.float32, jnp.bfloat16, jnp.int32
nt_dims = (((1,), (1,)), ((), ()))
tn_dims = (((0,), (0,)), ((), ()))
smem = pl.BlockSpec(memory_space=pltpu.SMEM)
vmem = pl.BlockSpec(memory_space=pltpu.VMEM)
anywhere = pl.BlockSpec(memory_space=pl.ANY)
stays = pl.BlockSpec(memory_space=pltpu.HBM)


def shifted(array, axis, by):
    size = lax.axis_size(axis)
    return lax.ppermute(array, axis, [(i, (i + by) % size) for i in range(size)])


def flipped(array, axis, bit):
    return lax.ppermute(array, axis, [(i, i ^ bit) for i in range(lax.axis_size(axis))])


def fits(megabytes):
    return pltpu.CompilerParams(vmem_limit_bytes=megabytes * 1024 * 1024)


def costs(flops, moved):
    return pl.CostEstimate(flops=flops, bytes_accessed=moved, transcendentals=0)


def dot(a, b, dims=(((1,), (0,)), ((), ())), precision=None):
    return lax.dot_general(a, b, dims, precision=precision, preferred_element_type=f32)


def one_hot(rows, targets_ref):
    ids = lax.broadcasted_iota(i32, (rows, targets_ref.shape[1]), 0)
    hits = [jnp.where(ids == targets_ref[k : k + 1, :], 1.0, 0.0) for k in range(targets_ref.shape[0])]
    return sum(hits[1:], hits[0]).astype(bf16)


def prepare_kernel(
    experts, capacity, part_ref, routes_ref, gates_ref, all_rows_ref, inputs_ref, grads_ref,
    targets_ref, tiled_ref, states_ref, payload_ref, own_ref, rows_ref, sems,
):
    row_count, share = rows_ref.shape
    steps, routes_each = targets_ref.shape[:2]
    stacked, width = states_ref.shape
    blocks = stacked // row_count
    own = pl.ds(pl.multiple_of(part_ref[0] * share, share), share)
    held = inputs_ref.shape[0]
    row_copy = pltpu.make_async_copy(all_rows_ref.at[:, own], rows_ref, sems.at[0])
    copies = [
        pltpu.make_async_copy(inputs_ref.at[:, own], own_ref.at[pl.ds(0, held)], sems.at[1]),
        pltpu.make_async_copy(grads_ref.at[:, own], own_ref.at[pl.ds(held, held)], sems.at[2]),
    ]
    row_copy.start()
    for copy in copies:
        copy.start()
    before = lax.broadcasted_iota(i32, (row_count, stacked), 0)
    after = lax.rem(lax.broadcasted_iota(i32, (row_count, stacked), 1), row_count)
    repeat = jnp.where(before == after, 1.0, 0.0)
    earlier = jnp.where(before < after, 1.0, 0.0).astype(bf16)
    every = jnp.ones((row_count, stacked), bf16)
    block_of = lax.div(lax.broadcasted_iota(i32, (1, stacked), 1), row_count)
    expert_ids = lax.broadcasted_iota(i32, (experts, row_count), 0)
    tall_ids = lax.broadcasted_iota(i32, (experts, stacked), 0)
    routes = dot(routes_ref[...].astype(f32), repeat, precision=lax.Precision.HIGHEST)
    routes = (routes + 0.5).astype(i32)
    tiled_ref[...] = dot(gates_ref[...], repeat, precision=lax.Precision.HIGHEST)
    for step in range(steps):
        seen = jnp.zeros((experts, stacked), f32)
        for k in range(routes_each):
            at = step * routes_each + k
            member = jnp.where(expert_ids == routes_ref[at : at + 1, :], 1.0, 0.0).astype(bf16)
            route = routes[at : at + 1, :]
            ahead = dot(member, earlier) + seen
            rank = jnp.sum(jnp.where(tall_ids == route, ahead, 0.0), axis=0, keepdims=True)
            seen = seen + dot(member, every)
            place = (route * blocks + block_of) * capacity + (rank + 0.5).astype(i32)
            targets_ref[step, k : k + 1, :] = place
    row_copy.wait()
    for block in range(blocks):
        columns = slice(block * width, (block + 1) * width)
        states_ref[block * row_count : (block + 1) * row_count, :] = rows_ref[:, columns].astype(f32)
    payload_ref[...] = dot(one_hot(payload_ref.shape[0], targets_ref.at[0]), states_ref[...].astype(bf16)).astype(bf16)
    for copy in copies:
        copy.wait()


def dispatch_kernel(step, targets_ref, states_ref, payload_ref):
    payload_ref[...] = dot(one_hot(payload_ref.shape[0], targets_ref.at[step]), states_ref[...].astype(bf16)).astype(bf16)


def combine_kernel(step, last, targets_ref, gates_ref, states_ref, returned_ref, new_ref, payload_ref):
    ids = lax.broadcasted_iota(i32, (returned_ref.shape[0], states_ref.shape[0]), 0)
    weights = jnp.zeros(ids.shape, f32)
    routes_each = targets_ref.shape[1]
    for k in range(routes_each):
        at = step * routes_each + k
        weights = weights + jnp.where(ids == targets_ref[step, k : k + 1, :], gates_ref[at : at + 1, :], 0.0)
    high = weights.astype(bf16)
    low = (weights - high.astype(f32)).astype(bf16)
    returned = returned_ref[...]
    states = states_ref[...] + (dot(high, returned, tn_dims) + dot(low, returned, tn_dims))
    new_ref[...] = states
    if last:
        payload_ref[...] = states.astype(bf16)
    else:
        payload_ref[...] = dot(one_hot(returned.shape[0], targets_ref.at[step + 1]), states.astype(bf16)).astype(bf16)


def expert_kernel(parts, slots, capacity, features, hidden, part_ref, gain_ref, *refs):
    arrived, (up_ref, down_ref) = refs[:parts], refs[parts : parts + 2]
    outs = refs[parts + 2 : 2 * parts + 2]
    up_held, down_held, normed_ref, stack_ref, order_ref, sems = refs[2 * parts + 2 :]
    width = arrived[0].shape[1]
    blocks = features // (parts * width)
    me = part_ref[0]
    up_copy = pltpu.make_async_copy(up_ref, up_held, sems.at[0])
    down_copy = pltpu.make_async_copy(down_ref, down_held, sems.at[1])
    up_copy.start()
    down_copy.start()
    moved = blocks * slots
    column = lax.broadcasted_iota(i32, (1, moved), 1)
    slot = lax.rem(column, slots)
    target = (lax.div(slot, capacity) * blocks + lax.div(column, slots)) * capacity + lax.rem(slot, capacity)
    hits = lax.broadcasted_iota(i32, (moved, moved), 0) == target
    order_ref[...] = jnp.where(hits, 1.0, 0.0).astype(bf16)
    square = jnp.zeros((slots, 1), f32)
    stacks = []
    for ref in arrived:
        stack = dot(order_ref[...], ref[...], tn_dims)
        stacks.append(stack)
        for block in range(blocks):
            rows = stack[block * slots : (block + 1) * slots]
            square = square + jnp.sum(rows * rows, axis=1, keepdims=True)
    scale = lax.rsqrt(square * (1.0 / features) + norm_eps)
    for j, stack in enumerate(stacks):
        start = lax.rem(me + parts - j, parts) * (blocks * width)
        for block in range(blocks):
            rows = stack[block * slots : (block + 1) * slots]
            columns = pl.ds(pl.multiple_of(start + block * width, width), width)
            normed_ref[:, columns] = (rows * scale * gain_ref[:, columns]).astype(bf16)
    up_copy.wait()
    before_act = dot(normed_ref[...], up_held[...], nt_dims) * features ** (-0.5)
    activated = (before_act / (1.0 + jnp.exp(-before_act))).astype(bf16)
    down_copy.wait()
    normed_ref[...] = (dot(activated, down_held[...]) * hidden ** (-0.5)).astype(bf16)
    for j, out_ref in enumerate(outs):
        start = lax.rem(me + j, parts) * (blocks * width)
        for block in range(blocks):
            columns = pl.ds(pl.multiple_of(start + block * width, width), width)
            stack_ref[block * slots : (block + 1) * slots, :] = normed_ref[:, columns]
        out_ref[...] = dot(order_ref[...], stack_ref[...]).astype(bf16)


def gathered_copies(part, parts, height, units, inputs_ref, grads_ref, sems):
    per_part = len(units) // parts
    width = units[0].shape[1]
    rows = (height - note_rows) // 2
    in_copies, grad_copies = [], []
    for j in range(parts):
        columns = pl.ds(pl.multiple_of(lax.rem(part + parts - j, parts) * width, width), width)
        blocks = [(u, at) for u in units[j * per_part : (j + 1) * per_part] for at in range(0, u.shape[0], height)]
        for i, (unit, at) in enumerate(blocks):
            place, sem = pl.ds(i * rows, rows), 2 * (j * len(blocks) + i)
            source = unit.at[pl.ds(at, rows)]
            in_copies.append(pltpu.make_async_copy(source, inputs_ref.at[place, columns], sems.at[sem]))
            source = unit.at[pl.ds(at + rows, rows)]
            grad_copies.append(pltpu.make_async_copy(source, grads_ref.at[place, columns], sems.at[sem + 1]))
    return in_copies, grad_copies


def unit_kernel(first_ref, second_ref, routes_ref, gates_ref, lengths_ref, shards_ref, unit_ref, sems):
    held = first_ref.shape[0] // 2
    copies = []
    for i, ref in enumerate((first_ref, second_ref)):
        for j in range(2):
            place = pl.ds((2 * j + i) * held, held)
            source = ref.at[pl.ds(j * held, held)]
            copies.append(pltpu.make_async_copy(source, unit_ref.at[place], sems.at[2 * i + j]))
    for copy in copies:
        copy.start()
    wide = routes_ref.shape[1]

    def widened(ref):
        count = ref.shape[1]
        places = lax.broadcasted_iota(i32, (count, wide), 0) == lax.broadcasted_iota(i32, (count, wide), 1)
        return dot(ref[...].astype(f32), jnp.where(places, 1.0, 0.0))

    gates = gates_ref[...]
    terms = []
    for _ in range(3):
        terms.append(gates.astype(bf16).astype(f32))
        gates = gates - terms[-1]
    tables = [routes_ref[...].astype(f32)] + terms + [widened(lengths_ref), widened(shards_ref)]
    ids = lax.broadcasted_iota(i32, (note_rows, wide), 0)
    notes, at = jnp.zeros((note_rows, wide), f32), 0
    for table in tables:
        for row in range(table.shape[0]):
            notes = notes + jnp.where(ids == at, table[row : row + 1, :], 0.0)
            at += 1
    base = 4 * held
    unit_ref[base:, :] = jnp.zeros((note_rows, unit_ref.shape[1]), bf16)
    unit_ref[base:, :wide] = notes.astype(bf16)
    for copy in copies:
        copy.wait()


def weights_kernel(height, halves, each, trajs, wide, sources, me_ref, *refs):
    units, (weights_ref, notes_ref, table_ref, facts_ref, sems) = refs[:-5], refs[-5:]
    blocks = [(u, at) for u in units for at in range(0, u.shape[0], height)]
    count = len(blocks)
    per_half = (height - note_rows) // (2 * halves)
    longest = wide // count
    total = weights_ref.shape[1]
    copies = []
    for i, (unit, at) in enumerate(blocks):
        source = unit.at[pl.ds(at + height - note_rows, note_rows), pl.ds(0, wide)]
        copies.append(pltpu.make_async_copy(source, notes_ref.at[i], sems.at[i]))
    for copy in copies:
        copy.start()
    for copy in copies:
        copy.wait()
    me = me_ref[0]
    ids = lax.broadcasted_iota(i32, (count, 1), 0)
    places = lax.broadcasted_iota(i32, (note_rows, wide), 1)
    holder_of = jnp.zeros((count, 1), f32)
    for i, (group, flip, far, near) in enumerate(sources):
        place = lax.rem((lax.rem(me, group) ^ flip) + group - far, group)
        holder = ((lax.div(me, group) * group + place) ^ near).astype(f32)
        holder_of = holder_of + jnp.where(ids == i, holder, 0.0)
        notes = notes_ref[i].astype(f32)
        row = jnp.zeros((1, wide), f32)
        for k in range(each):
            gate = sum(notes[(1 + t) * each + k : (1 + t) * each + k + 1, :] for t in range(3))
            row = row + jnp.where(notes[k : k + 1, :] == me.astype(f32), gate, 0.0)
        table_ref[i : i + 1, :] = row
        for half in range(halves):
            shards = pltpu.roll(notes, (trajs - half * trajs) % wide, 1) if half != 1 else notes
            shards = jnp.where((places >= trajs) & (places < 2 * trajs), shards, 0.0)
            shards = jnp.where(places == 2 * trajs, holder, shards)
            facts = notes[4 * each + half : 4 * each + half + 1, :] + shards[4 * each + halves : 4 * each + halves + 1, :]
            facts_ref[i * halves + half : i * halves + half + 1, :] = facts
    facts = facts_ref[...]
    down, across = [lax.broadcasted_iota(i32, (wide, wide), d) for d in (0, 1)]
    starts = dot(facts, jnp.where((down < across) & (down < trajs), 1.0, 0.0))
    row_ids = lax.broadcasted_iota(i32, (count * halves, total), 1)
    of_row = lax.div(row_ids, per_half) == lax.broadcasted_iota(i32, (count * halves, total), 0)
    of_row = jnp.where(of_row, 1.0, 0.0)
    facts, starts = dot(facts, of_row, tn_dims), dot(starts, of_row, tn_dims)[:trajs]
    place = lax.rem(lax.broadcasted_iota(i32, (1, total), 1), per_half).astype(f32)
    inside = (place >= starts) & (place < starts + facts[:trajs])
    offset = jnp.sum(jnp.where(inside, place - starts, 0.0), axis=0, keepdims=True)
    shard = jnp.sum(jnp.where(inside, facts[trajs : 2 * trajs], 0.0), axis=0, keepdims=True)
    slot = (facts[2 * trajs : 2 * trajs + 1] * longest + offset + 0.5).astype(i32)
    chosen = jnp.where(lax.broadcasted_iota(i32, (wide, total), 0) == slot, 1.0, 0.0)
    gates = dot(table_ref[...], chosen, precision=lax.Precision.HIGHEST)
    weights_ref[...] = jnp.sum(jnp.where(holder_of == shard, gates, 0.0), axis=0, keepdims=True)


def tile_copies(ref, held, tile, sems):
    places = [pl.ds(start, tile) for start in range(0, ref.shape[0], tile)]
    return [pltpu.make_async_copy(ref.at[p], held.at[p], sems.at[i]) for i, p in enumerate(places)]


def start_all(*groups):
    for copies in groups:
        for copy in copies:
            copy.start()


def wait_all(copies):
    for copy in copies:
        copy.wait()


def activation(features, up_tile, inputs, weight):
    before_act = dot(up_tile, inputs, nt_dims) * features ** (-0.5)
    sigmoid = 1.0 / (1.0 + jnp.exp(-before_act))
    return (before_act * sigmoid * weight).astype(bf16), sigmoid * (1.0 + before_act * (1.0 - sigmoid)) * weight


def new_tile(old, step, change, rows):
    return (old.astype(f32) - (step_size * step) * dot(change, rows)).astype(bf16)


def cut_kernel(go_ref, up_ref, down_ref, first_ref, second_ref, held, sems):
    rows, most = up_ref.shape[0], first_ref.shape[0]

    @pl.when(go_ref[0] == 0)
    def _():
        moves = [
            (up_ref, pl.ds(0, rows), first_ref.at[pl.ds(0, rows)]),
            (down_ref.at[pl.ds(0, most - rows)], pl.ds(rows, most - rows), first_ref.at[pl.ds(rows, most - rows)]),
            (down_ref.at[pl.ds(most - rows, 2 * rows - most)], pl.ds(most, 2 * rows - most), second_ref),
        ]
        ins = [pltpu.make_async_copy(a, held.at[p], sems.at[0, i]) for i, (a, p, _) in enumerate(moves)]
        outs = [pltpu.make_async_copy(held.at[p], b, sems.at[1, i]) for i, (_, p, b) in enumerate(moves)]
        start_all(ins)
        for copy, out in zip(ins, outs):
            copy.wait()
            out.start()
        wait_all(outs)


def update_rows(features, hidden, tile, weight, in_copies, grad_copies, up_from, down_from, up_to, down_to, space):
    inputs, grads, up, down, new_up, new_down, sems, out_sems = space
    up_copies = tile_copies(up_from, up, tile, sems.at[0])
    down_copies = tile_copies(down_from, down, tile, sems.at[1])
    up_outs = tile_copies(new_up, up_to, tile, out_sems.at[0])
    down_outs = tile_copies(new_down, down_to, tile, out_sems.at[1])
    start_all(up_copies[:1], in_copies, down_copies[:1], grad_copies, up_copies[1:], down_copies[1:])
    for i in range(len(up_copies)):
        here = pl.ds(i * tile, tile)
        up_copies[i].wait()
        if i == 0:
            wait_all(in_copies)
        activated, slope = activation(features, up[here, :], inputs[...], weight)
        down_copies[i].wait()
        if i == 0:
            wait_all(grad_copies)
        pre_grad = (dot(down[here, :], grads[...], nt_dims) * hidden ** (-0.5) * slope).astype(bf16)
        new_down[here, :] = new_tile(down[here, :], hidden ** (-0.5), activated, grads[...])
        down_outs[i].start()
        new_up[here, :] = new_tile(up[here, :], features ** (-0.5), pre_grad, inputs[...])
        up_outs[i].start()
    wait_all(up_outs + down_outs)


def learner_kernel(parts, height, features, hidden, tile, part_ref, weight_ref, *refs):
    units, (up_ref, down_ref, new_up_ref, new_down_ref), row_sems, space = refs[:-13], refs[-13:-9], refs[-9], refs[-8:]
    copies = gathered_copies(part_ref[0], parts, height, units, space[0], space[1], row_sems)
    rows = (up_ref, down_ref, new_up_ref, new_down_ref)
    update_rows(features, hidden, tile, weight_ref[...], *copies, *rows, space)


def assemble_kernel(parts, height, part_ref, *refs):
    units, (inputs_ref, grads_ref, sems) = refs[:-3], refs[-3:]
    in_copies, grad_copies = gathered_copies(part_ref[0], parts, height, units, inputs_ref, grads_ref, sems)
    start_all(in_copies, grad_copies)
    wait_all(in_copies + grad_copies)


def late_kernel(features, hidden, tile, places, go_ref, weight_ref, *refs):
    inputs_ref, grads_ref, up_ref, down_ref, _, _, new_up_ref, new_down_ref, row_sems, *space = refs
    count, to, up_at, down_at = places

    @pl.when(go_ref[0] == 1)
    def _():
        in_copies = [pltpu.make_async_copy(inputs_ref, space[0], row_sems.at[0])]
        grad_copies = [pltpu.make_async_copy(grads_ref, space[1], row_sems.at[1])]
        rows = [up_ref.at[pl.ds(up_at, count)], down_ref.at[pl.ds(down_at, count)]]
        rows = rows + [ref.at[pl.ds(to, count)] for ref in (new_up_ref, new_down_ref)]
        update_rows(features, hidden, tile, weight_ref[...], in_copies, grad_copies, *rows, space)


def hold_kernel(go_ref, array_ref, held_ref, sem):
    @pl.when(go_ref[0] == 0)
    def _():
        copy = pltpu.make_async_copy(array_ref, held_ref, sem)
        copy.start()
        copy.wait()


def join_kernel(parts, row_count, part_ref, *refs):
    pieces, (left_ref, right_ref, joined_ref) = refs[:parts], refs[parts:]
    width = pieces[0].shape[1]
    blocks = pieces[0].shape[0] // row_count
    for j, piece in enumerate(pieces):
        start = lax.rem(part_ref[0] + parts - j, parts) * (blocks * width)
        for block in range(blocks):
            columns = pl.ds(pl.multiple_of(start + block * width, width), width)
            joined_ref[:, columns] = piece[block * row_count : (block + 1) * row_count, :]
    half = left_ref.shape[1]
    left_ref[...] = joined_ref[:, :half]
    right_ref[...] = joined_ref[:, half:]


def unset_kernel(*refs):
    pass


def unset(*like):
    arrays = pl.pallas_call(
        unset_kernel,
        out_shape=[jax.ShapeDtypeStruct(a.shape, a.dtype) for a in like],
        out_specs=[anywhere] * len(like),
        cost_estimate=costs(1, 1),
    )()
    return tuple(arrays)


def on_device(
    decode_states,
    norm_gain,
    decode_routes,
    decode_gates,
    up_weight,
    down_weight,
    traj_inputs,
    traj_cotangents,
    traj_lengths,
    packing,
    learner_routes,
    learner_gates,
):
    experts, parts = lax.axis_size("exp"), lax.axis_size("dp")
    is_rollout = lax.axis_index("sect") == 0
    go = is_rollout.astype(i32).reshape(1)
    me = lax.axis_index("exp")
    part_ref = lax.axis_index("dp").reshape(1).astype(i32)
    up_here, down_here = up_weight[0, 0], down_weight[0, 0]
    hidden_here, features = up_here.shape
    hidden = hidden_here * parts
    steps, row_count, routes_each = decode_routes.shape
    half_steps = steps // 2
    share = features // parts
    blocks = share // lanes
    capacity = 3 * row_count * routes_each // (2 * experts)
    slots = experts * capacity
    stacked = blocks * row_count
    moved = blocks * slots
    tile = hidden_here // 3
    line = 8
    per_half = traj_inputs.shape[1]
    gathered = experts * 2 * per_half
    height = 4 * per_half + note_rows

    routes = jnp.swapaxes(decode_routes, 1, 2).reshape(steps * routes_each, row_count)
    gates = jnp.swapaxes(decode_gates, 1, 2).reshape(steps * routes_each, row_count)
    targets, gates, states, payload, own_rows = pl.pallas_call(
        functools.partial(prepare_kernel, experts, capacity),
        out_shape=[
            jax.ShapeDtypeStruct((steps, routes_each, stacked), i32),
            jax.ShapeDtypeStruct((steps * routes_each, stacked), f32),
            jax.ShapeDtypeStruct((stacked, lanes), f32),
            jax.ShapeDtypeStruct((moved, lanes), bf16),
            jax.ShapeDtypeStruct((2 * per_half, share), bf16),
        ],
        in_specs=[smem, vmem, vmem] + [stays] * 3,
        scratch_shapes=[pltpu.VMEM((row_count, share), bf16), pltpu.SemaphoreType.DMA((3,))],
        compiler_params=fits(60),
        cost_estimate=costs(1, 1),
    )(part_ref, routes, gates, decode_states, traj_inputs[0], traj_cotangents[0])

    crossed_rows = flipped(own_rows, "sect", 1)
    up_sent, down_sent, _ = lax.optimization_barrier((up_here, down_here, own_rows))
    cut = hidden_here + 2 * tile
    pieces = pl.pallas_call(
        cut_kernel,
        out_shape=[jax.ShapeDtypeStruct((rows, features), bf16) for rows in (cut, tile)],
        in_specs=[smem] + [stays] * 2,
        out_specs=[stays] * 2,
        scratch_shapes=[pltpu.VMEM((2 * hidden_here, features), bf16), pltpu.SemaphoreType.DMA((2, 3))],
        compiler_params=fits(60),
        cost_estimate=costs(1, 1),
    )(go, up_sent, down_sent)
    first_piece, second_piece, crossed_rows = lax.optimization_barrier((*pieces, crossed_rows))
    first_there = lax.ppermute(first_piece, "sect", [(1, 0)])
    second_there = lax.ppermute(second_piece, "sect", [(1, 0)])

    gain = norm_gain.reshape(1, features)
    def expert_forward(arrived, up_mat, down_mat):
        return pl.pallas_call(
            functools.partial(expert_kernel, parts, slots, capacity, features, hidden),
            out_shape=[jax.ShapeDtypeStruct((moved, lanes), bf16)] * parts,
            in_specs=[smem, vmem] + [vmem] * parts + [stays, stays],
            scratch_shapes=[
                pltpu.VMEM((hidden_here, features), bf16),
                pltpu.VMEM((hidden_here, features), bf16),
                pltpu.VMEM((slots, features), bf16),
                pltpu.VMEM((moved, lanes), bf16),
                pltpu.VMEM((moved, moved), bf16),
                pltpu.SemaphoreType.DMA((2,)),
            ],
            compiler_params=fits(48),
            cost_estimate=costs(1, 1),
        )(part_ref, gain, *arrived, up_mat, down_mat)

    def decode_step(step, states, payload, up_mat, down_mat):
        last = step in (half_steps - 1, steps - 1)
        arrived = lax.all_to_all(payload, "exp", split_axis=0, concat_axis=0, tiled=True)
        arrived = [arrived] + [shifted(arrived, "dp", j) for j in range(1, parts)]
        partials = expert_forward(arrived, up_mat, down_mat)
        received = [shifted(partials[j], "dp", j) for j in range(1, parts)]
        summed = sum((r.astype(f32) for r in received), partials[0].astype(f32)).astype(bf16)
        returned = lax.all_to_all(summed, "exp", split_axis=0, concat_axis=0, tiled=True)
        outs = [
            jax.ShapeDtypeStruct((stacked, lanes), f32),
            jax.ShapeDtypeStruct((stacked if last else moved, lanes), bf16),
        ]
        results = pl.pallas_call(
            functools.partial(combine_kernel, step, last),
            out_shape=outs,
            compiler_params=fits(16),
            cost_estimate=costs(1, 1),
        )(targets, gates, states, returned)
        return tuple(results)
    def learner_rows(halves):
        wide = learner_routes.shape[0]
        notes = [learner_routes.T, learner_gates.T, traj_lengths[0], packing]
        unit = pl.pallas_call(
            unit_kernel,
            out_shape=jax.ShapeDtypeStruct((height, share), bf16),
            in_specs=[anywhere] * 2 + [vmem] * 4,
            scratch_shapes=[pltpu.SemaphoreType.DMA((4,))],
            compiler_params=fits(16),
            cost_estimate=costs(1, 1),
        )(*halves, *notes)
        others, group = [0], experts
        while group > line:
            group = group // 2
            unit = jnp.concatenate([unit, flipped(unit, "exp", group)])
            others = others + [o ^ group for o in others]
        far = group // 2
        shifts = sorted(range(1, far), key=lambda s: (min(s, far - s), s))

        def along(array, s):
            pairs = [(i, i // group * group + (i + 2 * s) % group) for i in range(experts)]
            return lax.ppermute(array, "exp", pairs)

        side = flipped(unit, "exp", 1)
        near = [along(unit, s) for s in shifts[:-1]]
        unit, side, *near = lax.optimization_barrier((unit, side, *near))
        last = along(unit, shifts[-1])
        sides = [flipped(n, "exp", 1) for n in near]
        units = [
            jnp.concatenate([unit, side, *near]),
            jnp.concatenate(sides),
            jnp.concatenate([last, flipped(last, "exp", 1)]),
        ]
        places = [(0, 0), (1, 0)] + [(f, s) for f in range(2) for s in shifts[:-1]] + [(f, shifts[-1]) for f in range(2)]
        sources = [(group, flip, 2 * s, o) for flip, s in places for o in others]
        return units, sources

    def with_parts(units, sources):
        units = list(units)
        others = [shifted(u, "dp", j) for j in range(1, parts) for u in units]
        wide = learner_routes.shape[0]
        weights = pl.pallas_call(
            functools.partial(
                weights_kernel, height, 2, learner_routes.shape[1], traj_lengths.shape[2], wide, sources
            ),
            out_shape=jax.ShapeDtypeStruct((1, gathered), f32),
            in_specs=[smem] + [anywhere] * len(units),
            scratch_shapes=[
                pltpu.VMEM((experts, note_rows, wide), bf16),
                pltpu.VMEM((experts, wide), f32),
                pltpu.VMEM((2 * experts, wide), f32),
                pltpu.SemaphoreType.DMA((experts,)),
            ],
            compiler_params=fits(16),
            cost_estimate=costs(1, 1),
        )(me.reshape(1).astype(i32), *units)
        return units + others, weights

    rows_like = jax.ShapeDtypeStruct((gathered, features), bf16)
    weight_like = jax.ShapeDtypeStruct((hidden_here, features), bf16)
    weights_like = jax.ShapeDtypeStruct((1, gathered), f32)

    def sems_of(*shape):
        return pltpu.SemaphoreType.DMA(shape)

    def update_space(rows):
        held = [pltpu.VMEM((gathered, features), bf16)] * 2 + [pltpu.VMEM((rows, features), bf16)] * 4
        return held + [sems_of(2, rows // tile)] * 2

    def update(units, weights, up_mat, down_mat):
        return pl.pallas_call(
            functools.partial(learner_kernel, parts, height, features, hidden, tile),
            out_shape=[weight_like] * 2,
            in_specs=[smem, vmem] + [anywhere] * (len(units) + 2),
            out_specs=[anywhere] * 2,
            scratch_shapes=[sems_of(2 * parts * experts)] + update_space(hidden_here),
            compiler_params=fits(56),
            cost_estimate=costs(1, 1),
        )(part_ref, weights, *units, up_mat, down_mat)

    def update_late(count, places, piece, new_up, new_down):
        return pl.pallas_call(
            functools.partial(late_kernel, features, hidden, tile, (count, *places)),
            out_shape=[weight_like] * 2,
            in_specs=[smem, vmem] + [stays] * 6,
            out_specs=[anywhere] * 2,
            scratch_shapes=[sems_of(2)] + update_space(count),
            input_output_aliases={6: 0, 7: 1},
            compiler_params=fits(60),
            cost_estimate=costs(1, 1),
        )(go, weights, inputs, grads, first_there, piece, new_up, new_down)

    final_like = jax.ShapeDtypeStruct((stacked, lanes), bf16)
    block_rows = height * max(1, experts // line)
    gather_like = [jax.ShapeDtypeStruct((block_rows * n, share), bf16) for n in (line // 2, line // 2 - 2, 2)]

    sources = []

    def first_rollout():
        return decode_step(0, states, payload, up_here, down_here) + unset(*gather_like)

    def first_learner():
        units, places = learner_rows([crossed_rows, own_rows])
        sources.append(places)
        return (states, payload) + tuple(units)

    states, payload, *rows = lax.cond(is_rollout, first_rollout, first_learner)

    def second_rollout():
        now, sent = states, payload
        for step in range(1, half_steps):
            now, sent = decode_step(step, now, sent, up_here, down_here)
        return (now,) + tuple(unset(up_here, down_here))

    def second_learner():
        units, weights = with_parts(rows, sources[0])
        return (states,) + tuple(update(units, weights, up_here, down_here))

    states, new_up, new_down = lax.cond(is_rollout, second_rollout, second_learner)
    states_there = lax.ppermute(states, "sect", [(0, 1)])

    held_up = pl.pallas_call(
        hold_kernel,
        out_shape=weight_like,
        in_specs=[smem, stays],
        out_specs=vmem,
        scratch_shapes=[pltpu.SemaphoreType.DMA],
        compiler_params=fits(16),
        cost_estimate=costs(1, 1),
    )(go, new_up)

    def third_rollout():
        return (states, payload) + tuple(learner_rows([own_rows, crossed_rows])[0])

    def third_learner():
        sent = pl.pallas_call(
            functools.partial(dispatch_kernel, half_steps),
            out_shape=jax.ShapeDtypeStruct((moved, lanes), bf16),
            compiler_params=fits(16),
            cost_estimate=costs(1, 1),
        )(targets, states_there)
        return decode_step(half_steps, states_there, sent, held_up, new_down) + unset(*gather_like)

    states, payload, *rows = lax.cond(is_rollout, third_rollout, third_learner)

    def fourth_rollout():
        units, weights = with_parts(rows, sources[0])
        whole = pl.pallas_call(
            functools.partial(assemble_kernel, parts, height),
            out_shape=[rows_like] * 2,
            in_specs=[smem] + [anywhere] * len(units),
            scratch_shapes=[sems_of(2 * parts * experts)],
            compiler_params=fits(32),
            cost_estimate=costs(1, 1),
        )(part_ref, *units)
        return unset(final_like) + tuple(whole) + (weights,)

    def fourth_learner():
        now, sent = states, payload
        for step in range(half_steps + 1, steps):
            now, sent = decode_step(step, now, sent, held_up, new_down)
        return (sent,) + unset(rows_like, rows_like, weights_like)

    mine, inputs, grads, weights = lax.cond(is_rollout, fourth_rollout, fourth_learner)

    pieces = [mine] + [shifted(mine, "dp", j) for j in range(1, parts)]
    left, right = pl.pallas_call(
        functools.partial(join_kernel, parts, row_count),
        out_shape=[jax.ShapeDtypeStruct((row_count, features // 2), bf16)] * 2,
        in_specs=[smem] + [vmem] * parts,
        scratch_shapes=[pltpu.VMEM((row_count, features), bf16)],
        cost_estimate=costs(1, 1),
    )(part_ref, *pieces)
    new_up, new_down = update_late(2 * tile, (0, 0, hidden_here), first_there, new_up, new_down)
    delivered = lax.ppermute(left, "sect", [(1, 0)])
    new_up, new_down = update_late(tile, (2 * tile, 2 * tile, 0), second_there, new_up, new_down)
    right, new_up = lax.optimization_barrier((right, new_up))
    final_states = jnp.where(is_rollout, delivered, right)
    return final_states, new_up[None, None], new_down[None, None]


def solution(mesh):
    in_specs = (
        P("exp", None),
        P(),
        P(None, "exp", None),
        P(None, "exp", None),
        P("sect", "exp", "dp", None),
        P("sect", "exp", "dp", None),
        P("sect", "exp", None),
        P("sect", "exp", None),
        P("exp", None, None),
        P("exp", None),
        P("exp", None),
        P("exp", None),
    )
    out_specs = (P("exp", "sect"), P("sect", "exp", "dp", None), P("sect", "exp", "dp", None))
    return jax.shard_map(on_device, mesh=mesh, in_specs=in_specs, out_specs=out_specs, check_vma=False)
```

```python
import functools

import jax
import jax.numpy as jnp
from jax import lax
from jax.experimental import pallas as pl
from jax.experimental.pallas import tpu as pltpu
from jax.sharding import PartitionSpec as P

step_size = 3.0
norm_eps = 1e-06
lanes = 256
note_rows = 16
f32, bf16, i32 = jnp.float32, jnp.bfloat16, jnp.int32
nt_dims = (((1,), (1,)), ((), ()))
tn_dims = (((0,), (0,)), ((), ()))
smem = pl.BlockSpec(memory_space=pltpu.SMEM)
vmem = pl.BlockSpec(memory_space=pltpu.VMEM)
anywhere = pl.BlockSpec(memory_space=pl.ANY)
stays = pl.BlockSpec(memory_space=pltpu.HBM)


def shifted(array, axis, by):
    size = lax.axis_size(axis)
    return lax.ppermute(array, axis, [(i, (i + by) % size) for i in range(size)])


def flipped(array, axis, bit):
    return lax.ppermute(array, axis, [(i, i ^ bit) for i in range(lax.axis_size(axis))])


def fits(megabytes):
    return pltpu.CompilerParams(vmem_limit_bytes=megabytes * 1024 * 1024)


def costs(flops, moved):
    return pl.CostEstimate(flops=flops, bytes_accessed=moved, transcendentals=0)


def dot(a, b, dims=(((1,), (0,)), ((), ())), precision=None):
    return lax.dot_general(a, b, dims, precision=precision, preferred_element_type=f32)


def one_hot(rows, targets_ref):
    ids = lax.broadcasted_iota(i32, (rows, targets_ref.shape[1]), 0)
    hits = [jnp.where(ids == targets_ref[k : k + 1, :], 1.0, 0.0) for k in range(targets_ref.shape[0])]
    return sum(hits[1:], hits[0]).astype(bf16)


def prepare_kernel(
    experts, capacity, part_ref, routes_ref, gates_ref, all_rows_ref, inputs_ref, grads_ref,
    targets_ref, tiled_ref, states_ref, payload_ref, own_ref, rows_ref, sems,
):
    row_count, share = rows_ref.shape
    steps, routes_each = targets_ref.shape[:2]
    stacked, width = states_ref.shape
    blocks = stacked // row_count
    own = pl.ds(pl.multiple_of(part_ref[0] * share, share), share)
    held = inputs_ref.shape[0]
    row_copy = pltpu.make_async_copy(all_rows_ref.at[:, own], rows_ref, sems.at[0])
    copies = [
        pltpu.make_async_copy(inputs_ref.at[:, own], own_ref.at[pl.ds(0, held)], sems.at[1]),
        pltpu.make_async_copy(grads_ref.at[:, own], own_ref.at[pl.ds(held, held)], sems.at[2]),
    ]
    row_copy.start()
    for copy in copies:
        copy.start()
    before = lax.broadcasted_iota(i32, (row_count, stacked), 0)
    after = lax.rem(lax.broadcasted_iota(i32, (row_count, stacked), 1), row_count)
    repeat = jnp.where(before == after, 1.0, 0.0)
    earlier = jnp.where(before < after, 1.0, 0.0).astype(bf16)
    every = jnp.ones((row_count, stacked), bf16)
    block_of = lax.div(lax.broadcasted_iota(i32, (1, stacked), 1), row_count)
    expert_ids = lax.broadcasted_iota(i32, (experts, row_count), 0)
    tall_ids = lax.broadcasted_iota(i32, (experts, stacked), 0)
    routes = dot(routes_ref[...].astype(f32), repeat, precision=lax.Precision.HIGHEST)
    routes = (routes + 0.5).astype(i32)
    tiled_ref[...] = dot(gates_ref[...], repeat, precision=lax.Precision.HIGHEST)
    for step in range(steps):
        seen = jnp.zeros((experts, stacked), f32)
        for k in range(routes_each):
            at = step * routes_each + k
            member = jnp.where(expert_ids == routes_ref[at : at + 1, :], 1.0, 0.0).astype(bf16)
            route = routes[at : at + 1, :]
            ahead = dot(member, earlier) + seen
            rank = jnp.sum(jnp.where(tall_ids == route, ahead, 0.0), axis=0, keepdims=True)
            seen = seen + dot(member, every)
            place = (route * blocks + block_of) * capacity + (rank + 0.5).astype(i32)
            targets_ref[step, k : k + 1, :] = place
    row_copy.wait()
    for block in range(blocks):
        columns = slice(block * width, (block + 1) * width)
        states_ref[block * row_count : (block + 1) * row_count, :] = rows_ref[:, columns].astype(f32)
    payload_ref[...] = dot(one_hot(payload_ref.shape[0], targets_ref.at[0]), states_ref[...].astype(bf16)).astype(bf16)
    for copy in copies:
        copy.wait()


def dispatch_kernel(step, targets_ref, states_ref, payload_ref):
    payload_ref[...] = dot(one_hot(payload_ref.shape[0], targets_ref.at[step]), states_ref[...].astype(bf16)).astype(bf16)


def combine_kernel(step, last, targets_ref, gates_ref, states_ref, returned_ref, new_ref, payload_ref):
    ids = lax.broadcasted_iota(i32, (returned_ref.shape[0], states_ref.shape[0]), 0)
    weights = jnp.zeros(ids.shape, f32)
    routes_each = targets_ref.shape[1]
    for k in range(routes_each):
        at = step * routes_each + k
        weights = weights + jnp.where(ids == targets_ref[step, k : k + 1, :], gates_ref[at : at + 1, :], 0.0)
    high = weights.astype(bf16)
    low = (weights - high.astype(f32)).astype(bf16)
    returned = returned_ref[...]
    states = states_ref[...] + (dot(high, returned, tn_dims) + dot(low, returned, tn_dims))
    new_ref[...] = states
    if last:
        payload_ref[...] = states.astype(bf16)
    else:
        payload_ref[...] = dot(one_hot(returned.shape[0], targets_ref.at[step + 1]), states.astype(bf16)).astype(bf16)


def expert_kernel(parts, slots, capacity, features, hidden, part_ref, gain_ref, *refs):
    arrived, (up_ref, down_ref) = refs[:parts], refs[parts : parts + 2]
    outs = refs[parts + 2 : 2 * parts + 2]
    up_held, down_held, normed_ref, stack_ref, order_ref, sems = refs[2 * parts + 2 :]
    width = arrived[0].shape[1]
    blocks = features // (parts * width)
    me = part_ref[0]
    up_copy = pltpu.make_async_copy(up_ref, up_held, sems.at[0])
    down_copy = pltpu.make_async_copy(down_ref, down_held, sems.at[1])
    up_copy.start()
    down_copy.start()
    moved = blocks * slots
    column = lax.broadcasted_iota(i32, (1, moved), 1)
    slot = lax.rem(column, slots)
    target = (lax.div(slot, capacity) * blocks + lax.div(column, slots)) * capacity + lax.rem(slot, capacity)
    hits = lax.broadcasted_iota(i32, (moved, moved), 0) == target
    order_ref[...] = jnp.where(hits, 1.0, 0.0).astype(bf16)
    square = jnp.zeros((slots, 1), f32)
    stacks = []
    for ref in arrived:
        stack = dot(order_ref[...], ref[...], tn_dims)
        stacks.append(stack)
        for block in range(blocks):
            rows = stack[block * slots : (block + 1) * slots]
            square = square + jnp.sum(rows * rows, axis=1, keepdims=True)
    scale = lax.rsqrt(square * (1.0 / features) + norm_eps)
    for j, stack in enumerate(stacks):
        start = lax.rem(me + parts - j, parts) * (blocks * width)
        for block in range(blocks):
            rows = stack[block * slots : (block + 1) * slots]
            columns = pl.ds(pl.multiple_of(start + block * width, width), width)
            normed_ref[:, columns] = (rows * scale * gain_ref[:, columns]).astype(bf16)
    up_copy.wait()
    before_act = dot(normed_ref[...], up_held[...], nt_dims) * features ** (-0.5)
    activated = (before_act / (1.0 + jnp.exp(-before_act))).astype(bf16)
    down_copy.wait()
    normed_ref[...] = (dot(activated, down_held[...]) * hidden ** (-0.5)).astype(bf16)
    for j, out_ref in enumerate(outs):
        start = lax.rem(me + j, parts) * (blocks * width)
        for block in range(blocks):
            columns = pl.ds(pl.multiple_of(start + block * width, width), width)
            stack_ref[block * slots : (block + 1) * slots, :] = normed_ref[:, columns]
        out_ref[...] = dot(order_ref[...], stack_ref[...]).astype(bf16)


def gathered_copies(part, parts, height, units, inputs_ref, grads_ref, sems):
    per_part = len(units) // parts
    width = units[0].shape[1]
    rows = (height - note_rows) // 2
    in_copies, grad_copies = [], []
    for j in range(parts):
        columns = pl.ds(pl.multiple_of(lax.rem(part + parts - j, parts) * width, width), width)
        blocks = [(u, at) for u in units[j * per_part : (j + 1) * per_part] for at in range(0, u.shape[0], height)]
        for i, (unit, at) in enumerate(blocks):
            place, sem = pl.ds(i * rows, rows), 2 * (j * len(blocks) + i)
            source = unit.at[pl.ds(at, rows)]
            in_copies.append(pltpu.make_async_copy(source, inputs_ref.at[place, columns], sems.at[sem]))
            source = unit.at[pl.ds(at + rows, rows)]
            grad_copies.append(pltpu.make_async_copy(source, grads_ref.at[place, columns], sems.at[sem + 1]))
    return in_copies, grad_copies


def unit_kernel(first_ref, second_ref, routes_ref, gates_ref, lengths_ref, shards_ref, unit_ref, sems):
    held = first_ref.shape[0] // 2
    copies = []
    for i, ref in enumerate((first_ref, second_ref)):
        for j in range(2):
            place = pl.ds((2 * j + i) * held, held)
            source = ref.at[pl.ds(j * held, held)]
            copies.append(pltpu.make_async_copy(source, unit_ref.at[place], sems.at[2 * i + j]))
    for copy in copies:
        copy.start()
    wide = routes_ref.shape[1]

    def widened(ref):
        count = ref.shape[1]
        places = lax.broadcasted_iota(i32, (count, wide), 0) == lax.broadcasted_iota(i32, (count, wide), 1)
        return dot(ref[...].astype(f32), jnp.where(places, 1.0, 0.0))

    gates = gates_ref[...]
    terms = []
    for _ in range(3):
        terms.append(gates.astype(bf16).astype(f32))
        gates = gates - terms[-1]
    tables = [routes_ref[...].astype(f32)] + terms + [widened(lengths_ref), widened(shards_ref)]
    ids = lax.broadcasted_iota(i32, (note_rows, wide), 0)
    notes, at = jnp.zeros((note_rows, wide), f32), 0
    for table in tables:
        for row in range(table.shape[0]):
            notes = notes + jnp.where(ids == at, table[row : row + 1, :], 0.0)
            at += 1
    base = 4 * held
    unit_ref[base:, :] = jnp.zeros((note_rows, unit_ref.shape[1]), bf16)
    unit_ref[base:, :wide] = notes.astype(bf16)
    for copy in copies:
        copy.wait()


def weights_kernel(height, halves, each, trajs, wide, sources, me_ref, *refs):
    units, (weights_ref, notes_ref, table_ref, facts_ref, sems) = refs[:-5], refs[-5:]
    blocks = [(u, at) for u in units for at in range(0, u.shape[0], height)]
    count = len(blocks)
    per_half = (height - note_rows) // (2 * halves)
    longest = wide // count
    total = weights_ref.shape[1]
    copies = []
    for i, (unit, at) in enumerate(blocks):
        source = unit.at[pl.ds(at + height - note_rows, note_rows), pl.ds(0, wide)]
        copies.append(pltpu.make_async_copy(source, notes_ref.at[i], sems.at[i]))
    for copy in copies:
        copy.start()
    for copy in copies:
        copy.wait()
    me = me_ref[0]
    ids = lax.broadcasted_iota(i32, (count, 1), 0)
    places = lax.broadcasted_iota(i32, (note_rows, wide), 1)
    holder_of = jnp.zeros((count, 1), f32)
    for i, (group, flip, far, near) in enumerate(sources):
        place = lax.rem((lax.rem(me, group) ^ flip) + group - far, group)
        holder = ((lax.div(me, group) * group + place) ^ near).astype(f32)
        holder_of = holder_of + jnp.where(ids == i, holder, 0.0)
        notes = notes_ref[i].astype(f32)
        row = jnp.zeros((1, wide), f32)
        for k in range(each):
            gate = sum(notes[(1 + t) * each + k : (1 + t) * each + k + 1, :] for t in range(3))
            row = row + jnp.where(notes[k : k + 1, :] == me.astype(f32), gate, 0.0)
        table_ref[i : i + 1, :] = row
        for half in range(halves):
            shards = pltpu.roll(notes, (trajs - half * trajs) % wide, 1) if half != 1 else notes
            shards = jnp.where((places >= trajs) & (places < 2 * trajs), shards, 0.0)
            shards = jnp.where(places == 2 * trajs, holder, shards)
            facts = notes[4 * each + half : 4 * each + half + 1, :] + shards[4 * each + halves : 4 * each + halves + 1, :]
            facts_ref[i * halves + half : i * halves + half + 1, :] = facts
    facts = facts_ref[...]
    down, across = [lax.broadcasted_iota(i32, (wide, wide), d) for d in (0, 1)]
    starts = dot(facts, jnp.where((down < across) & (down < trajs), 1.0, 0.0))
    row_ids = lax.broadcasted_iota(i32, (count * halves, total), 1)
    of_row = lax.div(row_ids, per_half) == lax.broadcasted_iota(i32, (count * halves, total), 0)
    of_row = jnp.where(of_row, 1.0, 0.0)
    facts, starts = dot(facts, of_row, tn_dims), dot(starts, of_row, tn_dims)[:trajs]
    place = lax.rem(lax.broadcasted_iota(i32, (1, total), 1), per_half).astype(f32)
    inside = (place >= starts) & (place < starts + facts[:trajs])
    offset = jnp.sum(jnp.where(inside, place - starts, 0.0), axis=0, keepdims=True)
    shard = jnp.sum(jnp.where(inside, facts[trajs : 2 * trajs], 0.0), axis=0, keepdims=True)
    slot = (facts[2 * trajs : 2 * trajs + 1] * longest + offset + 0.5).astype(i32)
    chosen = jnp.where(lax.broadcasted_iota(i32, (wide, total), 0) == slot, 1.0, 0.0)
    gates = dot(table_ref[...], chosen, precision=lax.Precision.HIGHEST)
    weights_ref[...] = jnp.sum(jnp.where(holder_of == shard, gates, 0.0), axis=0, keepdims=True)


def tile_copies(ref, held, tile, sems):
    places = [pl.ds(start, tile) for start in range(0, ref.shape[0], tile)]
    return [pltpu.make_async_copy(ref.at[p], held.at[p], sems.at[i]) for i, p in enumerate(places)]


def start_all(*groups):
    for copies in groups:
        for copy in copies:
            copy.start()


def wait_all(copies):
    for copy in copies:
        copy.wait()


def activation(features, up_tile, inputs, weight):
    before_act = dot(up_tile, inputs, nt_dims) * features ** (-0.5)
    sigmoid = 1.0 / (1.0 + jnp.exp(-before_act))
    return (before_act * sigmoid * weight).astype(bf16), sigmoid * (1.0 + before_act * (1.0 - sigmoid)) * weight


def new_tile(old, step, change, rows):
    return (old.astype(f32) - (step_size * step) * dot(change, rows)).astype(bf16)


def cut_kernel(go_ref, up_ref, down_ref, first_ref, second_ref, held, sems):
    rows, most = up_ref.shape[0], first_ref.shape[0]

    @pl.when(go_ref[0] == 0)
    def _():
        moves = [
            (up_ref, pl.ds(0, rows), first_ref.at[pl.ds(0, rows)]),
            (down_ref.at[pl.ds(0, most - rows)], pl.ds(rows, most - rows), first_ref.at[pl.ds(rows, most - rows)]),
            (down_ref.at[pl.ds(most - rows, 2 * rows - most)], pl.ds(most, 2 * rows - most), second_ref),
        ]
        ins = [pltpu.make_async_copy(a, held.at[p], sems.at[0, i]) for i, (a, p, _) in enumerate(moves)]
        outs = [pltpu.make_async_copy(held.at[p], b, sems.at[1, i]) for i, (_, p, b) in enumerate(moves)]
        start_all(ins)
        for copy, out in zip(ins, outs):
            copy.wait()
            out.start()
        wait_all(outs)


def update_rows(features, hidden, tile, weight, in_copies, grad_copies, up_from, down_from, up_to, down_to, space):
    inputs, grads, up, down, new_up, new_down, sems, out_sems = space
    up_copies = tile_copies(up_from, up, tile, sems.at[0])
    down_copies = tile_copies(down_from, down, tile, sems.at[1])
    up_outs = tile_copies(new_up, up_to, tile, out_sems.at[0])
    down_outs = tile_copies(new_down, down_to, tile, out_sems.at[1])
    start_all(up_copies[:1], in_copies, down_copies[:1], grad_copies, up_copies[1:], down_copies[1:])
    for i in range(len(up_copies)):
        here = pl.ds(i * tile, tile)
        up_copies[i].wait()
        if i == 0:
            wait_all(in_copies)
        activated, slope = activation(features, up[here, :], inputs[...], weight)
        down_copies[i].wait()
        if i == 0:
            wait_all(grad_copies)
        pre_grad = (dot(down[here, :], grads[...], nt_dims) * hidden ** (-0.5) * slope).astype(bf16)
        new_down[here, :] = new_tile(down[here, :], hidden ** (-0.5), activated, grads[...])
        down_outs[i].start()
        new_up[here, :] = new_tile(up[here, :], features ** (-0.5), pre_grad, inputs[...])
        up_outs[i].start()
    wait_all(up_outs + down_outs)


def learner_kernel(parts, height, features, hidden, tile, part_ref, weight_ref, *refs):
    units, (up_ref, down_ref, new_up_ref, new_down_ref), row_sems, space = refs[:-13], refs[-13:-9], refs[-9], refs[-8:]
    copies = gathered_copies(part_ref[0], parts, height, units, space[0], space[1], row_sems)
    rows = (up_ref, down_ref, new_up_ref, new_down_ref)
    update_rows(features, hidden, tile, weight_ref[...], *copies, *rows, space)


def assemble_kernel(parts, height, part_ref, *refs):
    units, (inputs_ref, grads_ref, sems) = refs[:-3], refs[-3:]
    in_copies, grad_copies = gathered_copies(part_ref[0], parts, height, units, inputs_ref, grads_ref, sems)
    start_all(in_copies, grad_copies)
    wait_all(in_copies + grad_copies)


def late_kernel(features, hidden, tile, count, go_ref, weight_ref, *refs):
    inputs_ref, grads_ref, piece_ref, _, _, new_up_ref, new_down_ref, slopes_ref, gradient_ref = refs[:9]
    row_sems, ahead, slopes, gradient, ahead_sems, *space = refs[9:]
    hidden_here = new_up_ref.shape[0]

    @pl.when(go_ref[0] == 1)
    def _():
        ahead_copy = pltpu.make_async_copy(piece_ref.at[pl.ds(count, tile)], ahead, ahead_sems.at[0])
        in_copies = [pltpu.make_async_copy(inputs_ref, space[0], row_sems.at[0])]
        grad_copies = [pltpu.make_async_copy(grads_ref, space[1], row_sems.at[1])]
        rows = [piece_ref.at[pl.ds(start, count)] for start in (0, hidden_here)]
        rows = rows + [ref.at[pl.ds(0, count)] for ref in (new_up_ref, new_down_ref)]
        ahead_copy.start()
        update_rows(features, hidden, tile, weight_ref[...], in_copies, grad_copies, *rows, space)
        ahead_copy.wait()
        activated, slopes[...] = activation(features, ahead[...], space[0][...], weight_ref[...])
        gradient[...] = dot(activated, space[1][...])
        outs = [
            pltpu.make_async_copy(slopes, slopes_ref, ahead_sems.at[1]),
            pltpu.make_async_copy(gradient, gradient_ref, ahead_sems.at[2]),
        ]
        start_all(outs)
        wait_all(outs)


def last_kernel(features, hidden, go_ref, *refs):
    inputs_ref, grads_ref, first_ref, down_ref, slopes_ref, gradient_ref, _, _, new_up_ref, new_down_ref = refs[:10]
    inputs, grads, up, down, slopes, gradient, new_up, new_down, sems, out_sems = refs[10:]
    tile = down_ref.shape[0]
    place = pl.ds(new_up_ref.shape[0] - tile, tile)

    @pl.when(go_ref[0] == 1)
    def _():
        moves = [(down_ref, down), (grads_ref, grads), (slopes_ref, slopes), (inputs_ref, inputs)]
        moves = moves + [(first_ref.at[place], up), (gradient_ref, gradient)]
        copies = [pltpu.make_async_copy(a, b, sems.at[i]) for i, (a, b) in enumerate(moves)]
        up_out = pltpu.make_async_copy(new_up, new_up_ref.at[place], out_sems.at[0])
        down_out = pltpu.make_async_copy(new_down, new_down_ref.at[place], out_sems.at[1])
        start_all(copies)
        wait_all(copies[:3])
        hidden_grad = dot(down[...], grads[...], nt_dims) * hidden ** (-0.5)
        pre_grad = (hidden_grad * slopes[...]).astype(bf16)
        wait_all(copies[3:5])
        new_up[...] = new_tile(up[...], features ** (-0.5), pre_grad, inputs[...])
        up_out.start()
        copies[5].wait()
        new_down[...] = (down[...].astype(f32) - (step_size * hidden ** (-0.5)) * gradient[...]).astype(bf16)
        down_out.start()
        wait_all([up_out, down_out])


def hold_kernel(go_ref, array_ref, held_ref, sem):
    @pl.when(go_ref[0] == 0)
    def _():
        copy = pltpu.make_async_copy(array_ref, held_ref, sem)
        copy.start()
        copy.wait()


def join_kernel(parts, row_count, part_ref, *refs):
    pieces, (left_ref, right_ref, joined_ref) = refs[:parts], refs[parts:]
    width = pieces[0].shape[1]
    blocks = pieces[0].shape[0] // row_count
    for j, piece in enumerate(pieces):
        start = lax.rem(part_ref[0] + parts - j, parts) * (blocks * width)
        for block in range(blocks):
            columns = pl.ds(pl.multiple_of(start + block * width, width), width)
            joined_ref[:, columns] = piece[block * row_count : (block + 1) * row_count, :]
    half = left_ref.shape[1]
    left_ref[...] = joined_ref[:, :half]
    right_ref[...] = joined_ref[:, half:]


def unset_kernel(*refs):
    pass


def unset(after, *like):
    arrays = pl.pallas_call(
        unset_kernel,
        out_shape=[jax.ShapeDtypeStruct(a.shape, a.dtype) for a in like],
        in_specs=[anywhere],
        out_specs=[anywhere] * len(like),
        cost_estimate=costs(1, 1),
    )(after)
    return tuple(arrays)


def on_device(
    decode_states,
    norm_gain,
    decode_routes,
    decode_gates,
    up_weight,
    down_weight,
    traj_inputs,
    traj_cotangents,
    traj_lengths,
    packing,
    learner_routes,
    learner_gates,
):
    experts, parts = lax.axis_size("exp"), lax.axis_size("dp")
    is_rollout = lax.axis_index("sect") == 0
    go = is_rollout.astype(i32).reshape(1)
    me = lax.axis_index("exp")
    part_ref = lax.axis_index("dp").reshape(1).astype(i32)
    up_here, down_here = up_weight[0, 0], down_weight[0, 0]
    hidden_here, features = up_here.shape
    hidden = hidden_here * parts
    steps, row_count, routes_each = decode_routes.shape
    half_steps = steps // 2
    share = features // parts
    blocks = share // lanes
    capacity = 3 * row_count * routes_each // (2 * experts)
    slots = experts * capacity
    stacked = blocks * row_count
    moved = blocks * slots
    tile = hidden_here // 3
    line = 8
    per_half = traj_inputs.shape[1]
    gathered = experts * 2 * per_half
    height = 4 * per_half + note_rows

    routes = jnp.swapaxes(decode_routes, 1, 2).reshape(steps * routes_each, row_count)
    gates = jnp.swapaxes(decode_gates, 1, 2).reshape(steps * routes_each, row_count)
    targets, gates, states, payload, own_rows = pl.pallas_call(
        functools.partial(prepare_kernel, experts, capacity),
        out_shape=[
            jax.ShapeDtypeStruct((steps, routes_each, stacked), i32),
            jax.ShapeDtypeStruct((steps * routes_each, stacked), f32),
            jax.ShapeDtypeStruct((stacked, lanes), f32),
            jax.ShapeDtypeStruct((moved, lanes), bf16),
            jax.ShapeDtypeStruct((2 * per_half, share), bf16),
        ],
        in_specs=[smem, vmem, vmem] + [stays] * 3,
        scratch_shapes=[pltpu.VMEM((row_count, share), bf16), pltpu.SemaphoreType.DMA((3,))],
        compiler_params=fits(60),
        cost_estimate=costs(1, 1),
    )(part_ref, routes, gates, decode_states, traj_inputs[0], traj_cotangents[0])

    crossed_rows = flipped(own_rows, "sect", 1)
    up_sent, down_sent, _ = lax.optimization_barrier((up_here, down_here, own_rows))
    cut = hidden_here + 2 * tile
    pieces = pl.pallas_call(
        cut_kernel,
        out_shape=[jax.ShapeDtypeStruct((rows, features), bf16) for rows in (cut, tile)],
        in_specs=[smem] + [stays] * 2,
        out_specs=[stays] * 2,
        scratch_shapes=[pltpu.VMEM((2 * hidden_here, features), bf16), pltpu.SemaphoreType.DMA((2, 3))],
        compiler_params=fits(60),
        cost_estimate=costs(1, 1),
    )(go, up_sent, down_sent)
    first_piece, second_piece, crossed_rows = lax.optimization_barrier((*pieces, crossed_rows))
    first_there = lax.ppermute(first_piece, "sect", [(1, 0)])
    second_there = lax.ppermute(second_piece, "sect", [(1, 0)])

    gain = norm_gain.reshape(1, features)
    def expert_forward(arrived, up_mat, down_mat):
        return pl.pallas_call(
            functools.partial(expert_kernel, parts, slots, capacity, features, hidden),
            out_shape=[jax.ShapeDtypeStruct((moved, lanes), bf16)] * parts,
            in_specs=[smem, vmem] + [vmem] * parts + [stays, stays],
            scratch_shapes=[
                pltpu.VMEM((hidden_here, features), bf16),
                pltpu.VMEM((hidden_here, features), bf16),
                pltpu.VMEM((slots, features), bf16),
                pltpu.VMEM((moved, lanes), bf16),
                pltpu.VMEM((moved, moved), bf16),
                pltpu.SemaphoreType.DMA((2,)),
            ],
            compiler_params=fits(48),
            cost_estimate=costs(1, 1),
        )(part_ref, gain, *arrived, up_mat, down_mat)

    def decode_step(step, states, payload, up_mat, down_mat):
        last = step in (half_steps - 1, steps - 1)
        arrived = lax.all_to_all(payload, "exp", split_axis=0, concat_axis=0, tiled=True)
        arrived = [arrived] + [shifted(arrived, "dp", j) for j in range(1, parts)]
        partials = expert_forward(arrived, up_mat, down_mat)
        received = [shifted(partials[j], "dp", j) for j in range(1, parts)]
        summed = sum((r.astype(f32) for r in received), partials[0].astype(f32)).astype(bf16)
        returned = lax.all_to_all(summed, "exp", split_axis=0, concat_axis=0, tiled=True)
        outs = [
            jax.ShapeDtypeStruct((stacked, lanes), f32),
            jax.ShapeDtypeStruct((stacked if last else moved, lanes), bf16),
        ]
        results = pl.pallas_call(
            functools.partial(combine_kernel, step, last),
            out_shape=outs,
            compiler_params=fits(16),
            cost_estimate=costs(1, 1),
        )(targets, gates, states, returned)
        return tuple(results)
    def learner_rows(halves):
        wide = learner_routes.shape[0]
        notes = [learner_routes.T, learner_gates.T, traj_lengths[0], packing]
        unit = pl.pallas_call(
            unit_kernel,
            out_shape=jax.ShapeDtypeStruct((height, share), bf16),
            in_specs=[anywhere] * 2 + [vmem] * 4,
            scratch_shapes=[pltpu.SemaphoreType.DMA((4,))],
            compiler_params=fits(16),
            cost_estimate=costs(1, 1),
        )(*halves, *notes)
        others, group = [0], experts
        while group > line:
            group = group // 2
            unit = jnp.concatenate([unit, flipped(unit, "exp", group)])
            others = others + [o ^ group for o in others]
        far = group // 2
        shifts = sorted(range(1, far), key=lambda s: (min(s, far - s), s))

        def along(array, s):
            pairs = [(i, i // group * group + (i + 2 * s) % group) for i in range(experts)]
            return lax.ppermute(array, "exp", pairs)

        side = flipped(unit, "exp", 1)
        near = [along(unit, s) for s in shifts[:-1]]
        unit, side, *near = lax.optimization_barrier((unit, side, *near))
        last = along(unit, shifts[-1])
        sides = [flipped(n, "exp", 1) for n in near]
        units = [
            jnp.concatenate([unit, side, *near]),
            jnp.concatenate(sides),
            jnp.concatenate([last, flipped(last, "exp", 1)]),
        ]
        places = [(0, 0), (1, 0)] + [(f, s) for f in range(2) for s in shifts[:-1]] + [(f, shifts[-1]) for f in range(2)]
        sources = [(group, flip, 2 * s, o) for flip, s in places for o in others]
        return units, sources

    def with_parts(units, sources):
        units = list(units)
        others = [shifted(u, "dp", j) for j in range(1, parts) for u in units]
        wide = learner_routes.shape[0]
        weights = pl.pallas_call(
            functools.partial(
                weights_kernel, height, 2, learner_routes.shape[1], traj_lengths.shape[2], wide, sources
            ),
            out_shape=jax.ShapeDtypeStruct((1, gathered), f32),
            in_specs=[smem] + [anywhere] * len(units),
            scratch_shapes=[
                pltpu.VMEM((experts, note_rows, wide), bf16),
                pltpu.VMEM((experts, wide), f32),
                pltpu.VMEM((2 * experts, wide), f32),
                pltpu.SemaphoreType.DMA((experts,)),
            ],
            compiler_params=fits(16),
            cost_estimate=costs(1, 1),
        )(me.reshape(1).astype(i32), *units)
        return units + others, weights

    rows_like = jax.ShapeDtypeStruct((gathered, features), bf16)
    weight_like = jax.ShapeDtypeStruct((hidden_here, features), bf16)
    weights_like = jax.ShapeDtypeStruct((1, gathered), f32)

    def sems_of(*shape):
        return pltpu.SemaphoreType.DMA(shape)

    def update_space(rows):
        held = [pltpu.VMEM((gathered, features), bf16)] * 2 + [pltpu.VMEM((rows, features), bf16)] * 4
        return held + [sems_of(2, rows // tile)] * 2

    def update(units, weights, up_mat, down_mat):
        return pl.pallas_call(
            functools.partial(learner_kernel, parts, height, features, hidden, tile),
            out_shape=[weight_like] * 2,
            in_specs=[smem, vmem] + [anywhere] * (len(units) + 2),
            out_specs=[anywhere] * 2,
            scratch_shapes=[sems_of(2 * parts * experts)] + update_space(hidden_here),
            compiler_params=fits(56),
            cost_estimate=costs(1, 1),
        )(part_ref, weights, *units, up_mat, down_mat)

    slopes_like = jax.ShapeDtypeStruct((tile, gathered), f32)
    gradient_like = jax.ShapeDtypeStruct((tile, features), f32)

    def spaces(*like):
        return [pltpu.VMEM(a.shape, a.dtype) for a in like]

    def update_late(new_up, new_down):
        piece_like = jax.ShapeDtypeStruct((tile, features), bf16)
        return pl.pallas_call(
            functools.partial(late_kernel, features, hidden, tile, 2 * tile),
            out_shape=[weight_like] * 2 + [slopes_like, gradient_like],
            in_specs=[smem, vmem] + [stays] * 5,
            out_specs=[anywhere] * 4,
            scratch_shapes=[sems_of(2)]
            + spaces(piece_like, slopes_like, gradient_like)
            + [sems_of(3)]
            + update_space(2 * tile),
            input_output_aliases={5: 0, 6: 1},
            compiler_params=fits(60),
            cost_estimate=costs(1, 1),
        )(go, weights, inputs, grads, first_there, new_up, new_down)

    def update_last(slopes, gradient, new_up, new_down):
        piece_like = jax.ShapeDtypeStruct((tile, features), bf16)
        return pl.pallas_call(
            functools.partial(last_kernel, features, hidden),
            out_shape=[weight_like] * 2,
            in_specs=[smem] + [stays] * 8,
            out_specs=[anywhere] * 2,
            scratch_shapes=spaces(rows_like, rows_like, piece_like, piece_like, slopes_like, gradient_like)
            + spaces(piece_like, piece_like)
            + [sems_of(6), sems_of(2)],
            input_output_aliases={7: 0, 8: 1},
            compiler_params=fits(60),
            cost_estimate=costs(1, 1),
        )(go, inputs, grads, first_there, second_there, slopes, gradient, new_up, new_down)

    half_like = jax.ShapeDtypeStruct((row_count, features // 2), bf16)
    block_rows = height * max(1, experts // line)
    gather_like = [jax.ShapeDtypeStruct((block_rows * n, share), bf16) for n in (line // 2, line // 2 - 2, 2)]

    sources = []

    def first_rollout():
        now, sent = decode_step(0, states, payload, up_here, down_here)
        return (now, sent) + unset(sent, *gather_like)

    def first_learner():
        units, places = learner_rows([crossed_rows, own_rows])
        sources.append(places)
        return (states, payload) + tuple(units)

    states, payload, *rows = lax.cond(is_rollout, first_rollout, first_learner)

    def second_rollout():
        now, sent = states, payload
        for step in range(1, half_steps):
            now, sent = decode_step(step, now, sent, up_here, down_here)
        return (now,) + unset(now, up_here, down_here)

    def second_learner():
        units, weights = with_parts(rows, sources[0])
        return (states,) + tuple(update(units, weights, up_here, down_here))

    states, new_up, new_down = lax.cond(is_rollout, second_rollout, second_learner)
    states_there = lax.ppermute(states, "sect", [(0, 1)])

    held_up = pl.pallas_call(
        hold_kernel,
        out_shape=weight_like,
        in_specs=[smem, stays],
        out_specs=vmem,
        scratch_shapes=[pltpu.SemaphoreType.DMA],
        compiler_params=fits(16),
        cost_estimate=costs(1, 1),
    )(go, new_up)

    def third_rollout():
        return (states, payload) + tuple(learner_rows([own_rows, crossed_rows])[0])

    def third_learner():
        sent = pl.pallas_call(
            functools.partial(dispatch_kernel, half_steps),
            out_shape=jax.ShapeDtypeStruct((moved, lanes), bf16),
            compiler_params=fits(16),
            cost_estimate=costs(1, 1),
        )(targets, states_there)
        now, sent = decode_step(half_steps, states_there, sent, held_up, new_down)
        return (now, sent) + unset(sent, *gather_like)

    states, payload, *rows = lax.cond(is_rollout, third_rollout, third_learner)

    def fourth_rollout():
        units, weights = with_parts(rows, sources[0])
        whole = pl.pallas_call(
            functools.partial(assemble_kernel, parts, height),
            out_shape=[rows_like] * 2,
            in_specs=[smem] + [anywhere] * len(units),
            scratch_shapes=[sems_of(2 * parts * experts)],
            compiler_params=fits(62),
            cost_estimate=costs(1, 1),
        )(part_ref, *units)
        return unset(weights, half_like, half_like) + tuple(whole) + (weights,)

    def fourth_learner():
        now, sent = states, payload
        for step in range(half_steps + 1, steps):
            now, sent = decode_step(step, now, sent, held_up, new_down)
        pieces = [sent] + [shifted(sent, "dp", j) for j in range(1, parts)]
        left, right = pl.pallas_call(
            functools.partial(join_kernel, parts, row_count),
            out_shape=[half_like] * 2,
            in_specs=[smem] + [vmem] * parts,
            scratch_shapes=[pltpu.VMEM((row_count, features), bf16)],
            cost_estimate=costs(1, 1),
        )(part_ref, *pieces)
        return (left, right) + unset(left, rows_like, rows_like, weights_like)

    left, right, inputs, grads, weights = lax.cond(is_rollout, fourth_rollout, fourth_learner)

    new_up, new_down, slopes, gradient = update_late(new_up, new_down)
    delivered = lax.ppermute(left, "sect", [(1, 0)])
    new_up, new_down = update_last(slopes, gradient, new_up, new_down)
    right, new_up = lax.optimization_barrier((right, new_up))
    final_states = jnp.where(is_rollout, delivered, right)
    return final_states, new_up[None, None], new_down[None, None]


def solution(mesh):
    in_specs = (
        P("exp", None),
        P(),
        P(None, "exp", None),
        P(None, "exp", None),
        P("sect", "exp", "dp", None),
        P("sect", "exp", "dp", None),
        P("sect", "exp", None),
        P("sect", "exp", None),
        P("exp", None, None),
        P("exp", None),
        P("exp", None),
        P("exp", None),
    )
    out_specs = (P("exp", "sect"), P("sect", "exp", "dp", None), P("sect", "exp", "dp", None))
    return jax.shard_map(on_device, mesh=mesh, in_specs=in_specs, out_specs=out_specs, check_vma=False)
```

```python
import functools

import jax
import jax.numpy as jnp
from jax import lax
from jax.experimental import pallas as pl
from jax.experimental.pallas import tpu as pltpu
from jax.sharding import PartitionSpec as P

step_size = 3.0
norm_eps = 1e-06
lanes = 256
note_rows = 16
f32, bf16, i32 = jnp.float32, jnp.bfloat16, jnp.int32
nt_dims = (((1,), (1,)), ((), ()))
tn_dims = (((0,), (0,)), ((), ()))
smem = pl.BlockSpec(memory_space=pltpu.SMEM)
vmem = pl.BlockSpec(memory_space=pltpu.VMEM)
anywhere = pl.BlockSpec(memory_space=pl.ANY)
stays = pl.BlockSpec(memory_space=pltpu.HBM)


def shifted(array, axis, by):
    size = lax.axis_size(axis)
    return lax.ppermute(array, axis, [(i, (i + by) % size) for i in range(size)])


def flipped(array, axis, bit):
    return lax.ppermute(array, axis, [(i, i ^ bit) for i in range(lax.axis_size(axis))])


def fits(megabytes):
    return pltpu.CompilerParams(vmem_limit_bytes=megabytes * 1024 * 1024)


def costs(flops, moved):
    return pl.CostEstimate(flops=flops, bytes_accessed=moved, transcendentals=0)


def dot(a, b, dims=(((1,), (0,)), ((), ())), precision=None):
    return lax.dot_general(a, b, dims, precision=precision, preferred_element_type=f32)


def one_hot(rows, targets_ref):
    ids = lax.broadcasted_iota(i32, (rows, targets_ref.shape[1]), 0)
    hits = [jnp.where(ids == targets_ref[k : k + 1, :], 1.0, 0.0) for k in range(targets_ref.shape[0])]
    return sum(hits[1:], hits[0]).astype(bf16)


def prepare_kernel(
    experts, capacity, part_ref, all_routes_ref, all_gates_ref, all_rows_ref, inputs_ref, grads_ref,
    targets_ref, tiled_ref, states_ref, payload_ref, sent_ref, rows_ref, own_ref, routes_ref, gates_ref, sems,
):
    row_count, share = rows_ref.shape
    steps, routes_each = targets_ref.shape[:2]
    stacked, width = states_ref.shape
    blocks = stacked // row_count
    own = pl.ds(pl.multiple_of(part_ref[0] * share, share), share)
    held = inputs_ref.shape[0]
    row_copy = pltpu.make_async_copy(all_rows_ref.at[:, own], rows_ref, sems.at[0])
    copies = [
        pltpu.make_async_copy(inputs_ref.at[:, own], own_ref.at[pl.ds(0, held)], sems.at[1]),
        pltpu.make_async_copy(grads_ref.at[:, own], own_ref.at[pl.ds(held, held)], sems.at[2]),
    ]
    table_copies = [
        pltpu.make_async_copy(all_routes_ref, routes_ref, sems.at[3]),
        pltpu.make_async_copy(all_gates_ref, gates_ref, sems.at[4]),
    ]
    out_copy = pltpu.make_async_copy(own_ref, sent_ref, sems.at[5])
    for copy in table_copies + copies + [row_copy]:
        copy.start()
    before = lax.broadcasted_iota(i32, (row_count, stacked), 0)
    after = lax.rem(lax.broadcasted_iota(i32, (row_count, stacked), 1), row_count)
    repeat = jnp.where(before == after, 1.0, 0.0)
    earlier = jnp.where(before < after, 1.0, 0.0).astype(bf16)
    every = jnp.ones((row_count, stacked), bf16)
    block_of = lax.div(lax.broadcasted_iota(i32, (1, stacked), 1), row_count)
    expert_ids = lax.broadcasted_iota(i32, (experts, row_count), 0)
    tall_ids = lax.broadcasted_iota(i32, (experts, stacked), 0)
    for copy in table_copies + copies:
        copy.wait()
    out_copy.start()
    routes = dot(routes_ref[...].astype(f32), repeat, precision=lax.Precision.HIGHEST)
    routes = (routes + 0.5).astype(i32)
    tiled_ref[...] = dot(gates_ref[...], repeat, precision=lax.Precision.HIGHEST)
    for step in range(steps):
        seen = jnp.zeros((experts, stacked), f32)
        for k in range(routes_each):
            at = step * routes_each + k
            member = jnp.where(expert_ids == routes_ref[at : at + 1, :], 1.0, 0.0).astype(bf16)
            route = routes[at : at + 1, :]
            ahead = dot(member, earlier) + seen
            rank = jnp.sum(jnp.where(tall_ids == route, ahead, 0.0), axis=0, keepdims=True)
            seen = seen + dot(member, every)
            place = (route * blocks + block_of) * capacity + (rank + 0.5).astype(i32)
            targets_ref[step, k : k + 1, :] = place
    row_copy.wait()
    for block in range(blocks):
        columns = slice(block * width, (block + 1) * width)
        states_ref[block * row_count : (block + 1) * row_count, :] = rows_ref[:, columns].astype(f32)
    payload_ref[...] = dot(one_hot(payload_ref.shape[0], targets_ref.at[0]), states_ref[...].astype(bf16)).astype(bf16)
    out_copy.wait()


def dispatch_kernel(step, targets_ref, states_ref, payload_ref):
    payload_ref[...] = dot(one_hot(payload_ref.shape[0], targets_ref.at[step]), states_ref[...].astype(bf16)).astype(bf16)


def combine_kernel(step, last, targets_ref, gates_ref, states_ref, returned_ref, new_ref, payload_ref):
    ids = lax.broadcasted_iota(i32, (returned_ref.shape[0], states_ref.shape[0]), 0)
    weights = jnp.zeros(ids.shape, f32)
    routes_each = targets_ref.shape[1]
    for k in range(routes_each):
        at = step * routes_each + k
        weights = weights + jnp.where(ids == targets_ref[step, k : k + 1, :], gates_ref[at : at + 1, :], 0.0)
    high = weights.astype(bf16)
    low = (weights - high.astype(f32)).astype(bf16)
    returned = returned_ref[...]
    states = states_ref[...] + (dot(high, returned, tn_dims) + dot(low, returned, tn_dims))
    new_ref[...] = states
    if last:
        payload_ref[...] = states.astype(bf16)
    else:
        payload_ref[...] = dot(one_hot(returned.shape[0], targets_ref.at[step + 1]), states.astype(bf16)).astype(bf16)


def expert_kernel(parts, slots, capacity, features, hidden, part_ref, gain_ref, *refs):
    arrived, (up_ref, down_ref) = refs[:parts], refs[parts : parts + 2]
    outs = refs[parts + 2 : 2 * parts + 2]
    up_held, down_held, normed_ref, stack_ref, order_ref, sems = refs[2 * parts + 2 :]
    width = arrived[0].shape[1]
    blocks = features // (parts * width)
    me = part_ref[0]
    up_copy = pltpu.make_async_copy(up_ref, up_held, sems.at[0])
    down_copy = pltpu.make_async_copy(down_ref, down_held, sems.at[1])
    up_copy.start()
    down_copy.start()
    moved = blocks * slots
    column = lax.broadcasted_iota(i32, (1, moved), 1)
    slot = lax.rem(column, slots)
    target = (lax.div(slot, capacity) * blocks + lax.div(column, slots)) * capacity + lax.rem(slot, capacity)
    hits = lax.broadcasted_iota(i32, (moved, moved), 0) == target
    order_ref[...] = jnp.where(hits, 1.0, 0.0).astype(bf16)
    square = jnp.zeros((slots, 1), f32)
    stacks = []
    for ref in arrived:
        stack = dot(order_ref[...], ref[...], tn_dims)
        stacks.append(stack)
        for block in range(blocks):
            rows = stack[block * slots : (block + 1) * slots]
            square = square + jnp.sum(rows * rows, axis=1, keepdims=True)
    scale = lax.rsqrt(square * (1.0 / features) + norm_eps)
    for j, stack in enumerate(stacks):
        start = lax.rem(me + parts - j, parts) * (blocks * width)
        for block in range(blocks):
            rows = stack[block * slots : (block + 1) * slots]
            columns = pl.ds(pl.multiple_of(start + block * width, width), width)
            normed_ref[:, columns] = (rows * scale * gain_ref[:, columns]).astype(bf16)
    up_copy.wait()
    before_act = dot(normed_ref[...], up_held[...], nt_dims) * features ** (-0.5)
    activated = (before_act / (1.0 + jnp.exp(-before_act))).astype(bf16)
    down_copy.wait()
    normed_ref[...] = (dot(activated, down_held[...]) * hidden ** (-0.5)).astype(bf16)
    for j, out_ref in enumerate(outs):
        start = lax.rem(me + j, parts) * (blocks * width)
        for block in range(blocks):
            columns = pl.ds(pl.multiple_of(start + block * width, width), width)
            stack_ref[block * slots : (block + 1) * slots, :] = normed_ref[:, columns]
        out_ref[...] = dot(order_ref[...], stack_ref[...]).astype(bf16)


def gathered_copies(part, parts, height, units, inputs_ref, grads_ref, sems):
    per_part = len(units) // parts
    width = units[0].shape[1]
    rows = (height - note_rows) // 2
    in_copies, grad_copies = [], []
    for j in range(parts):
        columns = pl.ds(pl.multiple_of(lax.rem(part + parts - j, parts) * width, width), width)
        blocks = [(u, at) for u in units[j * per_part : (j + 1) * per_part] for at in range(0, u.shape[0], height)]
        for i, (unit, at) in enumerate(blocks):
            place, sem = pl.ds(i * rows, rows), 2 * (j * len(blocks) + i)
            source = unit.at[pl.ds(at, rows)]
            in_copies.append(pltpu.make_async_copy(source, inputs_ref.at[place, columns], sems.at[sem]))
            source = unit.at[pl.ds(at + rows, rows)]
            grad_copies.append(pltpu.make_async_copy(source, grads_ref.at[place, columns], sems.at[sem + 1]))
    return in_copies, grad_copies


def unit_kernel(first_ref, second_ref, routes_ref, gates_ref, lengths_ref, shards_ref, unit_ref, sems):
    held = first_ref.shape[0] // 2
    copies = []
    for i, ref in enumerate((first_ref, second_ref)):
        for j in range(2):
            place = pl.ds((2 * j + i) * held, held)
            source = ref.at[pl.ds(j * held, held)]
            copies.append(pltpu.make_async_copy(source, unit_ref.at[place], sems.at[2 * i + j]))
    for copy in copies:
        copy.start()
    wide = routes_ref.shape[1]

    def widened(ref):
        count = ref.shape[1]
        places = lax.broadcasted_iota(i32, (count, wide), 0) == lax.broadcasted_iota(i32, (count, wide), 1)
        return dot(ref[...].astype(f32), jnp.where(places, 1.0, 0.0))

    gates = gates_ref[...]
    terms = []
    for _ in range(3):
        terms.append(gates.astype(bf16).astype(f32))
        gates = gates - terms[-1]
    tables = [routes_ref[...].astype(f32)] + terms + [widened(lengths_ref), widened(shards_ref)]
    ids = lax.broadcasted_iota(i32, (note_rows, wide), 0)
    notes, at = jnp.zeros((note_rows, wide), f32), 0
    for table in tables:
        for row in range(table.shape[0]):
            notes = notes + jnp.where(ids == at, table[row : row + 1, :], 0.0)
            at += 1
    base = 4 * held
    unit_ref[base:, :] = jnp.zeros((note_rows, unit_ref.shape[1]), bf16)
    unit_ref[base:, :wide] = notes.astype(bf16)
    for copy in copies:
        copy.wait()


def weights_kernel(height, halves, each, trajs, wide, sources, me_ref, *refs):
    units, (weights_ref, notes_ref, table_ref, facts_ref, sems) = refs[:-5], refs[-5:]
    blocks = [(u, at) for u in units for at in range(0, u.shape[0], height)]
    count = len(blocks)
    per_half = (height - note_rows) // (2 * halves)
    longest = wide // count
    total = weights_ref.shape[1]
    copies = []
    for i, (unit, at) in enumerate(blocks):
        source = unit.at[pl.ds(at + height - note_rows, note_rows), pl.ds(0, wide)]
        copies.append(pltpu.make_async_copy(source, notes_ref.at[i], sems.at[i]))
    for copy in copies:
        copy.start()
    for copy in copies:
        copy.wait()
    me = me_ref[0]
    ids = lax.broadcasted_iota(i32, (count, 1), 0)
    places = lax.broadcasted_iota(i32, (note_rows, wide), 1)
    holder_of = jnp.zeros((count, 1), f32)
    for i, (group, flip, far, near) in enumerate(sources):
        place = lax.rem((lax.rem(me, group) ^ flip) + group - far, group)
        holder = ((lax.div(me, group) * group + place) ^ near).astype(f32)
        holder_of = holder_of + jnp.where(ids == i, holder, 0.0)
        notes = notes_ref[i].astype(f32)
        row = jnp.zeros((1, wide), f32)
        for k in range(each):
            gate = sum(notes[(1 + t) * each + k : (1 + t) * each + k + 1, :] for t in range(3))
            row = row + jnp.where(notes[k : k + 1, :] == me.astype(f32), gate, 0.0)
        table_ref[i : i + 1, :] = row
        for half in range(halves):
            shards = pltpu.roll(notes, (trajs - half * trajs) % wide, 1) if half != 1 else notes
            shards = jnp.where((places >= trajs) & (places < 2 * trajs), shards, 0.0)
            shards = jnp.where(places == 2 * trajs, holder, shards)
            facts = notes[4 * each + half : 4 * each + half + 1, :] + shards[4 * each + halves : 4 * each + halves + 1, :]
            facts_ref[i * halves + half : i * halves + half + 1, :] = facts
    facts = facts_ref[...]
    down, across = [lax.broadcasted_iota(i32, (wide, wide), d) for d in (0, 1)]
    starts = dot(facts, jnp.where((down < across) & (down < trajs), 1.0, 0.0))
    row_ids = lax.broadcasted_iota(i32, (count * halves, total), 1)
    of_row = lax.div(row_ids, per_half) == lax.broadcasted_iota(i32, (count * halves, total), 0)
    of_row = jnp.where(of_row, 1.0, 0.0)
    facts, starts = dot(facts, of_row, tn_dims), dot(starts, of_row, tn_dims)[:trajs]
    place = lax.rem(lax.broadcasted_iota(i32, (1, total), 1), per_half).astype(f32)
    inside = (place >= starts) & (place < starts + facts[:trajs])
    offset = jnp.sum(jnp.where(inside, place - starts, 0.0), axis=0, keepdims=True)
    shard = jnp.sum(jnp.where(inside, facts[trajs : 2 * trajs], 0.0), axis=0, keepdims=True)
    slot = (facts[2 * trajs : 2 * trajs + 1] * longest + offset + 0.5).astype(i32)
    chosen = jnp.where(lax.broadcasted_iota(i32, (wide, total), 0) == slot, 1.0, 0.0)
    gates = dot(table_ref[...], chosen, precision=lax.Precision.HIGHEST)
    weights_ref[...] = jnp.sum(jnp.where(holder_of == shard, gates, 0.0), axis=0, keepdims=True)


def tile_copies(ref, held, tile, sems):
    places = [pl.ds(start, tile) for start in range(0, ref.shape[0], tile)]
    return [pltpu.make_async_copy(ref.at[p], held.at[p], sems.at[i]) for i, p in enumerate(places)]


def start_all(*groups):
    for copies in groups:
        for copy in copies:
            copy.start()


def wait_all(copies):
    for copy in copies:
        copy.wait()


def activation(features, up_tile, inputs, weight):
    before_act = dot(up_tile, inputs, nt_dims) * features ** (-0.5)
    sigmoid = 1.0 / (1.0 + jnp.exp(-before_act))
    return (before_act * sigmoid * weight).astype(bf16), sigmoid * (1.0 + before_act * (1.0 - sigmoid)) * weight


def new_tile(old, step, change, rows):
    return (old.astype(f32) - (step_size * step) * dot(change, rows)).astype(bf16)


def cut_kernel(go_ref, up_ref, down_ref, first_ref, second_ref, held, sems):
    rows, most = up_ref.shape[0], first_ref.shape[0]

    @pl.when(go_ref[0] == 0)
    def _():
        moves = [
            (up_ref, pl.ds(0, rows), first_ref.at[pl.ds(0, rows)]),
            (down_ref.at[pl.ds(0, most - rows)], pl.ds(rows, most - rows), first_ref.at[pl.ds(rows, most - rows)]),
            (down_ref.at[pl.ds(most - rows, 2 * rows - most)], pl.ds(most, 2 * rows - most), second_ref),
        ]
        ins = [pltpu.make_async_copy(a, held.at[p], sems.at[0, i]) for i, (a, p, _) in enumerate(moves)]
        outs = [pltpu.make_async_copy(held.at[p], b, sems.at[1, i]) for i, (_, p, b) in enumerate(moves)]
        start_all(ins)
        for copy, out in zip(ins, outs):
            copy.wait()
            out.start()
        wait_all(outs)


def update_rows(features, hidden, tile, weight, in_copies, grad_copies, up_from, down_from, up_to, down_to, space):
    inputs, grads, up, down, new_up, new_down, sems, out_sems = space
    up_copies = tile_copies(up_from, up, tile, sems.at[0])
    down_copies = tile_copies(down_from, down, tile, sems.at[1])
    up_outs = tile_copies(new_up, up_to, tile, out_sems.at[0])
    down_outs = tile_copies(new_down, down_to, tile, out_sems.at[1])
    start_all(up_copies[:1], in_copies, down_copies[:1], grad_copies, up_copies[1:], down_copies[1:])
    for i in range(len(up_copies)):
        here = pl.ds(i * tile, tile)
        up_copies[i].wait()
        if i == 0:
            wait_all(in_copies)
        activated, slope = activation(features, up[here, :], inputs[...], weight)
        down_copies[i].wait()
        if i == 0:
            wait_all(grad_copies)
        pre_grad = (dot(down[here, :], grads[...], nt_dims) * hidden ** (-0.5) * slope).astype(bf16)
        new_down[here, :] = new_tile(down[here, :], hidden ** (-0.5), activated, grads[...])
        down_outs[i].start()
        new_up[here, :] = new_tile(up[here, :], features ** (-0.5), pre_grad, inputs[...])
        up_outs[i].start()
    wait_all(up_outs + down_outs)


def learner_kernel(parts, height, features, hidden, tile, part_ref, weight_ref, *refs):
    units, (up_ref, down_ref, new_up_ref, new_down_ref), row_sems, space = refs[:-13], refs[-13:-9], refs[-9], refs[-8:]
    copies = gathered_copies(part_ref[0], parts, height, units, space[0], space[1], row_sems)
    rows = (up_ref, down_ref, new_up_ref, new_down_ref)
    update_rows(features, hidden, tile, weight_ref[...], *copies, *rows, space)


def assemble_kernel(parts, height, part_ref, *refs):
    units, (inputs_ref, grads_ref, sems) = refs[:-3], refs[-3:]
    in_copies, grad_copies = gathered_copies(part_ref[0], parts, height, units, inputs_ref, grads_ref, sems)
    start_all(in_copies, grad_copies)
    wait_all(in_copies + grad_copies)


def late_kernel(features, hidden, tile, count, go_ref, weight_ref, *refs):
    inputs_ref, grads_ref, piece_ref, _, _, new_up_ref, new_down_ref, slopes_ref, gradient_ref = refs[:9]
    row_sems, ahead, slopes, gradient, ahead_sems, *space = refs[9:]
    hidden_here = new_up_ref.shape[0]

    @pl.when(go_ref[0] == 1)
    def _():
        ahead_copy = pltpu.make_async_copy(piece_ref.at[pl.ds(count, tile)], ahead, ahead_sems.at[0])
        in_copies = [pltpu.make_async_copy(inputs_ref, space[0], row_sems.at[0])]
        grad_copies = [pltpu.make_async_copy(grads_ref, space[1], row_sems.at[1])]
        rows = [piece_ref.at[pl.ds(start, count)] for start in (0, hidden_here)]
        rows = rows + [ref.at[pl.ds(0, count)] for ref in (new_up_ref, new_down_ref)]
        ahead_copy.start()
        update_rows(features, hidden, tile, weight_ref[...], in_copies, grad_copies, *rows, space)
        ahead_copy.wait()
        activated, slopes[...] = activation(features, ahead[...], space[0][...], weight_ref[...])
        gradient[...] = dot(activated, space[1][...])
        outs = [
            pltpu.make_async_copy(slopes, slopes_ref, ahead_sems.at[1]),
            pltpu.make_async_copy(gradient, gradient_ref, ahead_sems.at[2]),
        ]
        start_all(outs)
        wait_all(outs)


def last_kernel(features, hidden, go_ref, *refs):
    inputs_ref, grads_ref, first_ref, down_ref, slopes_ref, gradient_ref, _, _, new_up_ref, new_down_ref = refs[:10]
    inputs, grads, up, down, slopes, gradient, new_up, new_down, sems, out_sems = refs[10:]
    tile = down_ref.shape[0]
    place = pl.ds(new_up_ref.shape[0] - tile, tile)

    @pl.when(go_ref[0] == 1)
    def _():
        moves = [(down_ref, down), (grads_ref, grads), (slopes_ref, slopes), (inputs_ref, inputs)]
        moves = moves + [(first_ref.at[place], up), (gradient_ref, gradient)]
        copies = [pltpu.make_async_copy(a, b, sems.at[i]) for i, (a, b) in enumerate(moves)]
        up_out = pltpu.make_async_copy(new_up, new_up_ref.at[place], out_sems.at[0])
        down_out = pltpu.make_async_copy(new_down, new_down_ref.at[place], out_sems.at[1])
        start_all(copies)
        wait_all(copies[:3])
        hidden_grad = dot(down[...], grads[...], nt_dims) * hidden ** (-0.5)
        pre_grad = (hidden_grad * slopes[...]).astype(bf16)
        wait_all(copies[3:5])
        new_up[...] = new_tile(up[...], features ** (-0.5), pre_grad, inputs[...])
        up_out.start()
        copies[5].wait()
        new_down[...] = (down[...].astype(f32) - (step_size * hidden ** (-0.5)) * gradient[...]).astype(bf16)
        down_out.start()
        wait_all([up_out, down_out])


def hold_kernel(go_ref, array_ref, held_ref, sem):
    @pl.when(go_ref[0] == 0)
    def _():
        copy = pltpu.make_async_copy(array_ref, held_ref, sem)
        copy.start()
        copy.wait()


def join_kernel(parts, row_count, part_ref, *refs):
    pieces, (left_ref, right_ref, joined_ref) = refs[:parts], refs[parts:]
    width = pieces[0].shape[1]
    blocks = pieces[0].shape[0] // row_count
    for j, piece in enumerate(pieces):
        start = lax.rem(part_ref[0] + parts - j, parts) * (blocks * width)
        for block in range(blocks):
            columns = pl.ds(pl.multiple_of(start + block * width, width), width)
            joined_ref[:, columns] = piece[block * row_count : (block + 1) * row_count, :]
    half = left_ref.shape[1]
    left_ref[...] = joined_ref[:, :half]
    right_ref[...] = joined_ref[:, half:]


def unset_kernel(*refs):
    pass


def unset(after, *like):
    arrays = pl.pallas_call(
        unset_kernel,
        out_shape=[jax.ShapeDtypeStruct(a.shape, a.dtype) for a in like],
        in_specs=[anywhere],
        out_specs=[anywhere] * len(like),
        cost_estimate=costs(1, 1),
    )(after)
    return tuple(arrays)


def on_device(
    decode_states,
    norm_gain,
    decode_routes,
    decode_gates,
    up_weight,
    down_weight,
    traj_inputs,
    traj_cotangents,
    traj_lengths,
    packing,
    learner_routes,
    learner_gates,
):
    experts, parts = lax.axis_size("exp"), lax.axis_size("dp")
    is_rollout = lax.axis_index("sect") == 0
    go = is_rollout.astype(i32).reshape(1)
    me = lax.axis_index("exp")
    part_ref = lax.axis_index("dp").reshape(1).astype(i32)
    up_here, down_here = up_weight[0, 0], down_weight[0, 0]
    hidden_here, features = up_here.shape
    hidden = hidden_here * parts
    steps, row_count, routes_each = decode_routes.shape
    half_steps = steps // 2
    share = features // parts
    blocks = share // lanes
    capacity = 3 * row_count * routes_each // (2 * experts)
    slots = experts * capacity
    stacked = blocks * row_count
    moved = blocks * slots
    tile = hidden_here // 3
    line = 8
    per_half = traj_inputs.shape[1]
    gathered = experts * 2 * per_half
    height = 4 * per_half + note_rows

    routes = jnp.swapaxes(decode_routes, 1, 2).reshape(steps * routes_each, row_count)
    gates = jnp.swapaxes(decode_gates, 1, 2).reshape(steps * routes_each, row_count)
    targets, gates, states, payload, own_rows = pl.pallas_call(
        functools.partial(prepare_kernel, experts, capacity),
        out_shape=[
            jax.ShapeDtypeStruct((steps, routes_each, stacked), i32),
            jax.ShapeDtypeStruct((steps * routes_each, stacked), f32),
            jax.ShapeDtypeStruct((stacked, lanes), f32),
            jax.ShapeDtypeStruct((moved, lanes), bf16),
            jax.ShapeDtypeStruct((2 * per_half, share), bf16),
        ],
        in_specs=[smem] + [stays] * 5,
        out_specs=[vmem] * 4 + [stays],
        scratch_shapes=[
            pltpu.VMEM((row_count, share), bf16),
            pltpu.VMEM((2 * per_half, share), bf16),
            pltpu.VMEM(routes.shape, i32),
            pltpu.VMEM(gates.shape, f32),
            pltpu.SemaphoreType.DMA((6,)),
        ],
        compiler_params=fits(60),
        cost_estimate=costs(1, 1),
    )(part_ref, routes, gates, decode_states, traj_inputs[0], traj_cotangents[0])

    crossed_rows = flipped(own_rows, "sect", 1)
    up_sent, down_sent, _ = lax.optimization_barrier((up_here, down_here, own_rows))
    cut = hidden_here + 2 * tile
    pieces = pl.pallas_call(
        cut_kernel,
        out_shape=[jax.ShapeDtypeStruct((rows, features), bf16) for rows in (cut, tile)],
        in_specs=[smem] + [stays] * 2,
        out_specs=[stays] * 2,
        scratch_shapes=[pltpu.VMEM((2 * hidden_here, features), bf16), pltpu.SemaphoreType.DMA((2, 3))],
        compiler_params=fits(60),
        cost_estimate=costs(1, 1),
    )(go, up_sent, down_sent)
    first_piece, second_piece, crossed_rows = lax.optimization_barrier((*pieces, crossed_rows))
    first_there = lax.ppermute(first_piece, "sect", [(1, 0)])
    second_there = lax.ppermute(second_piece, "sect", [(1, 0)])

    gain = norm_gain.reshape(1, features)
    def expert_forward(arrived, up_mat, down_mat):
        return pl.pallas_call(
            functools.partial(expert_kernel, parts, slots, capacity, features, hidden),
            out_shape=[jax.ShapeDtypeStruct((moved, lanes), bf16)] * parts,
            in_specs=[smem, vmem] + [vmem] * parts + [stays, stays],
            scratch_shapes=[
                pltpu.VMEM((hidden_here, features), bf16),
                pltpu.VMEM((hidden_here, features), bf16),
                pltpu.VMEM((slots, features), bf16),
                pltpu.VMEM((moved, lanes), bf16),
                pltpu.VMEM((moved, moved), bf16),
                pltpu.SemaphoreType.DMA((2,)),
            ],
            compiler_params=fits(48),
            cost_estimate=costs(1, 1),
        )(part_ref, gain, *arrived, up_mat, down_mat)

    def decode_step(step, states, payload, up_mat, down_mat):
        last = step in (half_steps - 1, steps - 1)
        arrived = lax.all_to_all(payload, "exp", split_axis=0, concat_axis=0, tiled=True)
        arrived = [arrived] + [shifted(arrived, "dp", j) for j in range(1, parts)]
        partials = expert_forward(arrived, up_mat, down_mat)
        received = [shifted(partials[j], "dp", j) for j in range(1, parts)]
        summed = sum((r.astype(f32) for r in received), partials[0].astype(f32)).astype(bf16)
        returned = lax.all_to_all(summed, "exp", split_axis=0, concat_axis=0, tiled=True)
        outs = [
            jax.ShapeDtypeStruct((stacked, lanes), f32),
            jax.ShapeDtypeStruct((stacked if last else moved, lanes), bf16),
        ]
        results = pl.pallas_call(
            functools.partial(combine_kernel, step, last),
            out_shape=outs,
            compiler_params=fits(16),
            cost_estimate=costs(1, 1),
        )(targets, gates, states, returned)
        return tuple(results)
    def learner_rows(halves):
        wide = learner_routes.shape[0]
        notes = [learner_routes.T, learner_gates.T, traj_lengths[0], packing]
        unit = pl.pallas_call(
            unit_kernel,
            out_shape=jax.ShapeDtypeStruct((height, share), bf16),
            in_specs=[anywhere] * 2 + [vmem] * 4,
            scratch_shapes=[pltpu.SemaphoreType.DMA((4,))],
            compiler_params=fits(16),
            cost_estimate=costs(1, 1),
        )(*halves, *notes)
        others, group = [0], experts
        while group > line:
            group = group // 2
            unit = jnp.concatenate([unit, flipped(unit, "exp", group)])
            others = others + [o ^ group for o in others]
        far = group // 2
        shifts = sorted(range(1, far), key=lambda s: (min(s, far - s), s))

        def along(array, s):
            pairs = [(i, i // group * group + (i + 2 * s) % group) for i in range(experts)]
            return lax.ppermute(array, "exp", pairs)

        side = flipped(unit, "exp", 1)
        near = [along(unit, s) for s in shifts[:-1]]
        unit, side, *near = lax.optimization_barrier((unit, side, *near))
        last = along(unit, shifts[-1])
        sides = [flipped(n, "exp", 1) for n in near]
        units = [
            jnp.concatenate([unit, side, *near]),
            jnp.concatenate(sides),
            jnp.concatenate([last, flipped(last, "exp", 1)]),
        ]
        places = [(0, 0), (1, 0)] + [(f, s) for f in range(2) for s in shifts[:-1]] + [(f, shifts[-1]) for f in range(2)]
        sources = [(group, flip, 2 * s, o) for flip, s in places for o in others]
        return units, sources

    def with_parts(units, sources):
        units = list(units)
        others = [shifted(u, "dp", j) for j in range(1, parts) for u in units]
        wide = learner_routes.shape[0]
        weights = pl.pallas_call(
            functools.partial(
                weights_kernel, height, 2, learner_routes.shape[1], traj_lengths.shape[2], wide, sources
            ),
            out_shape=jax.ShapeDtypeStruct((1, gathered), f32),
            in_specs=[smem] + [anywhere] * len(units),
            scratch_shapes=[
                pltpu.VMEM((experts, note_rows, wide), bf16),
                pltpu.VMEM((experts, wide), f32),
                pltpu.VMEM((2 * experts, wide), f32),
                pltpu.SemaphoreType.DMA((experts,)),
            ],
            compiler_params=fits(16),
            cost_estimate=costs(1, 1),
        )(me.reshape(1).astype(i32), *units)
        return units + others, weights

    rows_like = jax.ShapeDtypeStruct((gathered, features), bf16)
    weight_like = jax.ShapeDtypeStruct((hidden_here, features), bf16)
    weights_like = jax.ShapeDtypeStruct((1, gathered), f32)

    def sems_of(*shape):
        return pltpu.SemaphoreType.DMA(shape)

    def update_space(rows):
        held = [pltpu.VMEM((gathered, features), bf16)] * 2 + [pltpu.VMEM((rows, features), bf16)] * 4
        return held + [sems_of(2, rows // tile)] * 2

    def update(units, weights, up_mat, down_mat):
        return pl.pallas_call(
            functools.partial(learner_kernel, parts, height, features, hidden, tile),
            out_shape=[weight_like] * 2,
            in_specs=[smem, vmem] + [anywhere] * (len(units) + 2),
            out_specs=[anywhere] * 2,
            scratch_shapes=[sems_of(2 * parts * experts)] + update_space(hidden_here),
            compiler_params=fits(56),
            cost_estimate=costs(1, 1),
        )(part_ref, weights, *units, up_mat, down_mat)

    slopes_like = jax.ShapeDtypeStruct((tile, gathered), f32)
    gradient_like = jax.ShapeDtypeStruct((tile, features), f32)

    def spaces(*like):
        return [pltpu.VMEM(a.shape, a.dtype) for a in like]

    def update_late(new_up, new_down):
        piece_like = jax.ShapeDtypeStruct((tile, features), bf16)
        return pl.pallas_call(
            functools.partial(late_kernel, features, hidden, tile, 2 * tile),
            out_shape=[weight_like] * 2 + [slopes_like, gradient_like],
            in_specs=[smem, vmem] + [stays] * 5,
            out_specs=[anywhere] * 4,
            scratch_shapes=[sems_of(2)]
            + spaces(piece_like, slopes_like, gradient_like)
            + [sems_of(3)]
            + update_space(2 * tile),
            input_output_aliases={5: 0, 6: 1},
            compiler_params=fits(60),
            cost_estimate=costs(1, 1),
        )(go, weights, inputs, grads, first_there, new_up, new_down)

    def update_last(slopes, gradient, new_up, new_down):
        piece_like = jax.ShapeDtypeStruct((tile, features), bf16)
        return pl.pallas_call(
            functools.partial(last_kernel, features, hidden),
            out_shape=[weight_like] * 2,
            in_specs=[smem] + [stays] * 8,
            out_specs=[anywhere] * 2,
            scratch_shapes=spaces(rows_like, rows_like, piece_like, piece_like, slopes_like, gradient_like)
            + spaces(piece_like, piece_like)
            + [sems_of(6), sems_of(2)],
            input_output_aliases={7: 0, 8: 1},
            compiler_params=fits(60),
            cost_estimate=costs(1, 1),
        )(go, inputs, grads, first_there, second_there, slopes, gradient, new_up, new_down)

    half_like = jax.ShapeDtypeStruct((row_count, features // 2), bf16)
    block_rows = height * max(1, experts // line)
    gather_like = [jax.ShapeDtypeStruct((block_rows * n, share), bf16) for n in (line // 2, line // 2 - 2, 2)]

    sources = []

    def first_rollout():
        now, sent = decode_step(0, states, payload, up_here, down_here)
        return (now, sent) + unset(sent, *gather_like)

    def first_learner():
        units, places = learner_rows([crossed_rows, own_rows])
        sources.append(places)
        return (states, payload) + tuple(units)

    states, payload, *rows = lax.cond(is_rollout, first_rollout, first_learner)

    def second_rollout():
        now, sent = states, payload
        for step in range(1, half_steps):
            now, sent = decode_step(step, now, sent, up_here, down_here)
        return (now,) + unset(now, up_here, down_here)

    def second_learner():
        units, weights = with_parts(rows, sources[0])
        return (states,) + tuple(update(units, weights, up_here, down_here))

    states, new_up, new_down = lax.cond(is_rollout, second_rollout, second_learner)
    states_there = lax.ppermute(states, "sect", [(0, 1)])

    held_up = pl.pallas_call(
        hold_kernel,
        out_shape=weight_like,
        in_specs=[smem, stays],
        out_specs=vmem,
        scratch_shapes=[pltpu.SemaphoreType.DMA],
        compiler_params=fits(16),
        cost_estimate=costs(1, 1),
    )(go, new_up)

    def third_rollout():
        return (states, payload) + tuple(learner_rows([own_rows, crossed_rows])[0])

    def third_learner():
        sent = pl.pallas_call(
            functools.partial(dispatch_kernel, half_steps),
            out_shape=jax.ShapeDtypeStruct((moved, lanes), bf16),
            compiler_params=fits(16),
            cost_estimate=costs(1, 1),
        )(targets, states_there)
        now, sent = decode_step(half_steps, states_there, sent, held_up, new_down)
        return (now, sent) + unset(sent, *gather_like)

    states, payload, *rows = lax.cond(is_rollout, third_rollout, third_learner)

    def fourth_rollout():
        units, weights = with_parts(rows, sources[0])
        whole = pl.pallas_call(
            functools.partial(assemble_kernel, parts, height),
            out_shape=[rows_like] * 2,
            in_specs=[smem] + [anywhere] * len(units),
            scratch_shapes=[sems_of(2 * parts * experts)],
            compiler_params=fits(62),
            cost_estimate=costs(1, 1),
        )(part_ref, *units)
        return unset(weights, half_like, half_like) + tuple(whole) + (weights,)

    def fourth_learner():
        now, sent = states, payload
        for step in range(half_steps + 1, steps):
            now, sent = decode_step(step, now, sent, held_up, new_down)
        pieces = [sent] + [shifted(sent, "dp", j) for j in range(1, parts)]
        left, right = pl.pallas_call(
            functools.partial(join_kernel, parts, row_count),
            out_shape=[half_like] * 2,
            in_specs=[smem] + [vmem] * parts,
            scratch_shapes=[pltpu.VMEM((row_count, features), bf16)],
            cost_estimate=costs(1, 1),
        )(part_ref, *pieces)
        return (left, right) + unset(left, rows_like, rows_like, weights_like)

    left, right, inputs, grads, weights = lax.cond(is_rollout, fourth_rollout, fourth_learner)

    new_up, new_down, slopes, gradient = update_late(new_up, new_down)
    delivered = lax.ppermute(left, "sect", [(1, 0)])
    new_up, new_down = update_last(slopes, gradient, new_up, new_down)
    right, new_up = lax.optimization_barrier((right, new_up))
    final_states = jnp.where(is_rollout, delivered, right)
    return final_states, new_up[None, None], new_down[None, None]


def solution(mesh):
    in_specs = (
        P("exp", None),
        P(),
        P(None, "exp", None),
        P(None, "exp", None),
        P("sect", "exp", "dp", None),
        P("sect", "exp", "dp", None),
        P("sect", "exp", None),
        P("sect", "exp", None),
        P("exp", None, None),
        P("exp", None),
        P("exp", None),
        P("exp", None),
    )
    out_specs = (P("exp", "sect"), P("sect", "exp", "dp", None), P("sect", "exp", "dp", None))
    return jax.shard_map(on_device, mesh=mesh, in_specs=in_specs, out_specs=out_specs, check_vma=False)
```

```python
import functools

import jax
import jax.numpy as jnp
from jax import lax
from jax.experimental import pallas as pl
from jax.experimental.pallas import tpu as pltpu
from jax.sharding import PartitionSpec as P

step_size = 3.0
norm_eps = 1e-06
lanes = 256
note_rows = 16
f32, bf16, i32 = jnp.float32, jnp.bfloat16, jnp.int32
nt_dims = (((1,), (1,)), ((), ()))
tn_dims = (((0,), (0,)), ((), ()))
smem = pl.BlockSpec(memory_space=pltpu.SMEM)
vmem = pl.BlockSpec(memory_space=pltpu.VMEM)
anywhere = pl.BlockSpec(memory_space=pl.ANY)
stays = pl.BlockSpec(memory_space=pltpu.HBM)


def shifted(array, axis, by):
    size = lax.axis_size(axis)
    return lax.ppermute(array, axis, [(i, (i + by) % size) for i in range(size)])


def flipped(array, axis, bit):
    return lax.ppermute(array, axis, [(i, i ^ bit) for i in range(lax.axis_size(axis))])


def fits(megabytes):
    return pltpu.CompilerParams(vmem_limit_bytes=megabytes * 1024 * 1024)


def costs(flops, moved):
    return pl.CostEstimate(flops=flops, bytes_accessed=moved, transcendentals=0)


def dot(a, b, dims=(((1,), (0,)), ((), ())), precision=None):
    return lax.dot_general(a, b, dims, precision=precision, preferred_element_type=f32)


def one_hot(rows, targets_ref):
    ids = lax.broadcasted_iota(i32, (rows, targets_ref.shape[1]), 0)
    hits = [jnp.where(ids == targets_ref[k : k + 1, :], 1.0, 0.0) for k in range(targets_ref.shape[0])]
    return sum(hits[1:], hits[0]).astype(bf16)


def prepare_kernel(
    experts, capacity, part_ref, all_routes_ref, all_gates_ref, all_rows_ref, inputs_ref, grads_ref,
    targets_ref, tiled_ref, states_ref, payload_ref, sent_ref, rows_ref, own_ref, routes_ref, gates_ref, sems,
):
    row_count, share = rows_ref.shape
    steps, routes_each = targets_ref.shape[:2]
    stacked, width = states_ref.shape
    blocks = stacked // row_count
    own = pl.ds(pl.multiple_of(part_ref[0] * share, share), share)
    held = inputs_ref.shape[0]
    row_copy = pltpu.make_async_copy(all_rows_ref.at[:, own], rows_ref, sems.at[0])
    copies = [
        pltpu.make_async_copy(inputs_ref.at[:, own], own_ref.at[pl.ds(0, held)], sems.at[1]),
        pltpu.make_async_copy(grads_ref.at[:, own], own_ref.at[pl.ds(held, held)], sems.at[2]),
    ]
    table_copies = [
        pltpu.make_async_copy(all_routes_ref, routes_ref, sems.at[3]),
        pltpu.make_async_copy(all_gates_ref, gates_ref, sems.at[4]),
    ]
    out_copy = pltpu.make_async_copy(own_ref, sent_ref, sems.at[5])
    for copy in table_copies + copies + [row_copy]:
        copy.start()
    before = lax.broadcasted_iota(i32, (row_count, stacked), 0)
    after = lax.rem(lax.broadcasted_iota(i32, (row_count, stacked), 1), row_count)
    repeat = jnp.where(before == after, 1.0, 0.0)
    earlier = jnp.where(before < after, 1.0, 0.0).astype(bf16)
    every = jnp.ones((row_count, stacked), bf16)
    block_of = lax.div(lax.broadcasted_iota(i32, (1, stacked), 1), row_count)
    expert_ids = lax.broadcasted_iota(i32, (experts, row_count), 0)
    tall_ids = lax.broadcasted_iota(i32, (experts, stacked), 0)
    for copy in table_copies + copies:
        copy.wait()
    out_copy.start()
    routes = dot(routes_ref[...].astype(f32), repeat, precision=lax.Precision.HIGHEST)
    routes = (routes + 0.5).astype(i32)
    tiled_ref[...] = dot(gates_ref[...], repeat, precision=lax.Precision.HIGHEST)
    for step in range(steps):
        seen = jnp.zeros((experts, stacked), f32)
        for k in range(routes_each):
            at = step * routes_each + k
            member = jnp.where(expert_ids == routes_ref[at : at + 1, :], 1.0, 0.0).astype(bf16)
            route = routes[at : at + 1, :]
            ahead = dot(member, earlier) + seen
            rank = jnp.sum(jnp.where(tall_ids == route, ahead, 0.0), axis=0, keepdims=True)
            seen = seen + dot(member, every)
            place = (route * blocks + block_of) * capacity + (rank + 0.5).astype(i32)
            targets_ref[step, k : k + 1, :] = place
    row_copy.wait()
    for block in range(blocks):
        columns = slice(block * width, (block + 1) * width)
        states_ref[block * row_count : (block + 1) * row_count, :] = rows_ref[:, columns].astype(f32)
    payload_ref[...] = dot(one_hot(payload_ref.shape[0], targets_ref.at[0]), states_ref[...].astype(bf16)).astype(bf16)
    out_copy.wait()


def dispatch_kernel(step, targets_ref, states_ref, payload_ref):
    payload_ref[...] = dot(one_hot(payload_ref.shape[0], targets_ref.at[step]), states_ref[...].astype(bf16)).astype(bf16)


def combine_kernel(step, last, targets_ref, gates_ref, states_ref, returned_ref, new_ref, payload_ref):
    ids = lax.broadcasted_iota(i32, (returned_ref.shape[0], states_ref.shape[0]), 0)
    weights = jnp.zeros(ids.shape, f32)
    routes_each = targets_ref.shape[1]
    for k in range(routes_each):
        at = step * routes_each + k
        weights = weights + jnp.where(ids == targets_ref[step, k : k + 1, :], gates_ref[at : at + 1, :], 0.0)
    high = weights.astype(bf16)
    low = (weights - high.astype(f32)).astype(bf16)
    returned = returned_ref[...]
    states = states_ref[...] + (dot(high, returned, tn_dims) + dot(low, returned, tn_dims))
    new_ref[...] = states
    if last:
        payload_ref[...] = states.astype(bf16)
    else:
        payload_ref[...] = dot(one_hot(returned.shape[0], targets_ref.at[step + 1]), states.astype(bf16)).astype(bf16)


def expert_kernel(parts, slots, capacity, features, hidden, part_ref, gain_ref, *refs):
    arrived, (up_ref, down_ref) = refs[:parts], refs[parts : parts + 2]
    outs = refs[parts + 2 : 2 * parts + 2]
    up_held, down_held, normed_ref, stack_ref, order_ref, sems = refs[2 * parts + 2 :]
    width = arrived[0].shape[1]
    blocks = features // (parts * width)
    me = part_ref[0]
    up_copy = pltpu.make_async_copy(up_ref, up_held, sems.at[0])
    down_copy = pltpu.make_async_copy(down_ref, down_held, sems.at[1])
    up_copy.start()
    down_copy.start()
    moved = blocks * slots
    column = lax.broadcasted_iota(i32, (1, moved), 1)
    slot = lax.rem(column, slots)
    target = (lax.div(slot, capacity) * blocks + lax.div(column, slots)) * capacity + lax.rem(slot, capacity)
    hits = lax.broadcasted_iota(i32, (moved, moved), 0) == target
    order_ref[...] = jnp.where(hits, 1.0, 0.0).astype(bf16)
    square = jnp.zeros((slots, 1), f32)
    stacks = []
    for ref in arrived:
        stack = dot(order_ref[...], ref[...], tn_dims)
        stacks.append(stack)
        for block in range(blocks):
            rows = stack[block * slots : (block + 1) * slots]
            square = square + jnp.sum(rows * rows, axis=1, keepdims=True)
    scale = lax.rsqrt(square * (1.0 / features) + norm_eps)
    for j, stack in enumerate(stacks):
        start = lax.rem(me + parts - j, parts) * (blocks * width)
        for block in range(blocks):
            rows = stack[block * slots : (block + 1) * slots]
            columns = pl.ds(pl.multiple_of(start + block * width, width), width)
            normed_ref[:, columns] = (rows * scale * gain_ref[:, columns]).astype(bf16)
    up_copy.wait()
    before_act = dot(normed_ref[...], up_held[...], nt_dims) * features ** (-0.5)
    activated = (before_act / (1.0 + jnp.exp(-before_act))).astype(bf16)
    down_copy.wait()
    normed_ref[...] = (dot(activated, down_held[...]) * hidden ** (-0.5)).astype(bf16)
    for j, out_ref in enumerate(outs):
        start = lax.rem(me + j, parts) * (blocks * width)
        for block in range(blocks):
            columns = pl.ds(pl.multiple_of(start + block * width, width), width)
            stack_ref[block * slots : (block + 1) * slots, :] = normed_ref[:, columns]
        out_ref[...] = dot(order_ref[...], stack_ref[...]).astype(bf16)


def gathered_copies(part, parts, height, units, inputs_ref, grads_ref, sems):
    per_part = len(units) // parts
    width = units[0].shape[1]
    rows = (height - note_rows) // 2
    in_copies, grad_copies = [], []
    for j in range(parts):
        columns = pl.ds(pl.multiple_of(lax.rem(part + parts - j, parts) * width, width), width)
        blocks = [(u, at) for u in units[j * per_part : (j + 1) * per_part] for at in range(0, u.shape[0], height)]
        for i, (unit, at) in enumerate(blocks):
            place, sem = pl.ds(i * rows, rows), 2 * (j * len(blocks) + i)
            source = unit.at[pl.ds(at, rows)]
            in_copies.append(pltpu.make_async_copy(source, inputs_ref.at[place, columns], sems.at[sem]))
            source = unit.at[pl.ds(at + rows, rows)]
            grad_copies.append(pltpu.make_async_copy(source, grads_ref.at[place, columns], sems.at[sem + 1]))
    return in_copies, grad_copies


def unit_kernel(first_ref, second_ref, routes_ref, gates_ref, lengths_ref, shards_ref, unit_ref, sems):
    held = first_ref.shape[0] // 2
    copies = []
    for i, ref in enumerate((first_ref, second_ref)):
        for j in range(2):
            place = pl.ds((2 * j + i) * held, held)
            source = ref.at[pl.ds(j * held, held)]
            copies.append(pltpu.make_async_copy(source, unit_ref.at[place], sems.at[2 * i + j]))
    for copy in copies:
        copy.start()
    wide = routes_ref.shape[1]

    def widened(ref):
        count = ref.shape[1]
        places = lax.broadcasted_iota(i32, (count, wide), 0) == lax.broadcasted_iota(i32, (count, wide), 1)
        return dot(ref[...].astype(f32), jnp.where(places, 1.0, 0.0))

    gates = gates_ref[...]
    terms = []
    for _ in range(3):
        terms.append(gates.astype(bf16).astype(f32))
        gates = gates - terms[-1]
    tables = [routes_ref[...].astype(f32)] + terms + [widened(lengths_ref), widened(shards_ref)]
    ids = lax.broadcasted_iota(i32, (note_rows, wide), 0)
    notes, at = jnp.zeros((note_rows, wide), f32), 0
    for table in tables:
        for row in range(table.shape[0]):
            notes = notes + jnp.where(ids == at, table[row : row + 1, :], 0.0)
            at += 1
    base = 4 * held
    unit_ref[base:, :] = jnp.zeros((note_rows, unit_ref.shape[1]), bf16)
    unit_ref[base:, :wide] = notes.astype(bf16)
    for copy in copies:
        copy.wait()


def weights_kernel(height, halves, each, trajs, wide, sources, me_ref, *refs):
    units, (weights_ref, notes_ref, table_ref, facts_ref, sems) = refs[:-5], refs[-5:]
    blocks = [(u, at) for u in units for at in range(0, u.shape[0], height)]
    count = len(blocks)
    per_half = (height - note_rows) // (2 * halves)
    longest = wide // count
    total = weights_ref.shape[1]
    copies = []
    for i, (unit, at) in enumerate(blocks):
        source = unit.at[pl.ds(at + height - note_rows, note_rows), pl.ds(0, wide)]
        copies.append(pltpu.make_async_copy(source, notes_ref.at[i], sems.at[i]))
    for copy in copies:
        copy.start()
    for copy in copies:
        copy.wait()
    me = me_ref[0]
    ids = lax.broadcasted_iota(i32, (count, 1), 0)
    places = lax.broadcasted_iota(i32, (note_rows, wide), 1)
    holder_of = jnp.zeros((count, 1), f32)
    for i, (group, flip, far, near) in enumerate(sources):
        place = lax.rem((lax.rem(me, group) ^ flip) + group - far, group)
        holder = ((lax.div(me, group) * group + place) ^ near).astype(f32)
        holder_of = holder_of + jnp.where(ids == i, holder, 0.0)
        notes = notes_ref[i].astype(f32)
        row = jnp.zeros((1, wide), f32)
        for k in range(each):
            gate = sum(notes[(1 + t) * each + k : (1 + t) * each + k + 1, :] for t in range(3))
            row = row + jnp.where(notes[k : k + 1, :] == me.astype(f32), gate, 0.0)
        table_ref[i : i + 1, :] = row
        for half in range(halves):
            shards = pltpu.roll(notes, (trajs - half * trajs) % wide, 1) if half != 1 else notes
            shards = jnp.where((places >= trajs) & (places < 2 * trajs), shards, 0.0)
            shards = jnp.where(places == 2 * trajs, holder, shards)
            facts = notes[4 * each + half : 4 * each + half + 1, :] + shards[4 * each + halves : 4 * each + halves + 1, :]
            facts_ref[i * halves + half : i * halves + half + 1, :] = facts
    facts = facts_ref[...]
    down, across = [lax.broadcasted_iota(i32, (wide, wide), d) for d in (0, 1)]
    starts = dot(facts, jnp.where((down < across) & (down < trajs), 1.0, 0.0))
    row_ids = lax.broadcasted_iota(i32, (count * halves, total), 1)
    of_row = lax.div(row_ids, per_half) == lax.broadcasted_iota(i32, (count * halves, total), 0)
    of_row = jnp.where(of_row, 1.0, 0.0)
    facts, starts = dot(facts, of_row, tn_dims), dot(starts, of_row, tn_dims)[:trajs]
    place = lax.rem(lax.broadcasted_iota(i32, (1, total), 1), per_half).astype(f32)
    inside = (place >= starts) & (place < starts + facts[:trajs])
    offset = jnp.sum(jnp.where(inside, place - starts, 0.0), axis=0, keepdims=True)
    shard = jnp.sum(jnp.where(inside, facts[trajs : 2 * trajs], 0.0), axis=0, keepdims=True)
    slot = (facts[2 * trajs : 2 * trajs + 1] * longest + offset + 0.5).astype(i32)
    chosen = jnp.where(lax.broadcasted_iota(i32, (wide, total), 0) == slot, 1.0, 0.0)
    gates = dot(table_ref[...], chosen, precision=lax.Precision.HIGHEST)
    weights_ref[...] = jnp.sum(jnp.where(holder_of == shard, gates, 0.0), axis=0, keepdims=True)


def tile_copies(ref, held, tile, sems):
    places = [pl.ds(start, tile) for start in range(0, ref.shape[0], tile)]
    return [pltpu.make_async_copy(ref.at[p], held.at[p], sems.at[i]) for i, p in enumerate(places)]


def start_all(*groups):
    for copies in groups:
        for copy in copies:
            copy.start()


def wait_all(copies):
    for copy in copies:
        copy.wait()


def activation(features, up_tile, inputs, weight):
    before_act = dot(up_tile, inputs, nt_dims) * features ** (-0.5)
    sigmoid = 1.0 / (1.0 + jnp.exp(-before_act))
    return (before_act * sigmoid * weight).astype(bf16), sigmoid * (1.0 + before_act * (1.0 - sigmoid)) * weight


def new_tile(old, step, change, rows):
    return (old.astype(f32) - (step_size * step) * dot(change, rows)).astype(bf16)


def cut_kernel(go_ref, up_ref, down_ref, first_ref, second_ref, held, sems):
    rows, most = up_ref.shape[0], first_ref.shape[0]

    @pl.when(go_ref[0] == 0)
    def _():
        moves = [
            (up_ref, pl.ds(0, rows), first_ref.at[pl.ds(0, rows)]),
            (down_ref.at[pl.ds(0, most - rows)], pl.ds(rows, most - rows), first_ref.at[pl.ds(rows, most - rows)]),
            (down_ref.at[pl.ds(most - rows, 2 * rows - most)], pl.ds(most, 2 * rows - most), second_ref),
        ]
        ins = [pltpu.make_async_copy(a, held.at[p], sems.at[0, i]) for i, (a, p, _) in enumerate(moves)]
        outs = [pltpu.make_async_copy(held.at[p], b, sems.at[1, i]) for i, (_, p, b) in enumerate(moves)]
        start_all(ins)
        for copy, out in zip(ins, outs):
            copy.wait()
            out.start()
        wait_all(outs)


def update_rows(features, hidden, tile, weight, in_copies, grad_copies, up_from, down_from, up_to, down_to, space):
    inputs, grads, up, down, new_up, new_down, sems, out_sems = space
    up_copies = tile_copies(up_from, up, tile, sems.at[0])
    down_copies = tile_copies(down_from, down, tile, sems.at[1])
    up_outs = tile_copies(new_up, up_to, tile, out_sems.at[0])
    down_outs = tile_copies(new_down, down_to, tile, out_sems.at[1])
    start_all(up_copies[:1], in_copies, down_copies[:1], grad_copies, up_copies[1:], down_copies[1:])
    for i in range(len(up_copies)):
        here = pl.ds(i * tile, tile)
        up_copies[i].wait()
        if i == 0:
            wait_all(in_copies)
        activated, slope = activation(features, up[here, :], inputs[...], weight)
        down_copies[i].wait()
        if i == 0:
            wait_all(grad_copies)
        pre_grad = (dot(down[here, :], grads[...], nt_dims) * hidden ** (-0.5) * slope).astype(bf16)
        new_down[here, :] = new_tile(down[here, :], hidden ** (-0.5), activated, grads[...])
        down_outs[i].start()
        new_up[here, :] = new_tile(up[here, :], features ** (-0.5), pre_grad, inputs[...])
        up_outs[i].start()
    wait_all(up_outs + down_outs)


def learner_kernel(parts, height, features, hidden, tile, part_ref, weight_ref, *refs):
    units, (up_ref, down_ref, new_up_ref, new_down_ref), row_sems, space = refs[:-13], refs[-13:-9], refs[-9], refs[-8:]
    copies = gathered_copies(part_ref[0], parts, height, units, space[0], space[1], row_sems)
    rows = (up_ref, down_ref, new_up_ref, new_down_ref)
    update_rows(features, hidden, tile, weight_ref[...], *copies, *rows, space)


def assemble_kernel(parts, height, part_ref, *refs):
    units, (inputs_ref, grads_ref, sems) = refs[:-3], refs[-3:]
    in_copies, grad_copies = gathered_copies(part_ref[0], parts, height, units, inputs_ref, grads_ref, sems)
    start_all(in_copies, grad_copies)
    wait_all(in_copies + grad_copies)


def late_kernel(features, hidden, tile, count, go_ref, weight_ref, *refs):
    inputs_ref, grads_ref, piece_ref, _, _, new_up_ref, new_down_ref, slopes_ref, gradient_ref = refs[:9]
    row_sems, ahead, slopes, gradient, ahead_sems, *space = refs[9:]
    hidden_here = new_up_ref.shape[0]

    @pl.when(go_ref[0] == 1)
    def _():
        ahead_copy = pltpu.make_async_copy(piece_ref.at[pl.ds(count, tile)], ahead, ahead_sems.at[0])
        in_copies = [pltpu.make_async_copy(inputs_ref, space[0], row_sems.at[0])]
        grad_copies = [pltpu.make_async_copy(grads_ref, space[1], row_sems.at[1])]
        rows = [piece_ref.at[pl.ds(start, count)] for start in (0, hidden_here)]
        rows = rows + [ref.at[pl.ds(0, count)] for ref in (new_up_ref, new_down_ref)]
        ahead_copy.start()
        update_rows(features, hidden, tile, weight_ref[...], in_copies, grad_copies, *rows, space)
        ahead_copy.wait()
        activated, slopes[...] = activation(features, ahead[...], space[0][...], weight_ref[...])
        gradient[...] = dot(activated, space[1][...])
        outs = [
            pltpu.make_async_copy(slopes, slopes_ref, ahead_sems.at[1]),
            pltpu.make_async_copy(gradient, gradient_ref, ahead_sems.at[2]),
        ]
        start_all(outs)
        wait_all(outs)


def last_kernel(features, hidden, go_ref, *refs):
    inputs_ref, grads_ref, first_ref, down_ref, slopes_ref, gradient_ref, _, _, new_up_ref, new_down_ref = refs[:10]
    inputs, grads, up, down, slopes, gradient, new_up, new_down, sems, out_sems = refs[10:]
    tile = down_ref.shape[0]
    place = pl.ds(new_up_ref.shape[0] - tile, tile)

    @pl.when(go_ref[0] == 1)
    def _():
        sides = [pl.ds(start, features // 2) for start in (0, features // 2)]
        moves = [(ref.at[:, c], held.at[:, c]) for c in sides for ref, held in ((down_ref, down), (grads_ref, grads))]
        moves = moves + [(slopes_ref, slopes)]
        for c in sides:
            moves = moves + [(inputs_ref.at[:, c], inputs.at[:, c]), (first_ref.at[place, c], up.at[:, c])]
        moves = moves + [(gradient_ref, gradient)]
        copies = [pltpu.make_async_copy(a, b, sems.at[i]) for i, (a, b) in enumerate(moves)]
        outs = [pltpu.make_async_copy(new_up.at[:, c], new_up_ref.at[place, c], out_sems.at[i]) for i, c in enumerate(sides)]
        outs = outs + [pltpu.make_async_copy(new_down, new_down_ref.at[place], out_sems.at[2])]
        start_all(copies)
        hidden_grad = jnp.zeros((tile, grads.shape[0]), f32)
        for i, c in enumerate(sides):
            wait_all(copies[2 * i : 2 * i + 2])
            hidden_grad = hidden_grad + dot(down[:, c], grads[:, c], nt_dims)
        copies[4].wait()
        pre_grad = (hidden_grad * hidden ** (-0.5) * slopes[...]).astype(bf16)
        for i, c in enumerate(sides):
            wait_all(copies[2 * i + 5 : 2 * i + 7])
            new_up[:, c] = new_tile(up[:, c], features ** (-0.5), pre_grad, inputs[:, c])
            outs[i].start()
        copies[9].wait()
        new_down[...] = (down[...].astype(f32) - (step_size * hidden ** (-0.5)) * gradient[...]).astype(bf16)
        outs[2].start()
        wait_all(outs)


def hold_kernel(go_ref, array_ref, held_ref, sem):
    @pl.when(go_ref[0] == 0)
    def _():
        copy = pltpu.make_async_copy(array_ref, held_ref, sem)
        copy.start()
        copy.wait()


def join_kernel(parts, row_count, part_ref, *refs):
    pieces, (left_ref, right_ref, joined_ref) = refs[:parts], refs[parts:]
    width = pieces[0].shape[1]
    blocks = pieces[0].shape[0] // row_count
    for j, piece in enumerate(pieces):
        start = lax.rem(part_ref[0] + parts - j, parts) * (blocks * width)
        for block in range(blocks):
            columns = pl.ds(pl.multiple_of(start + block * width, width), width)
            joined_ref[:, columns] = piece[block * row_count : (block + 1) * row_count, :]
    half = left_ref.shape[1]
    left_ref[...] = joined_ref[:, :half]
    right_ref[...] = joined_ref[:, half:]


def unset_kernel(*refs):
    pass


def unset(after, *like):
    arrays = pl.pallas_call(
        unset_kernel,
        out_shape=[jax.ShapeDtypeStruct(a.shape, a.dtype) for a in like],
        in_specs=[anywhere],
        out_specs=[anywhere] * len(like),
        cost_estimate=costs(1, 1),
    )(after)
    return tuple(arrays)


def on_device(
    decode_states,
    norm_gain,
    decode_routes,
    decode_gates,
    up_weight,
    down_weight,
    traj_inputs,
    traj_cotangents,
    traj_lengths,
    packing,
    learner_routes,
    learner_gates,
):
    experts, parts = lax.axis_size("exp"), lax.axis_size("dp")
    is_rollout = lax.axis_index("sect") == 0
    go = is_rollout.astype(i32).reshape(1)
    me = lax.axis_index("exp")
    part_ref = lax.axis_index("dp").reshape(1).astype(i32)
    up_here, down_here = up_weight[0, 0], down_weight[0, 0]
    hidden_here, features = up_here.shape
    hidden = hidden_here * parts
    steps, row_count, routes_each = decode_routes.shape
    half_steps = steps // 2
    share = features // parts
    blocks = share // lanes
    capacity = 3 * row_count * routes_each // (2 * experts)
    slots = experts * capacity
    stacked = blocks * row_count
    moved = blocks * slots
    tile = hidden_here // 3
    line = 8
    per_half = traj_inputs.shape[1]
    gathered = experts * 2 * per_half
    height = 4 * per_half + note_rows

    routes = jnp.swapaxes(decode_routes, 1, 2).reshape(steps * routes_each, row_count)
    gates = jnp.swapaxes(decode_gates, 1, 2).reshape(steps * routes_each, row_count)
    targets, gates, states, payload, own_rows = pl.pallas_call(
        functools.partial(prepare_kernel, experts, capacity),
        out_shape=[
            jax.ShapeDtypeStruct((steps, routes_each, stacked), i32),
            jax.ShapeDtypeStruct((steps * routes_each, stacked), f32),
            jax.ShapeDtypeStruct((stacked, lanes), f32),
            jax.ShapeDtypeStruct((moved, lanes), bf16),
            jax.ShapeDtypeStruct((2 * per_half, share), bf16),
        ],
        in_specs=[smem] + [stays] * 5,
        out_specs=[vmem] * 4 + [stays],
        scratch_shapes=[
            pltpu.VMEM((row_count, share), bf16),
            pltpu.VMEM((2 * per_half, share), bf16),
            pltpu.VMEM(routes.shape, i32),
            pltpu.VMEM(gates.shape, f32),
            pltpu.SemaphoreType.DMA((6,)),
        ],
        compiler_params=fits(60),
        cost_estimate=costs(1, 1),
    )(part_ref, routes, gates, decode_states, traj_inputs[0], traj_cotangents[0])

    crossed_rows = flipped(own_rows, "sect", 1)
    up_sent, down_sent, _ = lax.optimization_barrier((up_here, down_here, own_rows))
    cut = hidden_here + 2 * tile
    pieces = pl.pallas_call(
        cut_kernel,
        out_shape=[jax.ShapeDtypeStruct((rows, features), bf16) for rows in (cut, tile)],
        in_specs=[smem] + [stays] * 2,
        out_specs=[stays] * 2,
        scratch_shapes=[pltpu.VMEM((2 * hidden_here, features), bf16), pltpu.SemaphoreType.DMA((2, 3))],
        compiler_params=fits(60),
        cost_estimate=costs(1, 1),
    )(go, up_sent, down_sent)
    first_piece, second_piece, crossed_rows = lax.optimization_barrier((*pieces, crossed_rows))
    first_there = lax.ppermute(first_piece, "sect", [(1, 0)])
    second_there = lax.ppermute(second_piece, "sect", [(1, 0)])

    gain = norm_gain.reshape(1, features)
    def expert_forward(arrived, up_mat, down_mat):
        return pl.pallas_call(
            functools.partial(expert_kernel, parts, slots, capacity, features, hidden),
            out_shape=[jax.ShapeDtypeStruct((moved, lanes), bf16)] * parts,
            in_specs=[smem, vmem] + [vmem] * parts + [stays, stays],
            scratch_shapes=[
                pltpu.VMEM((hidden_here, features), bf16),
                pltpu.VMEM((hidden_here, features), bf16),
                pltpu.VMEM((slots, features), bf16),
                pltpu.VMEM((moved, lanes), bf16),
                pltpu.VMEM((moved, moved), bf16),
                pltpu.SemaphoreType.DMA((2,)),
            ],
            compiler_params=fits(48),
            cost_estimate=costs(1, 1),
        )(part_ref, gain, *arrived, up_mat, down_mat)

    def decode_step(step, states, payload, up_mat, down_mat):
        last = step in (half_steps - 1, steps - 1)
        arrived = lax.all_to_all(payload, "exp", split_axis=0, concat_axis=0, tiled=True)
        arrived = [arrived] + [shifted(arrived, "dp", j) for j in range(1, parts)]
        partials = expert_forward(arrived, up_mat, down_mat)
        received = [shifted(partials[j], "dp", j) for j in range(1, parts)]
        summed = sum((r.astype(f32) for r in received), partials[0].astype(f32)).astype(bf16)
        returned = lax.all_to_all(summed, "exp", split_axis=0, concat_axis=0, tiled=True)
        outs = [
            jax.ShapeDtypeStruct((stacked, lanes), f32),
            jax.ShapeDtypeStruct((stacked if last else moved, lanes), bf16),
        ]
        results = pl.pallas_call(
            functools.partial(combine_kernel, step, last),
            out_shape=outs,
            compiler_params=fits(16),
            cost_estimate=costs(1, 1),
        )(targets, gates, states, returned)
        return tuple(results)
    def learner_rows(halves):
        wide = learner_routes.shape[0]
        notes = [learner_routes.T, learner_gates.T, traj_lengths[0], packing]
        unit = pl.pallas_call(
            unit_kernel,
            out_shape=jax.ShapeDtypeStruct((height, share), bf16),
            in_specs=[anywhere] * 2 + [vmem] * 4,
            scratch_shapes=[pltpu.SemaphoreType.DMA((4,))],
            compiler_params=fits(16),
            cost_estimate=costs(1, 1),
        )(*halves, *notes)
        others, group = [0], experts
        while group > line:
            group = group // 2
            unit = jnp.concatenate([unit, flipped(unit, "exp", group)])
            others = others + [o ^ group for o in others]
        far = group // 2
        shifts = sorted(range(1, far), key=lambda s: (min(s, far - s), s))

        def along(array, s):
            pairs = [(i, i // group * group + (i + 2 * s) % group) for i in range(experts)]
            return lax.ppermute(array, "exp", pairs)

        side = flipped(unit, "exp", 1)
        near = [along(unit, s) for s in shifts[:-1]]
        unit, side, *near = lax.optimization_barrier((unit, side, *near))
        last = along(unit, shifts[-1])
        sides = [flipped(n, "exp", 1) for n in near]
        units = [
            jnp.concatenate([unit, side, *near]),
            jnp.concatenate(sides),
            jnp.concatenate([last, flipped(last, "exp", 1)]),
        ]
        places = [(0, 0), (1, 0)] + [(f, s) for f in range(2) for s in shifts[:-1]] + [(f, shifts[-1]) for f in range(2)]
        sources = [(group, flip, 2 * s, o) for flip, s in places for o in others]
        return units, sources

    def with_parts(units, sources):
        units = list(units)
        others = [shifted(u, "dp", j) for j in range(1, parts) for u in units]
        wide = learner_routes.shape[0]
        weights = pl.pallas_call(
            functools.partial(
                weights_kernel, height, 2, learner_routes.shape[1], traj_lengths.shape[2], wide, sources
            ),
            out_shape=jax.ShapeDtypeStruct((1, gathered), f32),
            in_specs=[smem] + [anywhere] * len(units),
            scratch_shapes=[
                pltpu.VMEM((experts, note_rows, wide), bf16),
                pltpu.VMEM((experts, wide), f32),
                pltpu.VMEM((2 * experts, wide), f32),
                pltpu.SemaphoreType.DMA((experts,)),
            ],
            compiler_params=fits(16),
            cost_estimate=costs(1, 1),
        )(me.reshape(1).astype(i32), *units)
        return units + others, weights

    rows_like = jax.ShapeDtypeStruct((gathered, features), bf16)
    weight_like = jax.ShapeDtypeStruct((hidden_here, features), bf16)
    weights_like = jax.ShapeDtypeStruct((1, gathered), f32)

    def sems_of(*shape):
        return pltpu.SemaphoreType.DMA(shape)

    def update_space(rows):
        held = [pltpu.VMEM((gathered, features), bf16)] * 2 + [pltpu.VMEM((rows, features), bf16)] * 4
        return held + [sems_of(2, rows // tile)] * 2

    def update(units, weights, up_mat, down_mat):
        return pl.pallas_call(
            functools.partial(learner_kernel, parts, height, features, hidden, tile),
            out_shape=[weight_like] * 2,
            in_specs=[smem, vmem] + [anywhere] * (len(units) + 2),
            out_specs=[anywhere] * 2,
            scratch_shapes=[sems_of(2 * parts * experts)] + update_space(hidden_here),
            compiler_params=fits(56),
            cost_estimate=costs(1, 1),
        )(part_ref, weights, *units, up_mat, down_mat)

    slopes_like = jax.ShapeDtypeStruct((tile, gathered), f32)
    gradient_like = jax.ShapeDtypeStruct((tile, features), f32)

    def spaces(*like):
        return [pltpu.VMEM(a.shape, a.dtype) for a in like]

    def update_late(new_up, new_down):
        piece_like = jax.ShapeDtypeStruct((tile, features), bf16)
        return pl.pallas_call(
            functools.partial(late_kernel, features, hidden, tile, 2 * tile),
            out_shape=[weight_like] * 2 + [slopes_like, gradient_like],
            in_specs=[smem, vmem] + [stays] * 5,
            out_specs=[anywhere] * 4,
            scratch_shapes=[sems_of(2)]
            + spaces(piece_like, slopes_like, gradient_like)
            + [sems_of(3)]
            + update_space(2 * tile),
            input_output_aliases={5: 0, 6: 1},
            compiler_params=fits(60),
            cost_estimate=costs(1, 1),
        )(go, weights, inputs, grads, first_there, new_up, new_down)

    def update_last(slopes, gradient, new_up, new_down):
        piece_like = jax.ShapeDtypeStruct((tile, features), bf16)
        return pl.pallas_call(
            functools.partial(last_kernel, features, hidden),
            out_shape=[weight_like] * 2,
            in_specs=[smem] + [stays] * 8,
            out_specs=[anywhere] * 2,
            scratch_shapes=spaces(rows_like, rows_like, piece_like, piece_like, slopes_like, gradient_like)
            + spaces(piece_like, piece_like)
            + [sems_of(10), sems_of(3)],
            input_output_aliases={7: 0, 8: 1},
            compiler_params=fits(60),
            cost_estimate=costs(1, 1),
        )(go, inputs, grads, first_there, second_there, slopes, gradient, new_up, new_down)

    half_like = jax.ShapeDtypeStruct((row_count, features // 2), bf16)
    block_rows = height * max(1, experts // line)
    gather_like = [jax.ShapeDtypeStruct((block_rows * n, share), bf16) for n in (line // 2, line // 2 - 2, 2)]

    sources = []

    def first_rollout():
        now, sent = decode_step(0, states, payload, up_here, down_here)
        return (now, sent) + unset(sent, *gather_like)

    def first_learner():
        units, places = learner_rows([crossed_rows, own_rows])
        sources.append(places)
        return (states, payload) + tuple(units)

    states, payload, *rows = lax.cond(is_rollout, first_rollout, first_learner)

    def second_rollout():
        now, sent = states, payload
        for step in range(1, half_steps):
            now, sent = decode_step(step, now, sent, up_here, down_here)
        return (now,) + unset(now, up_here, down_here)

    def second_learner():
        units, weights = with_parts(rows, sources[0])
        return (states,) + tuple(update(units, weights, up_here, down_here))

    states, new_up, new_down = lax.cond(is_rollout, second_rollout, second_learner)
    states_there = lax.ppermute(states, "sect", [(0, 1)])

    held_up = pl.pallas_call(
        hold_kernel,
        out_shape=weight_like,
        in_specs=[smem, stays],
        out_specs=vmem,
        scratch_shapes=[pltpu.SemaphoreType.DMA],
        compiler_params=fits(16),
        cost_estimate=costs(1, 1),
    )(go, new_up)

    def third_rollout():
        return (states, payload) + tuple(learner_rows([own_rows, crossed_rows])[0])

    def third_learner():
        sent = pl.pallas_call(
            functools.partial(dispatch_kernel, half_steps),
            out_shape=jax.ShapeDtypeStruct((moved, lanes), bf16),
            compiler_params=fits(16),
            cost_estimate=costs(1, 1),
        )(targets, states_there)
        now, sent = decode_step(half_steps, states_there, sent, held_up, new_down)
        return (now, sent) + unset(sent, *gather_like)

    states, payload, *rows = lax.cond(is_rollout, third_rollout, third_learner)

    def fourth_rollout():
        units, weights = with_parts(rows, sources[0])
        whole = pl.pallas_call(
            functools.partial(assemble_kernel, parts, height),
            out_shape=[rows_like] * 2,
            in_specs=[smem] + [anywhere] * len(units),
            scratch_shapes=[sems_of(2 * parts * experts)],
            compiler_params=fits(62),
            cost_estimate=costs(1, 1),
        )(part_ref, *units)
        return unset(weights, half_like, half_like) + tuple(whole) + (weights,)

    def fourth_learner():
        now, sent = states, payload
        for step in range(half_steps + 1, steps):
            now, sent = decode_step(step, now, sent, held_up, new_down)
        pieces = [sent] + [shifted(sent, "dp", j) for j in range(1, parts)]
        left, right = pl.pallas_call(
            functools.partial(join_kernel, parts, row_count),
            out_shape=[half_like] * 2,
            in_specs=[smem] + [vmem] * parts,
            scratch_shapes=[pltpu.VMEM((row_count, features), bf16)],
            cost_estimate=costs(1, 1),
        )(part_ref, *pieces)
        return (left, right) + unset(left, rows_like, rows_like, weights_like)

    left, right, inputs, grads, weights = lax.cond(is_rollout, fourth_rollout, fourth_learner)

    new_up, new_down, slopes, gradient = update_late(new_up, new_down)
    delivered = lax.ppermute(left, "sect", [(1, 0)])
    new_up, new_down = update_last(slopes, gradient, new_up, new_down)
    right, new_up = lax.optimization_barrier((right, new_up))
    final_states = jnp.where(is_rollout, delivered, right)
    return final_states, new_up[None, None], new_down[None, None]


def solution(mesh):
    in_specs = (
        P("exp", None),
        P(),
        P(None, "exp", None),
        P(None, "exp", None),
        P("sect", "exp", "dp", None),
        P("sect", "exp", "dp", None),
        P("sect", "exp", None),
        P("sect", "exp", None),
        P("exp", None, None),
        P("exp", None),
        P("exp", None),
        P("exp", None),
    )
    out_specs = (P("exp", "sect"), P("sect", "exp", "dp", None), P("sect", "exp", "dp", None))
    return jax.shard_map(on_device, mesh=mesh, in_specs=in_specs, out_specs=out_specs, check_vma=False)
```
